32 devices in a mesh: gx: 4 (over x, core), gy: 8 (over z, y).
Axes of the slice: x: 2, y: 2, z: 4, core: 2. Of those that a mesh axis runs over, the one named last changes fastest.
Arguments:
- spectrum: bfloat16 [64, 128, 1152], P('gx', 'gy'), may hold values from 0.099609375 to 1
- courant: float32 [2, 1152], replicated, may hold values from -0.45 to 0.45
- source: float32 [64, 128], P('gx', 'gy'), may hold values from 0.2 to 2
- wave_land: int32 [64, 128], P('gx', 'gy'), may hold values 0 or 1
- stokes_kernel: bfloat16 [1152, 128], replicated, may hold values from -0.1875 to 0.1875
- velocity: float32 [128, 512, 128], P('gx', 'gy'), may hold values from -6 to 6
- coriolis: float32 [128, 512], P('gx', 'gy'), may hold values from 0.5 to 1.5
- ocean_codes: int32 [128, 512, 4], P('gx', 'gy'), may hold values from 0 to 8
- ocean_weights: float32 [128, 512, 4], P('gx', 'gy'), may hold values from 0.2 to 2
- wave_codes: int32 [64, 128, 4], P('gx', 'gy'), may hold values from 0 to 23
- wave_weights: float32 [64, 128, 4], P('gx', 'gy'), may hold values from 0.2 to 2
Outputs:
- new_spectrum: bfloat16 [64, 128, 1152], P('gx', 'gy')
- new_velocity: float32 [128, 512, 128], P('gx', 'gy')
- wave_current: float32 [2, 64, 128], P(None, 'gx', 'gy')
The draws below stay inside these ranges and needn't reach their ends.
All inputs are finite; a program needn't handle non-finite values. No bound on the sum of `wave_land` on one device may be relied on, other than what follows from the above.
Results may differ from the reference program's by a relative error of at most 0.002.
Values may be sent and summed in bfloat16 or wider, within the bound.
No kernel may reach another device: no remote copies, remote signals or barrier semaphores. Data moves between devices by JAX's collectives and lax.ppermute only.
A program may use at most 64 MiB of HBM per device.

```python
import math
import jax
import jax.numpy as jnp
from jax import lax

NB = 1152
NL = 64
K = 4
RX = 2
RY = 4
NWX = 64
NWY = 128
NOX = 128
NOY = 512


def set_ends(drawn, stream_key, least, high):
    dims = drawn.shape
    place = [jax.random.randint(jax.random.fold_in(stream_key, axis), (), 0, dims[axis]) for axis in range(len(dims))]
    drawn = drawn.at[tuple(place)].set(least)
    longest = dims.index(max(dims))
    place[longest] = (place[longest] + 1) % dims[longest]
    return drawn.at[tuple(place)].set(high)


def steps_of(key, dims, shards, least, high):
    level = 1.0
    for position, parts in shards:
        draws = jax.random.uniform(jax.random.fold_in(jax.random.fold_in(key, 6), position), (parts,), jnp.float32, least / len(shards), high / len(shards))
        level = level * jnp.repeat(jnp.exp(draws), dims[position] // parts).reshape((-1,) + (1,) * (len(dims) - 1 - position))
    return level


def noise(stream_key, shape, width, bound, shards=(), held_as=jnp.bfloat16):
    level = steps_of(stream_key, shape, shards, -0.22, 0.18) if shards else 1.0
    result = jax.random.normal(stream_key, shape, jnp.float32) * width * level
    return jnp.minimum(jnp.maximum(result, -bound), bound).astype(held_as)


def setup_inputs(seed: int = 0) -> dict:
    seeds = jax.random.split(jax.random.key(seed), 12)
    spectrum = jnp.clip(jnp.exp(math.log(1.0) - 2.306499 * jax.random.uniform(seeds[0], (NWX, NWY, NB), jnp.float32) ** steps_of(seeds[0], (NWX, NWY, NB), ((0, 4), (1, 8)), -0.2, 0.2)), 0.099609375, 1.0).astype(jnp.bfloat16)
    courant = jnp.clip(jax.random.uniform(seeds[1], (2, NB), jnp.float32, -0.45, 0.45), -0.45, 0.45)
    source = jnp.clip(jnp.exp(math.log(2.0) - 2.3025851 * jax.random.uniform(seeds[2], (NWX, NWY), jnp.float32) ** steps_of(seeds[2], (NWX, NWY), ((0, 4), (1, 8)), -0.2, 0.2)), 0.2, 2.0)
    wave_land = set_ends((jax.random.randint(seeds[3], (NWX, NWY), 0, 4) < 3).astype(jnp.int32), jax.random.fold_in(seeds[3], 1), 0, 1)
    stokes_kernel = noise(seeds[4], (NB, 2 * NL), NB ** -0.5, 0.1875)
    velocity = noise(seeds[5], (NOX, NOY, 2 * NL), 1.0, 6.0, ((0, 4), (1, 8)), jnp.float32)
    coriolis = jnp.clip(0.5 + 1.0 * jax.random.uniform(seeds[6], (NOX, NOY), jnp.float32) ** steps_of(seeds[6], (NOX, NOY), ((0, 4), (1, 8)), -0.2, 0.2), 0.5, 1.5)
    ocean_codes = set_ends(jax.random.randint(seeds[7], (NOX, NOY, K), 0, 9), jax.random.fold_in(seeds[7], 1), 0, 8).astype(jnp.int32)
    ocean_weights = jnp.clip(jnp.exp(math.log(2.0) - 2.3025851 * jax.random.uniform(seeds[8], (NOX, NOY, K), jnp.float32) ** steps_of(seeds[8], (NOX, NOY, K), ((0, 4), (1, 8)), -0.2, 0.2)), 0.2, 2.0)
    wave_codes = set_ends(jax.random.randint(seeds[9], (NWX, NWY, K), 0, (RX + 2) * (RY + 2)), jax.random.fold_in(seeds[9], 1), 0, ((RX + 2) * (RY + 2)) - 1).astype(jnp.int32)
    wave_weights = jnp.clip(jnp.exp(math.log(2.0) - 2.3025851 * jax.random.uniform(seeds[10], (NWX, NWY, K), jnp.float32) ** steps_of(seeds[10], (NWX, NWY, K), ((0, 4), (1, 8)), -0.2, 0.2)), 0.2, 2.0)
    return {"spectrum": spectrum, "courant": courant, "source": source, "wave_land": wave_land, "stokes_kernel": stokes_kernel, "velocity": velocity, "coriolis": coriolis, "ocean_codes": ocean_codes, "ocean_weights": ocean_weights, "wave_codes": wave_codes, "wave_weights": wave_weights}


time_step = 0.5


def wave_rows(spectrum, courant, source, wave_land, stokes_kernel):
    speed_x = courant[0]
    speed_y = courant[1]

    def one_row(row_index):
        picked = jnp.take(spectrum, (row_index + jnp.arange(-1, 2, dtype=jnp.int32)) % NWX, axis=0).astype(jnp.float32)
        center = picked[1]
        padded = jnp.pad(center, ((1, 1), (0, 0)))
        advected = (center - jnp.maximum(speed_x, 0.0) * (center - picked[0])
                    - jnp.maximum(-speed_x, 0.0) * (center - picked[2])
                    - jnp.maximum(speed_y, 0.0) * (center - padded[:-2])
                    - jnp.maximum(-speed_y, 0.0) * (center - padded[2:]))
        land_row = jnp.take(wave_land, row_index, axis=0).astype(jnp.float32)[:, None]
        source_row = jnp.take(source, row_index, axis=0)[:, None]
        updated = (land_row * (advected + 0.2 * source_row * advected - 0.1 * advected * advected)).astype(jnp.bfloat16)
        profile = jnp.dot(updated, stokes_kernel, preferred_element_type=jnp.float32).astype(jnp.bfloat16)
        return updated, profile

    return lax.map(one_row, jnp.arange(NWX, dtype=jnp.int32))


def ocean_tendency(state, profiles_padded, coriolis, ocean_codes, ocean_weights):
    column = jnp.arange(NOY, dtype=jnp.int32)

    def one_row(row_index):
        rows = jnp.take(state, (row_index + jnp.arange(-2, 3, dtype=jnp.int32)) % NOX, axis=0)
        along_x = rows[:, :, NL:]
        dvdx = (8.0 * (along_x[3] - along_x[1]) - (along_x[4] - along_x[0])) / 12.0
        along_y = jnp.pad(rows[2, :, :NL], ((2, 2), (0, 0)))
        dudy = (8.0 * (along_y[3:-1] - along_y[1:-3]) - (along_y[4:] - along_y[:-4])) / 12.0
        codes = jnp.take(ocean_codes, row_index, axis=0)
        weights = jnp.take(ocean_weights, row_index, axis=0)
        normed = weights / jnp.sum(weights, axis=-1, keepdims=True)
        stokes = jnp.zeros((NOY, 2 * NL), jnp.float32)
        for entry in range(K):
            code = codes[:, entry]
            wave_x = (row_index // RX + code // 3 - 1) % NWX
            wave_y = column // RY + code % 3
            stokes = stokes + normed[:, entry:entry + 1] * profiles_padded[wave_x, wave_y].astype(jnp.float32)
        absolute = jnp.take(coriolis, row_index, axis=0)[:, None] + dvdx - dudy
        return jnp.concatenate([absolute * stokes[:, NL:], -absolute * stokes[:, :NL]], axis=-1)

    return lax.map(one_row, jnp.arange(NOX, dtype=jnp.int32))


def reference(spectrum, courant, source, wave_land, stokes_kernel, velocity, coriolis, ocean_codes, ocean_weights, wave_codes, wave_weights):
    new_spectrum, profiles = wave_rows(spectrum, courant, source, wave_land, stokes_kernel)
    profiles_padded = jnp.pad(profiles, ((0, 0), (1, 1), (0, 0)))
    first = ocean_tendency(velocity, profiles_padded, coriolis, ocean_codes, ocean_weights)
    middle = velocity + time_step * first
    second = ocean_tendency(middle, profiles_padded, coriolis, ocean_codes, ocean_weights)
    new_velocity = velocity + 0.5 * time_step * (first + second)
    means = jnp.stack([jnp.mean(new_velocity[:, :, :NL], axis=-1), jnp.mean(new_velocity[:, :, NL:], axis=-1)], axis=0)
    means_padded = jnp.pad(means, ((0, 0), (0, 0), (1, 1)))
    grid_x = lax.broadcasted_iota(jnp.int32, (NWX, NWY), 0)
    grid_y = lax.broadcasted_iota(jnp.int32, (NWX, NWY), 1)
    normed = wave_weights / jnp.sum(wave_weights, axis=-1, keepdims=True)
    current = jnp.zeros((2, NWX, NWY), jnp.float32)
    for entry in range(K):
        code = wave_codes[:, :, entry]
        ocean_x = (RX * grid_x + code // (RY + 2) - 1) % NOX
        ocean_y = RY * grid_y + code % (RY + 2)
        current = current + normed[None, :, :, entry] * means_padded[:, ocean_x, ocean_y]
    return new_spectrum, new_velocity, current
```

```python
import jax
import jax.numpy as jnp
from jax import lax
from jax.experimental import pallas as pl
from jax.experimental.pallas import tpu as pltpu
from jax.sharding import PartitionSpec as P

K = 4
RX = 2
RY = 4
STEP = 0.5
PAD = 8
WIDE = 24
HV, HL = 5, 3
HX, HY = 3, 2
BF = jnp.bfloat16
F32 = jnp.float32


def partners(count, parity):
    return [(i ^ 1) if parity == 0 else ((i + 1) ^ 1) - 1 for i in range(count)]


def swap_pairs(axis, parity):
    nx, ny = lax.axis_size("gx"), lax.axis_size("gy")
    pairs = []
    for x in range(nx):
        for y in range(ny):
            tx, ty = x, y
            if axis == "gx":
                tx = partners(nx, parity)[x] % nx
            else:
                ty = partners(ny, parity)[y]
                if not 0 <= ty < ny:
                    tx, ty = x ^ 1, y
            pairs.append((x * ny + y, tx * ny + ty))
    return pairs


def exchange(axis, last, first):
    even = lax.axis_index(axis) % 2 == 0
    to_a = jnp.where(even, last, first)
    to_b = jnp.where(even, first, last)
    from_b = lax.ppermute(to_b, ("gx", "gy"), swap_pairs(axis, 1))
    from_a = lax.ppermute(to_a, ("gx", "gy"), swap_pairs(axis, 0))
    return jnp.where(even, from_b, from_a), jnp.where(even, from_a, from_b)


def packed(parts):
    flat = jnp.concatenate([p.reshape(-1) for p in parts])
    return jnp.pad(flat, (0, -flat.shape[0] % 2048)).reshape(-1, 128)


def unpacked(buffer, shapes):
    flat, at, out = buffer.reshape(-1), 0, []
    for shape in shapes:
        size = 1
        for n in shape:
            size *= n
        out.append(flat[at : at + size].reshape(shape))
        at += size
    return out


def split(value):
    high = value.astype(BF)
    return high, (value - high.astype(F32)).astype(BF)


def split3(value):
    high, rest = value.astype(BF), value - value.astype(BF).astype(F32)
    middle = rest.astype(BF)
    return high, middle, (rest - middle.astype(F32)).astype(BF)


def wave_kernel(spec, west, east, south, north, courant, source, land, weights, out, profile):
    rows, cols, _ = spec.shape
    cx, cy = courant[0:1, :], courant[1:2, :]
    ax, ay = jnp.abs(cx), jnp.abs(cy)
    from_west, from_south = cx > 0.0, cy > 0.0
    keep = 1.0 - ax - ay
    sub = lax.broadcasted_iota(jnp.int32, (cols, 1), 0)
    for x in range(rows):
        center = spec[x].astype(F32)
        before = (spec[x - 1] if x else west[...]).astype(F32)
        after = (spec[x + 1] if x < rows - 1 else east[...]).astype(F32)
        below = jnp.where(sub == 0, south[x : x + 1, :].astype(F32), pltpu.roll(center, 1, 0))
        above = jnp.where(sub == cols - 1, north[x : x + 1, :].astype(F32), pltpu.roll(center, cols - 1, 0))
        advected = (
            keep * center
            + ax * jnp.where(from_west, before, after)
            + ay * jnp.where(from_south, below, above)
        )
        wind = 1.0 + 0.2 * source[:, x : x + 1]
        updated = land[:, x : x + 1] * (advected * (wind - 0.1 * advected))
        updated = updated.astype(BF)
        out[x] = updated
        profile[x] = jnp.dot(updated, weights[...], preferred_element_type=F32).astype(BF)


def ocean_kernel(
    own, before, after, before_low, after_low, left, right, left_low, right_low,
    slots, shares, coriolis, profiles, gather, wave_codes, wave_shares, spread,
    out, current,
    vel, mid, prof, drift, spin, mean, picked,
):
    rows, cols, lanes = own.shape
    half = lanes // 2
    listed = slots.shape[0]
    wide = cols + 2 * PAD
    lane = lax.broadcasted_iota(jnp.int32, (1, lanes), 1)
    is_u = lane < half
    zero = jnp.zeros((wide, lanes), F32)

    def clear(r, _):
        vel[r, 0:PAD, :] = zero[0:PAD]
        vel[r, PAD + cols :, :] = zero[0:PAD]
        return 0

    lax.fori_loop(0, rows + 2 * HV, clear, 0)

    def fill(r, _):
        vel[r + HV, PAD : PAD + cols, :] = own[r]
        return 0

    lax.fori_loop(0, rows, fill, 0)
    for r in range(HV):
        vel[r, PAD : PAD + cols, :] = before[r].astype(F32)
        vel[HV + rows + r, PAD : PAD + cols, :] = after[r].astype(F32)
    vel[HV - 1, PAD : PAD + cols, :] += before_low[0].astype(F32)
    vel[HV + rows, PAD : PAD + cols, :] += after_low[0].astype(F32)
    for j in range(HV):
        vel[:, PAD - HV + j, :] = left[j].astype(F32)
        vel[:, PAD + cols + j, :] = right[j].astype(F32)
    vel[HV - 1 : HV + rows + 1, PAD - 1, :] += left_low[...].astype(F32)
    vel[HV - 1 : HV + rows + 1, PAD + cols, :] += right_low[...].astype(F32)
    sign = jnp.where(is_u, 1.0, -1.0)
    prof[...] = pltpu.roll(profiles[...].astype(F32), half, 1) * sign
    block = 3 * WIDE
    place = lax.broadcasted_iota(jnp.int32, (block, lanes), 0)
    contract = (((0,), (0,)), ((), ()))
    ones = jnp.ones((8, lanes), BF)
    sub8 = lax.broadcasted_iota(jnp.int32, (8, lanes), 0)

    def zeta_of(ref, r):
        def at(dx, dy):
            return ref[r + dx, PAD // 2 + dy : PAD // 2 + dy + cols + PAD, :]
        d1 = jnp.where(is_u, at(0, -1), at(1, 0)) - jnp.where(is_u, at(0, 1), at(-1, 0))
        d2 = jnp.where(is_u, at(0, -2), at(2, 0)) - jnp.where(is_u, at(0, 2), at(-2, 0))
        part = 8.0 * d1 - d2
        return part + pltpu.roll(part, half, 1)

    inner = slice(PAD // 2, PAD // 2 + cols + PAD)

    def first_step(r, _):
        table = jnp.zeros((block, lanes), F32)
        for k in range(K):
            table = table + jnp.where(place == slots[r, k : k + 1, :], shares[r, k : k + 1, :], 0.0)
        start = pl.multiple_of(((r + 1) // 2) * WIDE, 8)
        names = prof[pl.ds(start, block), :].astype(BF)
        stokes = lax.dot_general(table.astype(BF), names, contract, preferred_element_type=F32)
        turn = coriolis[pl.ds(r, 1), :]
        high, middle, low = (p.astype(F32) for p in split3(turn))
        parts = jnp.where(sub8 == 0, high, jnp.where(sub8 == 1, middle, jnp.where(sub8 == 2, low, 0.0)))
        turned = lax.dot_general(parts.astype(BF), ones, contract, preferred_element_type=F32)
        drift[r] = stokes[0:wide]
        spin[r] = turned[0:wide]
        absolute = spin[r, inner, :] + zeta_of(vel, r + HV - HL) * (1.0 / 12.0)
        mid[r, 0 : PAD // 2, :] = zero[0 : PAD // 2]
        mid[r, wide - PAD // 2 :, :] = zero[0 : PAD // 2]
        mid[r, inner, :] = vel[r + HV - HL, inner, :] + STEP * absolute * drift[r, inner, :]
        return 0

    lax.fori_loop(0, listed, first_step, 0)

    mean[...] = jnp.zeros(mean.shape, F32)
    half_of = lax.broadcasted_iota(jnp.int32, (8, lanes), 0)
    lane8 = lax.broadcasted_iota(jnp.int32, (8, lanes), 1)
    averager = jnp.where(lane8 // half == half_of, 1.0 / half, 0.0).astype(BF)
    across = (((1,), (1,)), ((), ()))

    def second_step(n, _):
        r = n + HL - 1
        absolute = spin[r, inner, :] + zeta_of(mid, r) * (1.0 / 12.0)
        second = absolute * drift[r, inner, :]
        new = 0.5 * (vel[r + HV - HL, inner, :] + mid[r, inner, :]) + (0.5 * STEP) * second
        mid_new = new
        high, middle, low = split3(mid_new)
        sums = sum(
            lax.dot_general(averager, p, across, preferred_element_type=F32) for p in (high, middle, low)
        )
        mean[0, pl.ds(n, 1), 0 : cols + PAD] = sums[0:1]
        mean[1, pl.ds(n, 1), 0 : cols + PAD] = sums[1:2]

        @pl.when(jnp.logical_and(n >= 1, n <= rows))
        def _():
            out[n - 1] = new[PAD // 2 : PAD // 2 + cols]

        return 0

    lax.fori_loop(0, rows + 2, second_step, 0)

    cells_x = wave_codes.shape[1]
    lane1 = lax.broadcasted_iota(jnp.int32, (1, lanes), 1)
    group = lane1 // current.shape[2]
    for c in range(2):
        picked[...] = sum(jnp.dot(p, gather[...], preferred_element_type=F32) for p in split3(mean[c]))
        total = jnp.zeros((cells_x, lanes), F32)
        for near in range(RX + 2):
            share = jnp.zeros((cells_x, lanes), F32)
            for k in range(K):
                share = share + jnp.where(wave_codes[k] == near * (RY + 2) + group, wave_shares[k], 0.0)
            total = total + share * picked[pl.ds(near, cells_x, stride=RX), :]
        sums = sum(jnp.dot(p, spread[...], preferred_element_type=F32) for p in split3(total))
        current[c] = sums[:, 0 : current.shape[2]]


VMEM = pl.BlockSpec(memory_space=pltpu.VMEM)


def shards(
    spectrum, courant, source, wave_land, stokes_kernel, velocity, coriolis,
    ocean_codes, ocean_weights, wave_codes, wave_weights,
):
    wr, wc, bins = spectrum.shape
    rows, cols, lanes = velocity.shape
    half = lanes // 2
    gy, ny = lax.axis_index("gy"), lax.axis_size("gy")
    at_start, at_end = gy == 0, gy == ny - 1

    def clear_before(value):
        return jnp.where(at_start, jnp.zeros((), value.dtype), value)

    def clear_after(value):
        return jnp.where(at_end, jnp.zeros((), value.dtype), value)

    codes = jnp.transpose(ocean_codes, (0, 2, 1)).astype(BF)
    weights = jnp.transpose(ocean_weights, (0, 2, 1))
    shares = (weights / jnp.sum(weights, axis=1, keepdims=True)).astype(BF)
    cor_high, cor_low = split(coriolis)

    def x_edge(at_last):
        def cut(value, n):
            return value[-n:] if at_last else value[:n]
        edge = cut(velocity, HV)
        ring = velocity[-1:] if at_last else velocity[:1]
        ring_low = split(ring)[1]
        return packed([
            cut(spectrum, 1), edge.astype(BF), ring_low,
            cut(codes, HL), cut(shares, HL), cut(cor_high, HL), cut(cor_low, HL),
        ])

    shapes_x = [(wc, bins), (HV, cols, lanes), (1, cols, lanes), (HL, K, cols), (HL, K, cols), (HL, cols), (HL, cols)]
    with jax.named_scope("edges"):
        xb, xa = exchange("gx", x_edge(True), x_edge(False))
        south, north = exchange("gy", spectrum[:, -1, :], spectrum[:, 0, :])
    west, vel_b, low_b, codes_b, shares_b, ch_b, cl_b = unpacked(xb, shapes_x)
    east, vel_a, low_a, codes_a, shares_a, ch_a, cl_a = unpacked(xa, shapes_x)
    south, north = clear_before(south), clear_after(north)

    new_spectrum, profiles = pl.pallas_call(
        wave_kernel,
        out_shape=(jax.ShapeDtypeStruct(spectrum.shape, BF), jax.ShapeDtypeStruct((wr, wc, lanes), BF)),
        in_specs=[VMEM] * 9, out_specs=(VMEM, VMEM),
        compiler_params=pltpu.CompilerParams(vmem_limit_bytes=48 << 20),
        name="wave",
    )(spectrum, west, east, south, north, courant, source.T, wave_land.T.astype(F32), stokes_kernel)

    with jax.named_scope("profiles_x"):
        pb, pa = exchange("gx", profiles[-HX:], profiles[:HX])
    profiles = jnp.concatenate([pb, profiles, pa], axis=0)
    codes = jnp.concatenate([codes_b, codes, codes_a], axis=0)
    shares = jnp.concatenate([shares_b, shares, shares_a], axis=0)
    cor_high = jnp.concatenate([ch_b, cor_high, ch_a], axis=0)
    cor_low = jnp.concatenate([cl_b, cor_low, cl_a], axis=0)

    def y_edge(at_last):
        def cut(value, n, dim):
            length = value.shape[dim]
            return lax.slice_in_dim(value, length - n, length, axis=dim) if at_last else lax.slice_in_dim(value, 0, n, axis=dim)
        vel = jnp.concatenate([cut(v, HV, 1).astype(BF) for v in (vel_b, velocity, vel_a)], axis=0)
        ring = jnp.concatenate([cut(low_b, 1, 1), split(cut(velocity, 1, 1))[1], cut(low_a, 1, 1)], axis=0)
        return packed([
            cut(profiles, HY, 1), jnp.transpose(vel, (1, 0, 2)), ring[:, 0],
            cut(codes, HL, 2), cut(shares, HL, 2), cut(cor_high, HL, 1), cut(cor_low, HL, 1),
        ])

    prow, vrow, lrow = wr + 2 * HX, rows + 2 * HV, rows + 2 * HL
    shapes_y = [(prow, HY, lanes), (HV, vrow, lanes), (rows + 2, lanes), (lrow, K, HL), (lrow, K, HL), (lrow, HL), (lrow, HL)]
    with jax.named_scope("halo_y"):
        yb, ya = exchange("gy", y_edge(True), y_edge(False))
    yb, ya = clear_before(yb), clear_after(ya)
    prof_b, left, left_low, codes_b, shares_b, ch_b, cl_b = unpacked(yb, shapes_y)
    prof_a, right, right_low, codes_a, shares_a, ch_a, cl_a = unpacked(ya, shapes_y)
    profiles = jnp.concatenate([prof_b, profiles, prof_a, jnp.zeros((prow, WIDE - wc - 2 * HY, lanes), BF)], axis=1)
    profiles = profiles.reshape(prow * WIDE, lanes)

    def widened(b, own, a):
        joined = jnp.concatenate([b, own, a], axis=-1).astype(F32)
        edge = [(0, 0)] * (joined.ndim - 1)
        return jnp.pad(joined, edge + [(PAD - HL, lanes - PAD - cols - HL)])

    codes = widened(codes_b, codes, codes_a).astype(jnp.int32)
    shares = widened(shares_b, shares, shares_a)
    turn = widened(ch_b, cor_high, ch_a) + widened(cl_b, cor_low, cl_a)
    third = (codes >= 3).astype(jnp.int32) + (codes >= 6).astype(jnp.int32)
    lane = lax.broadcasted_iota(jnp.int32, codes.shape, 2)
    slots = third * (WIDE - 3) + codes + lane // RY - (PAD // RY - 1)

    reach = RY + 2
    wc_t = jnp.transpose(wave_codes, (2, 0, 1))
    ww_t = jnp.transpose(wave_weights, (2, 0, 1))
    ww_t = ww_t / jnp.sum(ww_t, axis=0, keepdims=True)
    spare = [(0, 0), (0, 0), (0, lanes - reach * wc)]
    wc_t = jnp.pad(jnp.tile(wc_t, (1, 1, reach)), spare)
    ww_t = jnp.pad(jnp.tile(ww_t, (1, 1, reach)), spare)
    at = lax.broadcasted_iota(jnp.int32, (lanes, lanes), 0)
    to = lax.broadcasted_iota(jnp.int32, (lanes, lanes), 1)
    used = to < reach * wc
    gather = (used & (at == RY * (to % wc) + to // wc + PAD // 2 - 1)).astype(BF)
    spread = ((at < reach * wc) & (at % wc == to)).astype(BF)

    scratch = [
        pltpu.VMEM((vrow, cols + 2 * PAD, lanes), F32),
        pltpu.VMEM((lrow, cols + 2 * PAD, lanes), F32),
        pltpu.VMEM((prow * WIDE, lanes), F32),
        pltpu.VMEM((lrow, cols + 2 * PAD, lanes), F32),
        pltpu.VMEM((lrow, cols + 2 * PAD, lanes), F32),
        pltpu.VMEM((2, rows + 8, lanes), F32),
        pltpu.VMEM((rows + 8, lanes), F32),
    ]
    new_velocity, current = pl.pallas_call(
        ocean_kernel,
        out_shape=(jax.ShapeDtypeStruct(velocity.shape, F32), jax.ShapeDtypeStruct((2, wr, wc), F32)),
        in_specs=[VMEM] * 17, out_specs=(VMEM, VMEM),
        scratch_shapes=scratch,
        compiler_params=pltpu.CompilerParams(vmem_limit_bytes=48 << 20),
        name="ocean",
    )(
        velocity, vel_b, vel_a, low_b, low_a, left, right, left_low, right_low,
        slots, shares, turn, profiles, gather, wc_t, ww_t, spread,
    )
    return new_spectrum, new_velocity, current


def solution(mesh):
    return jax.shard_map(
        shards,
        mesh=mesh,
        in_specs=(
            P("gx", "gy", None), P(), P("gx", "gy"), P("gx", "gy"), P(), P("gx", "gy", None),
            P("gx", "gy"), P("gx", "gy", None), P("gx", "gy", None), P("gx", "gy", None), P("gx", "gy", None),
        ),
        out_specs=(P("gx", "gy", None), P("gx", "gy", None), P(None, "gx", "gy")),
        check_vma=False,
    )
```

```python
import jax
import jax.numpy as jnp
from jax import lax
from jax.experimental import pallas as pl
from jax.experimental.pallas import tpu as pltpu
from jax.sharding import PartitionSpec as P

K = 4
RX = 2
RY = 4
STEP = 0.5
WIDE = 24
LEAD = 4
HV, HL = 5, 3
HX, HY = 3, 2
EDGE = 8
BF = jnp.bfloat16
F32 = jnp.float32
ROWS_DOT = (((0,), (0,)), ((), ()))


def partner(i, count, parity):
    return (i ^ 1) if parity == 0 else ((i + 1) ^ 1) - 1


def swap(value, axis, parity):
    nx, ny = lax.axis_size("gx"), lax.axis_size("gy")
    pairs = []
    for x in range(nx):
        for y in range(ny):
            tx, ty = x, y
            if axis == "gx":
                tx = partner(x, nx, parity) % nx
            else:
                ty = partner(y, ny, parity)
                if not 0 <= ty < ny:
                    tx, ty = x ^ 1, y
            pairs.append((x * ny + y, tx * ny + ty))
    return lax.ppermute(value, ("gx", "gy"), pairs)


def exchange(axis, to_a, to_b):
    from_b = swap(to_b, axis, 1)
    from_a = swap(to_a, axis, 0)
    return from_a, from_b


def is_even(axis):
    return lax.axis_index(axis) % 2 == 0


def inside(axis):
    index = lax.axis_index(axis)
    before = jnp.where(index == 0, 0.0, 1.0).astype(F32)
    after = jnp.where(index == lax.axis_size(axis) - 1, 0.0, 1.0).astype(F32)
    return before, after


def pick(cond, one, other):
    return jnp.where(cond, one.astype(F32), other.astype(F32))


def split(value):
    high = value.astype(BF)
    return high, (value - high.astype(F32)).astype(BF)


def split3(value):
    high = value.astype(BF)
    rest = value - high.astype(F32)
    middle = rest.astype(BF)
    return high, middle, (rest - middle.astype(F32)).astype(BF)


def iota(shape, dim):
    return lax.broadcasted_iota(jnp.int32, shape, dim)


def edges_kernel(spec, xa, xb, ya, yb):
    rows, cols, bins = spec.shape
    even_x, even_y = is_even("gx"), is_even("gy")
    first, last = spec[0].astype(F32), spec[rows - 1].astype(F32)
    xa[...] = jnp.where(even_x, last, first).astype(BF)
    xb[...] = jnp.where(even_x, first, last).astype(BF)
    at, cell = iota((2 * rows, rows * cols), 0), iota((2 * rows, rows * cols), 1)
    wanted = jnp.where(at < rows, at * cols, (at - rows) * cols + cols - 1)
    chosen = (cell == wanted).astype(F32).astype(BF)
    sides = jnp.dot(chosen, spec[...].reshape(rows * cols, bins), preferred_element_type=F32)
    first, last = sides[0:rows], sides[rows:]
    ya[...] = jnp.where(even_y, last, first).astype(BF)
    yb[...] = jnp.where(even_y, first, last).astype(BF)


def ocean_edges_kernel(vel, lists, xa, xb):
    rows, cols, lanes = vel.shape
    even = is_even("gx")

    def put(at, last, first):
        n = last.shape[0]
        xa[at : at + n] = jnp.where(even, last, first).astype(BF)
        xb[at : at + n] = jnp.where(even, first, last).astype(BF)

    for i in range(HV):
        put(i * cols, vel[rows - HV + i], vel[i])
    last, first = vel[rows - 1], vel[0]
    put(HV * cols, last - last.astype(BF).astype(F32), first - first.astype(BF).astype(F32))
    for i in range(HL):
        put((HV + 1) * cols + i * 16, lists[rows - HL + i].astype(F32), lists[i].astype(F32))


def wave_kernel(spec, xa, xb, ya, yb, courant, source, land, weights, out, profile, pa, pb):
    rows, cols, _ = spec.shape
    even_x, even_y = is_even("gx"), is_even("gy")
    has_south, has_north = inside("gy")
    west, east = pick(even_x, xb[...], xa[...]), pick(even_x, xa[...], xb[...])
    south = pick(even_y, yb[...], ya[...]) * has_south
    north = pick(even_y, ya[...], yb[...]) * has_north
    cx, cy = courant[0:1, :], courant[1:2, :]
    ax, ay = jnp.abs(cx), jnp.abs(cy)
    from_west, from_south = cx > 0.0, cy > 0.0
    keep = 1.0 - ax - ay
    sub = iota((cols, 1), 0)
    parts = []
    for x in range(rows):
        center = spec[x].astype(F32)
        before = spec[x - 1].astype(F32) if x else west
        after = spec[x + 1].astype(F32) if x < rows - 1 else east
        below = jnp.where(sub == 0, south[x : x + 1, :], pltpu.roll(center, 1, 0))
        above = jnp.where(sub == cols - 1, north[x : x + 1, :], pltpu.roll(center, cols - 1, 0))
        advected = (
            keep * center
            + ax * jnp.where(from_west, before, after)
            + ay * jnp.where(from_south, below, above)
        )
        wind = 1.0 + 0.2 * source[:, x : x + 1]
        updated = land[:, x : x + 1] * (advected * (wind - 0.1 * advected))
        updated = updated.astype(BF)
        out[x] = updated
        part = jnp.dot(updated, weights[...], preferred_element_type=F32).astype(BF)
        profile[x] = part
        parts.append(part.astype(F32))
    for i in range(HX):
        first, last = parts[i], parts[rows - HX + i]
        pa[i] = jnp.where(even_x, last, first).astype(BF)
        pb[i] = jnp.where(even_x, first, last).astype(BF)


def halo_kernel(vel, oa, ob, lists, profile, pa, pb, ya, yb):
    rows, cols, lanes = vel.shape
    even_x, even_y = is_even("gx"), is_even("gy")
    wr, wc = profile.shape[0], profile.shape[1]

    def put(at, last, first):
        n = last.shape[0]
        ya[at : at + n] = jnp.where(even_y, last, first).astype(BF)
        yb[at : at + n] = jnp.where(even_y, first, last).astype(BF)

    before, after = pick(even_x, pb[...], pa[...]), pick(even_x, pa[...], pb[...])
    joined = jnp.concatenate([before.astype(BF), profile[...], after.astype(BF)], axis=0)
    count = (wr + 2 * HX) * wc
    slots = 24 * HY
    at, cell = iota((2 * slots, count), 0), iota((2 * slots, count), 1)
    side, rest = at // slots, at % slots
    column = rest // 24 + jnp.where(side == 0, wc - HY, 0)
    row = rest % 24
    chosen = ((row < wr + 2 * HX) & (cell == row * wc + column)).astype(F32).astype(BF)
    sides = jnp.dot(chosen, joined.reshape(count, lanes), preferred_element_type=F32)
    put(0, sides[0:slots], sides[slots:])

    sub = iota((EDGE, 1), 0)
    blocks = []
    low_at = HV * cols
    for r in range(rows + 2 * HV):
        if HV <= r < HV + rows:
            last, first = vel[r - HV, cols - EDGE : cols, :], vel[r - HV, 0:EDGE, :]
            low_last = last - last.astype(BF).astype(F32)
            low_first = first - first.astype(BF).astype(F32)
        else:
            i = r if r < HV else r - HV - rows
            ref_one, ref_two = (ob, oa) if r < HV else (oa, ob)

            def tail(start):
                both = pick(even_x, ref_one[start : start + cols, :], ref_two[start : start + cols, :])
                return both[cols - EDGE :], both[0:EDGE]

            last, first = tail(i * cols)
            if r in (HV - 1, HV + rows):
                low_last, low_first = tail(low_at)
            else:
                low_last = low_first = jnp.zeros((EDGE, lanes), F32)
        last = jnp.where(sub == 0, pltpu.roll(low_last, 1, 0), last)
        first = jnp.where(sub == EDGE - 1, pltpu.roll(low_first, EDGE - 1, 0), first)
        blocks.append((last, first))
    for r in range(0, rows + 2 * HV, 2):
        put(
            slots + r * EDGE,
            jnp.concatenate([blocks[r][0], blocks[r + 1][0]], axis=0),
            jnp.concatenate([blocks[r][1], blocks[r + 1][1]], axis=0),
        )

    lane = iota((1, lanes), 1)
    group = lane // LEAD
    per = lanes // LEAD
    acc = None
    start = slots + (rows + 2 * HV) * EDGE
    for r in range(rows + 2 * HL):
        if r % per == 0:
            acc = [jnp.zeros((16, lanes), F32)] * 2
        if HL <= r < HL + rows:
            own = lists[r - HL].astype(F32)
        else:
            i = r if r < HL else r - HL - rows
            at = (HV + 1) * cols + i * 16
            one, two = (ob, oa) if r < HL else (oa, ob)
            own = pick(even_x, one[at : at + 16, :], two[at : at + 16, :])
        to = (r % per) * LEAD
        acc = [
            jnp.where(group == r % per, pltpu.roll(own, (to - where) % lanes, 1), a)
            for a, where in zip(acc, (cols, LEAD))
        ]
        if r % per == per - 1 or r == rows + 2 * HL - 1:
            put(start + (r // per) * 16, acc[0], acc[1])


def ocean_kernel(
    own, oa, ob, lists, profile, pa, pb, ya, yb, wave_codes, wave_shares,
    out, current,
    vel, mid, prof, names, table, drift, spin, mean, picked,
):
    rows, cols, lanes = own.shape
    wr, wc = profile.shape[0], profile.shape[1]
    half = lanes // 2
    listed = rows + 2 * HL
    inner = cols + 2 * LEAD
    even_x, even_y = is_even("gx"), is_even("gy")
    has_south, has_north = inside("gy")
    lane = iota((1, lanes), 1)
    is_u = lane < half
    slots = 24 * HY

    def from_x(r, halo, start, n):
        one, two = (ob, oa) if r < halo else (oa, ob)
        return pick(even_x, one[start : start + n, :], two[start : start + n, :])

    def from_y(start, n):
        a, b = ya[start : start + n, :], yb[start : start + n, :]
        return pick(even_y, b, a) * has_south, pick(even_y, a, b) * has_north

    def fill(r, _):
        vel[r + HV, EDGE : EDGE + cols, :] = own[r]
        return 0

    lax.fori_loop(0, rows, fill, 0, unroll=4)
    for r in range(HV):
        vel[r, EDGE : EDGE + cols, :] = from_x(r, HV, r * cols, cols)
        vel[HV + rows + r, EDGE : EDGE + cols, :] = from_x(HV + rows, HV, r * cols, cols)
    vel[HV - 1, EDGE : EDGE + cols, :] += from_x(0, HV, HV * cols, cols)
    vel[HV + rows, EDGE : EDGE + cols, :] += from_x(HV, HV, HV * cols, cols)
    sub = iota((EDGE, 1), 0)
    for r in range(0, rows + 2 * HV, 2):
        south, north = from_y(slots + r * EDGE, 2 * EDGE)
        for i in range(2):
            low, high = south[i * EDGE : i * EDGE + EDGE], north[i * EDGE : i * EDGE + EDGE]
            low = jnp.where(sub == 0, 0.0, low) + jnp.where(sub == EDGE - 1, pltpu.roll(low, EDGE - 1, 0), 0.0)
            high = jnp.where(sub == EDGE - 1, 0.0, high) + jnp.where(sub == 0, pltpu.roll(high, 1, 0), 0.0)
            vel[r + i, 0:EDGE, :] = low
            vel[r + i, EDGE + cols :, :] = high

    group = lane // LEAD
    per = lanes // LEAD
    sub16 = iota((16, 1), 0)
    start = slots + (rows + 2 * HV) * EDGE
    place_of = (lane // RY).astype(F32)
    for r in range(listed):
        if r % per == 0:
            south, north = from_y(start + (r // per) * 16, 16)
        if HL <= r < HL + rows:
            full = lists[r - HL].astype(F32)
        else:
            i = r if r < HL else r - HL - rows
            full = from_x(0 if r < HL else HL, HL, (HV + 1) * cols + i * 16, 16)
        at = (r % per) * LEAD
        full = jnp.where(group == 0, pltpu.roll(south, (-at) % lanes, 1), full)
        full = jnp.where(group == 1 + cols // LEAD, pltpu.roll(north, (LEAD + cols - at) % lanes, 1), full)
        third = jnp.where(full >= 6.0, 2.0, jnp.where(full >= 3.0, 1.0, 0.0))
        table[r] = jnp.where(sub16 < K, third * (WIDE - 3.0) + full + place_of, full)

    prof[...] = jnp.zeros(prof.shape, F32)
    for x in range(wr + 2 * HX):
        if HX <= x < HX + wr:
            part = profile[x - HX].astype(F32)
        elif x < HX:
            part = pick(even_x, pb[x], pa[x])
        else:
            part = pick(even_x, pa[x - HX - wr], pb[x - HX - wr])
        prof[x * WIDE + HY : x * WIDE + HY + wc, :] = part
    south, north = from_y(0, slots)
    for c in range(HY):
        prof[pl.ds(c, wr + 2 * HX, stride=WIDE), :] = south[24 * c : 24 * c + wr + 2 * HX]
        prof[pl.ds(HY + wc + c, wr + 2 * HX, stride=WIDE), :] = north[24 * c : 24 * c + wr + 2 * HX]
    sign = jnp.where(is_u, 1.0, -1.0)
    block = 3 * WIDE
    for x in range(wr + 2 * HX - 2):
        part = pltpu.roll(prof[x * WIDE : x * WIDE + block, :], half, 1) * sign
        none = jnp.zeros((8, lanes), F32)
        names[x, :, 0:lanes] = jnp.concatenate([part, none], axis=0).astype(BF)
        names[x, :, lanes:] = jnp.concatenate([jnp.zeros((block, lanes), F32), none + 1.0], axis=0).astype(BF)

    place = iota((block, lanes), 0).astype(F32)

    def stokes(m, _):
        for u in range(UNROLL):
            r = m * UNROLL + u
            hot = jnp.where(place == table[r, 0:1, :], table[r, K : K + 1, :], 0.0)
            for k in range(1, K):
                hot = hot + jnp.where(place == table[r, k : k + 1, :], table[r, K + k : K + k + 1, :], 0.0)
            left = jnp.concatenate([hot, table[r, 8:16, :]], axis=0).astype(BF)
            both = lax.dot_general(left, names[(r + 1) // 2], ROWS_DOT, preferred_element_type=F32)
            drift[r] = both[0:inner, 0:lanes]
            spin[r] = both[0:inner, lanes:]
        return 0

    lax.fori_loop(0, listed // UNROLL, stokes, 0)

    def zeta(ref, r, base):
        def at(dx, dy):
            return ref[r + dx, base + dy : base + dy + inner, :]

        near = jnp.where(is_u, at(0, -1), at(1, 0)) - jnp.where(is_u, at(0, 1), at(-1, 0))
        far = jnp.where(is_u, at(0, -2), at(2, 0)) - jnp.where(is_u, at(0, 2), at(-2, 0))
        part = (8.0 / 12.0) * near - (1.0 / 12.0) * far
        return part + pltpu.roll(part, half, 1)

    base = EDGE - LEAD
    lift = HV - HL
    none = jnp.zeros((8, lanes), F32)

    def first_step(m, _):
        for u in range(UNROLL):
            r = m * UNROLL + u
            absolute = spin[r] + zeta(vel, r + lift, base)
            mid[r, 0:8, :] = none
            mid[r, 8 + inner :, :] = none
            mid[r, 8 : 8 + inner, :] = vel[r + lift, base : base + inner, :] + STEP * (absolute * drift[r])
        return 0

    lax.fori_loop(0, listed // UNROLL, first_step, 0)

    at = iota((2 * lanes, lanes), 0)
    to = iota((2 * lanes, lanes), 1)
    average = jnp.where((at % lanes) // half == to % 2, 1.0 / half, 0.0).astype(BF)
    total = jnp.zeros((inner, lanes), F32)
    for n in range(rows + 2):
        r = n + HL - 1
        absolute = spin[r] + zeta(mid, r, 8)
        old = vel[r + lift, base : base + inner, :] + mid[r, 8 : 8 + inner, :]
        new = 0.5 * old + (0.5 * STEP) * (absolute * drift[r])
        sums = jnp.dot(jnp.concatenate(split(new), axis=1), average, preferred_element_type=F32)
        total = jnp.where(lane // 2 == n, sums, total)
        if 1 <= n <= rows:
            out[n - 1] = new[LEAD : LEAD + cols]

    at, to = iota((inner, lanes), 0), iota((inner, lanes), 1)
    reach = (RY + 2) * wc
    chosen = ((to < reach) & (at == RY * (to % wc) + to // wc + LEAD - 1)).astype(F32).astype(BF)
    picked[...] = sum(
        lax.dot_general(p, chosen, ROWS_DOT, preferred_element_type=F32) for p in split3(total)
    )
    at, to = iota((lanes, lanes), 0), iota((lanes, lanes), 1)
    spread = ((at < reach) & (at % wc == to)).astype(F32).astype(BF)
    offset = lane // wc
    for c in range(2):
        summed = jnp.zeros((wr, lanes), F32)
        for near in range(RX + 2):
            share = jnp.zeros((wr, lanes), F32)
            for k in range(K):
                share = share + jnp.where(wave_codes[k] == near * (RY + 2) + offset, wave_shares[k], 0.0)
            summed = summed + share * picked[pl.ds(2 * near + c, wr, stride=2 * RX), :]
        sums = sum(jnp.dot(p, spread, preferred_element_type=F32) for p in split3(summed))
        current[c] = sums[:, 0:wc]


UNROLL = 19
VMEM = pl.BlockSpec(memory_space=pltpu.VMEM)
PARAMS = pltpu.CompilerParams(vmem_limit_bytes=40 << 20)


def call(kernel, name, outs, *args, scratch=()):
    return pl.pallas_call(
        kernel,
        out_shape=tuple(jax.ShapeDtypeStruct(shape, dtype) for shape, dtype in outs),
        in_specs=[VMEM] * len(args),
        out_specs=tuple([VMEM] * len(outs)),
        scratch_shapes=list(scratch),
        compiler_params=PARAMS,
        name=name,
    )(*args)


def shards(
    spectrum, courant, source, wave_land, stokes_kernel, velocity, coriolis,
    ocean_codes, ocean_weights, wave_codes, wave_weights,
):
    wr, wc, bins = spectrum.shape
    rows, cols, lanes = velocity.shape
    listed = rows + 2 * HL

    with jax.named_scope("spectrum_edges"):
        edge = ((wc, bins), BF)
        xa, xb, ya, yb = call(edges_kernel, "edges", [edge] * 2 + [((wr, bins), BF)] * 2, spectrum)
        xa, xb = exchange("gx", xa, xb)
        ya, yb = exchange("gy", ya, yb)

    with jax.named_scope("lists"):
        codes = jnp.transpose(ocean_codes, (0, 2, 1)).astype(BF)
        weights = jnp.transpose(ocean_weights, (0, 2, 1))
        shares = (weights / jnp.sum(weights, axis=1, keepdims=True)).astype(BF)
        high, low = split(coriolis)
        spare = jnp.zeros((rows, 16 - 2 * K - 2, cols), BF)
        lists = jnp.concatenate([codes, shares, high[:, None], low[:, None], spare], axis=1)
        lists = jnp.pad(lists, ((0, 0), (0, 0), (LEAD, lanes - LEAD - cols)))

    with jax.named_scope("ocean_edges"):
        size = (HV + 1) * cols + HL * 16
        oa, ob = call(ocean_edges_kernel, "ocean_edges", [((size, lanes), BF)] * 2, velocity, lists)
        oa, ob = exchange("gx", oa, ob)

    with jax.named_scope("wave"):
        new_spectrum, profiles, pa, pb = call(
            wave_kernel, "wave",
            [(spectrum.shape, BF), ((wr, wc, lanes), BF), ((HX, wc, lanes), BF), ((HX, wc, lanes), BF)],
            spectrum, xa, xb, ya, yb, courant, source.T, wave_land.T.astype(F32), stokes_kernel,
        )
        pa, pb = exchange("gx", pa, pb)

    with jax.named_scope("halo"):
        per = lanes // LEAD
        size = 24 * HY + (rows + 2 * HV) * EDGE + -(-listed // per) * 16
        ya, yb = call(
            halo_kernel, "halo", [((size, lanes), BF)] * 2, velocity, oa, ob, lists, profiles, pa, pb
        )
        ya, yb = exchange("gy", ya, yb)

    with jax.named_scope("wave_lists"):
        reach = RY + 2
        wc_t = jnp.transpose(wave_codes, (2, 0, 1))
        ww_t = jnp.transpose(wave_weights, (2, 0, 1))
        ww_t = ww_t / jnp.sum(ww_t, axis=0, keepdims=True)
        spare = [(0, 0), (0, 0), (0, lanes - reach * wc)]
        wc_t = jnp.pad(jnp.tile(wc_t, (1, 1, reach)), spare)
        ww_t = jnp.pad(jnp.tile(ww_t, (1, 1, reach)), spare)

    with jax.named_scope("ocean"):
        wide = cols + 2 * EDGE
        inner = cols + 2 * LEAD
        prow = wr + 2 * HX
        scratch = [
            pltpu.VMEM((rows + 2 * HV, wide, lanes), F32),
            pltpu.VMEM((listed, inner + 16, lanes), F32),
            pltpu.VMEM((prow * WIDE, lanes), F32),
            pltpu.VMEM((prow - 2, 3 * WIDE + 8, 2 * lanes), BF),
            pltpu.VMEM((listed, 16, lanes), F32),
            pltpu.VMEM((listed, inner, lanes), F32),
            pltpu.VMEM((listed, inner, lanes), F32),
            pltpu.VMEM((8, lanes), F32),
            pltpu.VMEM((lanes, lanes), F32),
        ]
        new_velocity, current = call(
            ocean_kernel, "ocean", [(velocity.shape, F32), ((2, wr, wc), F32)],
            velocity, oa, ob, lists, profiles, pa, pb, ya, yb, wc_t, ww_t, scratch=scratch,
        )
    return new_spectrum, new_velocity, current


def solution(mesh):
    return jax.shard_map(
        shards,
        mesh=mesh,
        in_specs=(
            P("gx", "gy", None), P(), P("gx", "gy"), P("gx", "gy"), P(), P("gx", "gy", None),
            P("gx", "gy"), P("gx", "gy", None), P("gx", "gy", None), P("gx", "gy", None), P("gx", "gy", None),
        ),
        out_specs=(P("gx", "gy", None), P("gx", "gy", None), P(None, "gx", "gy")),
        check_vma=False,
    )
```

```python
import jax
import jax.numpy as jnp
from jax import lax
from jax.experimental import pallas as pl
from jax.experimental.pallas import tpu as pltpu
from jax.sharding import PartitionSpec as P

K = 4
RX = 2
RY = 4
STEP = 0.5
TALL = 24
RIM = 4
HV, HL = 5, 3
HX, HY = 3, 2
EDGE = 8
BF = jnp.bfloat16
F32 = jnp.float32
ROWS_DOT = (((0,), (0,)), ((), ()))


def partner(i, count, parity):
    return (i ^ 1) if parity == 0 else ((i + 1) ^ 1) - 1


def swap(value, axis, parity):
    nx, ny = lax.axis_size("gx"), lax.axis_size("gy")
    pairs = []
    for x in range(nx):
        for y in range(ny):
            tx, ty = x, y
            if axis == "gx":
                tx = partner(x, nx, parity) % nx
            else:
                ty = partner(y, ny, parity)
                if not 0 <= ty < ny:
                    tx, ty = x ^ 1, y
            pairs.append((x * ny + y, tx * ny + ty))
    return lax.ppermute(value, ("gx", "gy"), pairs)


def exchange(axis, to_a, to_b):
    from_b = swap(to_b, axis, 1)
    from_a = swap(to_a, axis, 0)
    return from_a, from_b


def is_even(axis):
    return lax.axis_index(axis) % 2 == 0


def inside(axis):
    index = lax.axis_index(axis)
    before = jnp.where(index == 0, 0.0, 1.0).astype(F32)
    after = jnp.where(index == lax.axis_size(axis) - 1, 0.0, 1.0).astype(F32)
    return before, after


def pick(cond, one, other):
    return jnp.where(cond, one.astype(F32), other.astype(F32))


def split(value):
    high = value.astype(BF)
    return high, (value - high.astype(F32)).astype(BF)


def split3(value):
    high = value.astype(BF)
    rest = value - high.astype(F32)
    middle = rest.astype(BF)
    return high, middle, (rest - middle.astype(F32)).astype(BF)


def iota(shape, dim):
    return lax.broadcasted_iota(jnp.int32, shape, dim)


def edges_kernel(*refs):
    count = (len(refs) - 5) // 2
    given, (xa, xb, ya, yb), kept, sems = refs[:count], refs[count : count + 4], refs[count + 4 : -1], refs[-1]
    copies = [pltpu.make_async_copy(v, k, sems.at[i]) for i, (v, k) in enumerate(zip(given, kept))]
    for copy in copies:
        copy.start()
    copies[0].wait()
    spec = kept[0]
    rows, cols, bins = spec.shape
    even_x, even_y = is_even("gx"), is_even("gy")
    first, last = spec[0].astype(F32), spec[rows - 1].astype(F32)
    xa[...] = jnp.where(even_x, last, first).astype(BF)
    xb[...] = jnp.where(even_x, first, last).astype(BF)
    at, cell = iota((2 * rows, rows * cols), 0), iota((2 * rows, rows * cols), 1)
    wanted = jnp.where(at < rows, at * cols, (at - rows) * cols + cols - 1)
    chosen = (cell == wanted).astype(F32).astype(BF)
    sides = jnp.dot(chosen, spec[...].reshape(rows * cols, bins), preferred_element_type=F32)
    first, last = sides[0:rows], sides[rows:]
    ya[...] = jnp.where(even_y, last, first).astype(BF)
    yb[...] = jnp.where(even_y, first, last).astype(BF)
    for copy in copies[1:]:
        copy.wait()


def ocean_edges_kernel(vel_far, given, codes, weights, coriolis, xa, xb, lists, vel, kept, sems):
    rows, cols, lanes = vel.shape
    copies = [pltpu.make_async_copy(vel_far, vel, sems.at[0]), pltpu.make_async_copy(given, kept, sems.at[1])]
    for copy in copies:
        copy.start()
    even = is_even("gx")
    for r in range(rows):
        lists[r] = jnp.zeros((16, lanes), F32)
        weight = weights[r]
        turn = coriolis[r : r + 1, :]
        high = turn.astype(BF).astype(F32)
        lists[r, 0:K, 0:cols] = codes[r].astype(F32)
        lists[r, K : 2 * K, 0:cols] = weight / jnp.sum(weight, axis=0, keepdims=True)
        lists[r, 2 * K : 2 * K + 1, 0:cols] = high
        lists[r, 2 * K + 1 : 2 * K + 2, 0:cols] = turn - high

    copies[0].wait()

    def put(at, last, first):
        n = last.shape[0]
        xa[at : at + n] = jnp.where(even, last, first).astype(BF)
        xb[at : at + n] = jnp.where(even, first, last).astype(BF)

    for i in range(HV):
        put(i * cols, vel[rows - HV + i], vel[i])
    last, first = vel[rows - 1], vel[0]
    put(HV * cols, last - last.astype(BF).astype(F32), first - first.astype(BF).astype(F32))
    for i in range(HL):
        put((HV + 1) * cols + i * 16, lists[rows - HL + i], lists[i])
    copies[1].wait()


def wave_kernel(spec, xa, xb, ya, yb, courant, source, land, weights, out, profile, pa, pb):
    rows, cols, _ = spec.shape
    even_x, even_y = is_even("gx"), is_even("gy")
    has_south, has_north = inside("gy")
    west, east = pick(even_x, xb[...], xa[...]), pick(even_x, xa[...], xb[...])
    south = pick(even_y, yb[...], ya[...]) * has_south
    north = pick(even_y, ya[...], yb[...]) * has_north
    cx, cy = courant[0:1, :], courant[1:2, :]
    ax, ay = jnp.abs(cx), jnp.abs(cy)
    from_west, from_south = cx > 0.0, cy > 0.0
    keep = 1.0 - ax - ay
    sub = iota((cols, 1), 0)
    parts = []
    for x in range(rows):
        center = spec[x].astype(F32)
        before = spec[x - 1].astype(F32) if x else west
        after = spec[x + 1].astype(F32) if x < rows - 1 else east
        below = jnp.where(sub == 0, south[x : x + 1, :], pltpu.roll(center, 1, 0))
        above = jnp.where(sub == cols - 1, north[x : x + 1, :], pltpu.roll(center, cols - 1, 0))
        advected = (
            keep * center
            + ax * jnp.where(from_west, before, after)
            + ay * jnp.where(from_south, below, above)
        )
        wind = 1.0 + 0.2 * source[:, x : x + 1]
        updated = land[:, x : x + 1] * (advected * (wind - 0.1 * advected))
        updated = updated.astype(BF)
        out[x] = updated
        part = jnp.dot(updated, weights[...], preferred_element_type=F32).astype(BF)
        profile[x] = part
        parts.append(part.astype(F32))
    for i in range(HX):
        first, last = parts[i], parts[rows - HX + i]
        pa[i] = jnp.where(even_x, last, first).astype(BF)
        pb[i] = jnp.where(even_x, first, last).astype(BF)


def list_place(r, lanes):
    per = lanes // 16
    return r // (4 * per), (r % per) * 16 + RIM * ((r // per) % 4)


def halo_kernel(vel, oa, ob, lists, profile, pa, pb, ya, yb):
    rows, cols, lanes = vel.shape
    even_x, even_y = is_even("gx"), is_even("gy")
    wr, wc = profile.shape[0], profile.shape[1]

    def put(at, last, first):
        n = last.shape[0]
        ya[at : at + n] = jnp.where(even_y, last, first).astype(BF)
        yb[at : at + n] = jnp.where(even_y, first, last).astype(BF)

    before, after = pick(even_x, pb[...], pa[...]), pick(even_x, pa[...], pb[...])
    joined = jnp.concatenate([before.astype(BF), profile[...], after.astype(BF)], axis=0)
    count = (wr + 2 * HX) * wc
    slots = TALL * HY
    at, cell = iota((2 * slots, count), 0), iota((2 * slots, count), 1)
    side, rest = at // slots, at % slots
    column = rest // TALL + jnp.where(side == 0, wc - HY, 0)
    row = rest % TALL
    chosen = ((row < wr + 2 * HX) & (cell == row * wc + column)).astype(F32).astype(BF)
    sides = jnp.dot(chosen, joined.reshape(count, lanes), preferred_element_type=F32)
    put(0, sides[0:slots], sides[slots:])

    sub = iota((EDGE, 1), 0)
    blocks = []
    low_at = HV * cols
    for r in range(rows + 2 * HV):
        if HV <= r < HV + rows:
            last, first = vel[r - HV, cols - EDGE : cols, :], vel[r - HV, 0:EDGE, :]
            low_last = last - last.astype(BF).astype(F32)
            low_first = first - first.astype(BF).astype(F32)
        else:
            i = r if r < HV else r - HV - rows
            one, two = (ob, oa) if r < HV else (oa, ob)

            def ends(start):
                both = pick(even_x, one[start : start + cols, :], two[start : start + cols, :])
                return both[cols - EDGE :], both[0:EDGE]

            last, first = ends(i * cols)
            if r in (HV - 1, HV + rows):
                low_last, low_first = ends(low_at)
            else:
                low_last = low_first = jnp.zeros((EDGE, lanes), F32)
        last = jnp.where(sub == 0, pltpu.roll(low_last, 1, 0), last)
        first = jnp.where(sub == EDGE - 1, pltpu.roll(low_first, EDGE - 1, 0), first)
        blocks.append((last, first))
    for r in range(0, rows + 2 * HV, 2):
        put(
            slots + r * EDGE,
            jnp.concatenate([blocks[r][0], blocks[r + 1][0]], axis=0),
            jnp.concatenate([blocks[r][1], blocks[r + 1][1]], axis=0),
        )

    group = iota((1, lanes), 1) // RIM
    start = slots + (rows + 2 * HV) * EDGE
    tiles = list_place(rows + 2 * HL - 1, lanes)[0] + 1
    acc = [[jnp.zeros((16, lanes), F32)] * 2 for _ in range(tiles)]
    for r in range(rows + 2 * HL):
        if HL <= r < HL + rows:
            own = lists[r - HL]
        else:
            i = r if r < HL else r - HL - rows
            at = (HV + 1) * cols + i * 16
            one, two = (ob, oa) if r < HL else (oa, ob)
            own = pick(even_x, one[at : at + 16, :], two[at : at + 16, :])
        tile, to = list_place(r, lanes)
        acc[tile] = [
            jnp.where(group == to // RIM, pltpu.roll(own, (to - where) % lanes, 1), a)
            for a, where in zip(acc[tile], (cols - RIM, 0))
        ]
    for tile in range(tiles):
        put(start + tile * 16, acc[tile][0], acc[tile][1])


def vorticity(ref, r, base, count):
    half = ref.shape[-1] // 2
    is_u = iota((1, 2 * half), 1) < half

    def at(dx, dy):
        return ref[r + dx, base + dy : base + dy + count, :]

    near = jnp.where(is_u, at(0, -1), at(1, 0)) - jnp.where(is_u, at(0, 1), at(-1, 0))
    far = jnp.where(is_u, at(0, -2), at(2, 0)) - jnp.where(is_u, at(0, 2), at(-2, 0))
    part = (8.0 / 12.0) * near - (1.0 / 12.0) * far
    return part + pltpu.roll(part, half, 1)


def averager(lanes):
    at = iota((2 * lanes, lanes), 0)
    to = iota((2 * lanes, lanes), 1)
    half = lanes // 2
    return jnp.where((at % lanes) // half == to % 2, 1.0 / half, 0.0).astype(BF)


def turned(value):
    half = value.shape[-1] // 2
    sign = jnp.where(iota((1, 2 * half), 1) < half, 1.0, -1.0)
    return pltpu.roll(value, half, 1) * sign


def prepare_kernel(own, oa, ob, lists, vel, spin, turn, table, list_rim):
    rows, cols, lanes = own.shape
    wc = cols // RY
    listed = rows + 2 * HL
    unroll = listed // 2
    even_x = is_even("gx")
    lane = iota((1, lanes), 1)

    def from_x(r, halo, start, n):
        one, two = (ob, oa) if r < halo else (oa, ob)
        return pick(even_x, one[start : start + n, :], two[start : start + n, :])

    blank = jnp.zeros((EDGE, lanes), F32)

    def fill(r, _):
        vel[r + HV, EDGE : EDGE + cols, :] = own[r]
        return 0

    lax.fori_loop(0, rows, fill, 0, unroll=4)
    for r in range(rows + 2 * HV):
        vel[r, 0:EDGE, :] = blank
        vel[r, EDGE + cols :, :] = blank
    for r in range(HV):
        vel[r, EDGE : EDGE + cols, :] = from_x(r, HV, r * cols, cols)
        vel[HV + rows + r, EDGE : EDGE + cols, :] = from_x(HV, HV, r * cols, cols)
    vel[HV - 1, EDGE : EDGE + cols, :] += from_x(0, HV, HV * cols, cols)
    vel[HV + rows, EDGE : EDGE + cols, :] += from_x(HV, HV, HV * cols, cols)

    sub16 = iota((16, 1), 0)
    place_of = (lane // RY).astype(F32) - 1.0
    per = lanes // 16
    rim = jnp.zeros((16, lanes), F32)
    for r in range(listed):
        if HL <= r < HL + rows:
            full = lists[r - HL]
        else:
            i = r if r < HL else r - HL - rows
            full = from_x(0 if r < HL else HL, HL, (HV + 1) * cols + i * 16, 16)
        third = jnp.where(full >= 6.0, 2.0, jnp.where(full >= 3.0, 1.0, 0.0))
        table[r] = jnp.where(sub16 < K, third * (wc - 3.0) + full + place_of, full)
        to = (r % per) * 16
        rim = jnp.where(lane // RIM == to // RIM + 1, pltpu.roll(full, (to + RIM) % lanes, 1), rim)
        rim = jnp.where(lane // RIM == to // RIM + 2, pltpu.roll(full, (to + 3 * RIM - cols) % lanes, 1), rim)
        if r % per == per - 1 or r == listed - 1:
            list_rim[r // per] = rim
            rim = jnp.zeros((16, lanes), F32)

    ones = jnp.ones((8, lanes), BF)

    def absolute(m, _):
        for u in range(unroll):
            r = m * unroll + u
            wide = lax.dot_general(table[r, 2 * K :, :].astype(BF), ones, ROWS_DOT, preferred_element_type=F32)
            spin[r] = wide[0:cols]
            turn[r] = wide[0:cols] + vorticity(vel, r + HV - HL, EDGE, cols)
        return 0

    lax.fori_loop(0, listed // unroll, absolute, 0)


def inner_kernel(
    vel, spin, turn, table, profile, pa, pb,
    out, mid_rim, drift_rim, spin_rim, total, prof_rim,
    mid, names, prof, drift,
):
    rows, cols, lanes = out.shape
    wr, wc = profile.shape[0], profile.shape[1]
    listed = rows + 2 * HL
    prow = wr + 2 * HX
    unroll = listed // 2
    even_x = is_even("gx")
    lane = iota((1, lanes), 1)
    blank = jnp.zeros((EDGE, lanes), F32)
    for x in range(prow):
        if HX <= x < HX + wr:
            part = profile[x - HX].astype(F32)
        elif x < HX:
            part = pick(even_x, pb[x], pa[x])
        else:
            part = pick(even_x, pa[x - HX - wr], pb[x - HX - wr])
        part = turned(part)
        prof[x * wc : (x + 1) * wc, :] = part
        names[x * wc : (x + 1) * wc, :] = part.astype(BF)
    prof_rim[...] = jnp.zeros(prof_rim.shape, F32)
    for c in range(HY):
        prof_rim[0, pl.ds(HY + c, prow, stride=2 * HY), :] = prof[pl.ds(c, prow, stride=wc), :]
        prof_rim[1, pl.ds(c, prow, stride=2 * HY), :] = prof[pl.ds(wc - HY + c, prow, stride=wc), :]

    block = 3 * wc
    place = iota((block, lanes), 0).astype(F32)
    lift = HV - HL

    def first_step(m, _):
        for u in range(unroll):
            r = m * unroll + u
            hot = jnp.where(place == table[r, 0:1, :], table[r, K : K + 1, :], 0.0)
            for k in range(1, K):
                hot = hot + jnp.where(place == table[r, k : k + 1, :], table[r, K + k : K + k + 1, :], 0.0)
            named = names[pl.ds(pl.multiple_of((r + 1) // 2 * wc, wc), block), :]
            stokes = lax.dot_general(hot.astype(BF), named, ROWS_DOT, preferred_element_type=F32)[0:cols]
            drift[r] = stokes
            new = vel[r + lift, EDGE : EDGE + cols, :] + STEP * (turn[r] * stokes)
            mid[r, 0:EDGE, :] = blank
            mid[r, EDGE + cols :, :] = blank
            mid[r, EDGE : EDGE + cols, :] = new
            mid_rim[r, 0] = new[0 : 2 * EDGE]
            mid_rim[r, 1] = new[cols - 2 * EDGE :]
            for where in range(2):
                begin = RIM if where == 0 else cols - RIM - EDGE
                drift_rim[r, where] = drift[r, begin : begin + EDGE, :]
                spin_rim[r, where] = spin[r, begin : begin + EDGE, :]
        return 0

    lax.fori_loop(0, listed // unroll, first_step, 0)

    average = averager(lanes)
    means = jnp.zeros((cols, lanes), F32)
    for n in range(rows + 2):
        r = n + HL - 1
        absolute = spin[r] + vorticity(mid, r, EDGE, cols)
        old = vel[r + lift, EDGE : EDGE + cols, :] + mid[r, EDGE : EDGE + cols, :]
        new = 0.5 * old + (0.5 * STEP) * (absolute * drift[r])
        sums = jnp.dot(jnp.concatenate(split(new), axis=1), average, preferred_element_type=F32)
        means = jnp.where(lane // 2 == n, sums, means)
        if 1 <= n <= rows:
            out[n - 1] = new
    total[...] = means


def rim_kernel(
    own, oa, ob, ya, yb, mid_rim, drift_rim, spin_rim, total, list_rim, prof_rim,
    wave_codes, wave_shares, velocity_in,
    velocity_out, current,
    vel, mid, prof, drift, spin, picked, means, strips, sems,
):
    rows, cols, lanes = own.shape
    wr, wc = wave_codes.shape[1], current.shape[2]
    listed = rows + 2 * HL
    prow = wr + 2 * HX
    wide = 3 * EDGE
    even_x, even_y = is_even("gx"), is_even("gy")
    has_south, has_north = inside("gy")
    lane = iota((1, lanes), 1)
    sub = iota((EDGE, 1), 0)
    slots = TALL * HY

    def from_x(r, halo, start, n):
        one, two = (ob, oa) if r < halo else (oa, ob)
        return pick(even_x, one[start : start + n, :], two[start : start + n, :])

    def from_y(start, n):
        a, b = ya[start : start + n, :], yb[start : start + n, :]
        return pick(even_y, b, a) * has_south, pick(even_y, a, b) * has_north

    for r in range(rows + 2 * HV):
        if HV <= r < HV + rows:
            near, far = own[r - HV, 0 : 2 * EDGE, :], own[r - HV, cols - 2 * EDGE :, :]
        else:
            i = r if r < HV else r - HV - rows
            at = 0 if r < HV else HV
            near = from_x(at, HV, i * cols, 2 * EDGE)
            far = from_x(at, HV, (i + 1) * cols - 2 * EDGE, 2 * EDGE)
            if r in (HV - 1, HV + rows):
                near = near + from_x(at, HV, HV * cols, 2 * EDGE)
                far = far + from_x(at, HV, (HV + 1) * cols - 2 * EDGE, 2 * EDGE)
        vel[0, r, EDGE:, :] = near
        vel[1, r, 0 : 2 * EDGE, :] = far
    for r in range(0, rows + 2 * HV, 2):
        south, north = from_y(slots + r * EDGE, 2 * EDGE)
        for i in range(2):
            low, high = south[i * EDGE : i * EDGE + EDGE], north[i * EDGE : i * EDGE + EDGE]
            low = jnp.where(sub == 0, 0.0, low) + jnp.where(sub == EDGE - 1, pltpu.roll(low, EDGE - 1, 0), 0.0)
            high = jnp.where(sub == EDGE - 1, 0.0, high) + jnp.where(sub == 0, pltpu.roll(high, 1, 0), 0.0)
            vel[0, r + i, 0:EDGE, :] = low
            vel[1, r + i, 2 * EDGE :, :] = high

    prof[...] = prof_rim[...]
    south, north = from_y(0, slots)
    south, north = turned(south), turned(north)
    for c in range(HY):
        prof[0, pl.ds(c, TALL, stride=2 * HY), :] = south[TALL * c : TALL * (c + 1)]
        prof[1, pl.ds(HY + c, TALL, stride=2 * HY), :] = north[TALL * c : TALL * (c + 1)]

    per = lanes // 16
    start = slots + (rows + 2 * HV) * EDGE
    span = 2 * per * HY
    place = iota((2 * span, lanes), 0).astype(F32)
    part = lane % 16
    offset = (part // EDGE) * span + ((lane // 16 + 1) // 2) * (2 * HY) + (part % EDGE) // RIM
    sub16 = iota((16, 1), 0)
    ones = jnp.ones((8, lanes), F32)
    none = jnp.zeros((2 * span, lanes), F32)
    blank = jnp.zeros((8, lanes), F32)
    for g in range(-(-listed // per)):
        tile, to = list_place(g * per, lanes)
        south, north = from_y(start + tile * 16, 16)
        full = list_rim[g]
        full = jnp.where(part // RIM == 0, pltpu.roll(south, (-to) % lanes, 1), full)
        full = jnp.where(part // RIM == 3, pltpu.roll(north, (3 * RIM - to) % lanes, 1), full)
        third = jnp.where(full >= 6.0, 2.0, jnp.where(full >= 3.0, 1.0, 0.0))
        full = jnp.where(sub16 < K, third + full + offset.astype(F32), full)
        hot = jnp.zeros((2 * span, lanes), F32)
        for k in range(K):
            hot = hot + jnp.where(place == full[k : k + 1], full[K + k : K + k + 1], 0.0)
        left = jnp.concatenate([hot, full[2 * K :], blank], axis=0).astype(BF)
        begin = g * (per // 2) * 2 * HY
        named = jnp.concatenate([prof[0, begin : begin + span, :], prof[1, begin : begin + span, :]], axis=0)
        right = jnp.concatenate([
            jnp.concatenate([named, blank, blank], axis=0),
            jnp.concatenate([none, ones, blank], axis=0),
        ], axis=1).astype(BF)
        both = lax.dot_general(left, right, ROWS_DOT, preferred_element_type=F32)
        for i in range(min(per, listed - g * per)):
            for side in range(2):
                at = i * 16 + side * EDGE
                drift[side, g * per + i, side * EDGE : side * EDGE + EDGE, :] = both[at : at + EDGE, 0:lanes]
                spin[side, g * per + i, side * EDGE : side * EDGE + EDGE, :] = both[at : at + EDGE, lanes:]

    lift = HV - HL
    for r in range(listed):
        for side in range(2):
            base = RIM + side * EDGE
            drift[side, r, EDGE - side * EDGE : 2 * EDGE - side * EDGE, :] = drift_rim[r, side]
            spin[side, r, EDGE - side * EDGE : 2 * EDGE - side * EDGE, :] = spin_rim[r, side]
            mid[side, r, 2 * EDGE * side : 2 * EDGE * side + EDGE, :] = blank
            mid[side, r, EDGE - side * EDGE : wide - side * EDGE, :] = mid_rim[r, side]
            tile = slice(side * EDGE, side * EDGE + EDGE)
            absolute = spin[side, r, tile, :] + vorticity(vel.at[side], r + lift, base, EDGE)
            new = vel[side, r + lift, base : base + EDGE, :] + STEP * (absolute * drift[side, r, tile, :])
            mid[side, r, base : base + EDGE, :] = new

    average = averager(lanes)
    acc = jnp.zeros((4 * EDGE, lanes), F32)
    for n in range(rows + 2):
        r = n + HL - 1
        both = []
        for side in range(2):
            absolute = spin[side, r] + vorticity(mid.at[side], r, RIM, 2 * EDGE)
            tile = slice(RIM, RIM + 2 * EDGE)
            old = vel[side, r + lift, tile, :] + mid[side, r, tile, :]
            new = 0.5 * old + (0.5 * STEP) * (absolute * drift[side, r])
            both.append(new)
            if 1 <= n <= rows:
                strips[side, n - 1] = new[RIM : RIM + EDGE]
        sums = jnp.dot(
            jnp.concatenate(split(jnp.concatenate(both, axis=0)), axis=1), average, preferred_element_type=F32
        )
        acc = jnp.where(lane // 2 == n, sums, acc)
    copies = [
        pltpu.make_async_copy(strips.at[side], velocity_out.at[:, pl.ds(at, EDGE), :], sems.at[side])
        for side, at in ((0, 0), (1, cols - EDGE))
    ]
    for copy in copies:
        copy.start()
    means[0 : 2 * EDGE] = acc[0 : 2 * EDGE]
    means[2 * EDGE : 2 * RIM + cols - 2 * EDGE] = total[2 * EDGE - RIM : cols - 2 * EDGE + RIM, :]
    means[2 * RIM + cols - 2 * EDGE :] = acc[2 * EDGE :]

    count = cols + 2 * RIM
    at, to = iota((count, lanes), 0), iota((count, lanes), 1)
    reach = (RY + 2) * wc
    chosen = ((to < reach) & (at == RY * (to % wc) + to // wc + RIM - 1)).astype(F32).astype(BF)
    picked[...] = sum(
        lax.dot_general(p, chosen, ROWS_DOT, preferred_element_type=F32) for p in split3(means[...])
    )
    at, to = iota((lanes, lanes), 0), iota((lanes, lanes), 1)
    spread = ((at < reach) & (at % wc == to)).astype(F32).astype(BF)
    shift = lane // wc
    for c in range(2):
        summed = jnp.zeros((wr, lanes), F32)
        for near in range(RX + 2):
            share = jnp.zeros((wr, lanes), F32)
            for k in range(K):
                share = share + jnp.where(wave_codes[k] == near * (RY + 2) + shift, wave_shares[k], 0.0)
            summed = summed + share * picked[pl.ds(2 * near + c, wr, stride=2 * RX), :]
        sums = sum(jnp.dot(p, spread, preferred_element_type=F32) for p in split3(summed))
        current[c] = sums[:, 0:wc]
    for copy in copies:
        copy.wait()


VMEM = pl.BlockSpec(memory_space=pltpu.VMEM)
ANY = pl.BlockSpec(memory_space=pltpu.HBM)


def call(kernel, name, outs, *args, scratch=(), any_in=(), any_out=(), aliases=None):
    args = [pltpu.with_memory_space_constraint(v, pltpu.HBM) if i in any_in else v for i, v in enumerate(args)]
    return pl.pallas_call(
        kernel,
        out_shape=tuple(jax.ShapeDtypeStruct(shape, dtype) for shape, dtype in outs),
        in_specs=[ANY if i in any_in else VMEM for i in range(len(args))],
        out_specs=tuple(ANY if i in any_out else VMEM for i in range(len(outs))),
        scratch_shapes=list(scratch),
        input_output_aliases=aliases or {},
        compiler_params=pltpu.CompilerParams(vmem_limit_bytes=28 << 20),
        name=name,
    )(*args)


def shards(
    spectrum, courant, source, wave_land, stokes_kernel, velocity, coriolis,
    ocean_codes, ocean_weights, wave_codes, wave_weights,
):
    wr, wc, bins = spectrum.shape
    rows, cols, lanes = velocity.shape
    listed = rows + 2 * HL
    prow = wr + 2 * HX

    with jax.named_scope("spectrum_edges"):
        edge = ((wc, bins), BF)
        raw = [
            spectrum, courant, source, wave_land, coriolis,
            jnp.transpose(ocean_codes, (0, 2, 1)), jnp.transpose(ocean_weights, (0, 2, 1)),
        ]
        xa, xb, ya, yb, spectrum, courant, source, wave_land, coriolis, codes, weights = call(
            edges_kernel, "edges",
            [edge] * 2 + [((wr, bins), BF)] * 2 + [(v.shape, v.dtype) for v in raw],
            *raw, any_in=range(len(raw)), scratch=[pltpu.SemaphoreType.DMA((len(raw),))],
        )
        xa, xb = exchange("gx", xa, xb)
        ya, yb = exchange("gy", ya, yb)

    with jax.named_scope("ocean_edges"):
        size = (HV + 1) * cols + HL * 16
        oa, ob, lists, velocity, stokes_kernel = call(
            ocean_edges_kernel, "ocean_edges",
            [((size, lanes), BF)] * 2
            + [((rows, 16, lanes), F32), (velocity.shape, F32), (stokes_kernel.shape, BF)],
            velocity, stokes_kernel, codes, weights, coriolis,
            any_in=(0, 1), scratch=[pltpu.SemaphoreType.DMA((2,))],
        )
        oa, ob = exchange("gx", oa, ob)

    with jax.named_scope("wave"):
        new_spectrum, profiles, pa, pb = call(
            wave_kernel, "wave",
            [(spectrum.shape, BF), ((wr, wc, lanes), BF), ((HX, wc, lanes), BF), ((HX, wc, lanes), BF)],
            spectrum, xa, xb, ya, yb, courant, source.T, wave_land.T.astype(F32), stokes_kernel,
        )
        pa, pb = exchange("gx", pa, pb)

    with jax.named_scope("halo"):
        size = TALL * HY + (rows + 2 * HV) * EDGE + (list_place(listed - 1, lanes)[0] + 1) * 16
        ya, yb = call(
            halo_kernel, "halo", [((size, lanes), BF)] * 2, velocity, oa, ob, lists, profiles, pa, pb
        )
        ya, yb = exchange("gy", ya, yb)

    with jax.named_scope("wave_lists"):
        reach = RY + 2
        wc_t = jnp.transpose(wave_codes, (2, 0, 1))
        ww_t = jnp.transpose(wave_weights, (2, 0, 1))
        ww_t = ww_t / jnp.sum(ww_t, axis=0, keepdims=True)
        spare = [(0, 0), (0, 0), (0, lanes - reach * wc)]
        wc_t = jnp.pad(jnp.tile(wc_t, (1, 1, reach)), spare)
        ww_t = jnp.pad(jnp.tile(ww_t, (1, 1, reach)), spare)

    with jax.named_scope("prepare"):
        wide = cols + 2 * EDGE
        groups = -(-listed // (lanes // 16))
        vel, spin, turn, table, list_rim = call(
            prepare_kernel, "prepare",
            [
                ((rows + 2 * HV, wide, lanes), F32),
                ((listed, cols, lanes), F32),
                ((listed, cols, lanes), F32),
                ((listed, 16, lanes), F32),
                ((groups, 16, lanes), F32),
            ],
            velocity, oa, ob, lists,
        )

    with jax.named_scope("inner"):
        scratch = [
            pltpu.VMEM((listed, wide, lanes), F32),
            pltpu.VMEM((prow * wc, lanes), BF),
            pltpu.VMEM((prow * wc, lanes), F32),
            pltpu.VMEM((listed, cols, lanes), F32),
        ]
        new_velocity, mid_rim, drift_rim, spin_rim, total, prof_rim = call(
            inner_kernel, "inner",
            [
                (velocity.shape, F32),
                ((listed, 2, 2 * EDGE, lanes), F32),
                ((listed, 2, EDGE, lanes), F32),
                ((listed, 2, EDGE, lanes), F32),
                ((cols, lanes), F32),
                ((2, 2 * HY * (TALL + 4), lanes), F32),
            ],
            vel, spin, turn, table, profiles, pa, pb, scratch=scratch,
        )

    with jax.named_scope("rim"):
        scratch = [
            pltpu.VMEM((2, rows + 2 * HV, 3 * EDGE, lanes), F32),
            pltpu.VMEM((2, listed, 3 * EDGE, lanes), F32),
            pltpu.VMEM((2, 2 * HY * (TALL + 4), lanes), F32),
            pltpu.VMEM((2, listed, 2 * EDGE, lanes), F32),
            pltpu.VMEM((2, listed, 2 * EDGE, lanes), F32),
            pltpu.VMEM((lanes, lanes), F32),
            pltpu.VMEM((cols + 2 * RIM, lanes), F32),
            pltpu.VMEM((2, rows, EDGE, lanes), F32),
            pltpu.SemaphoreType.DMA((2,)),
        ]
        new_velocity, current = call(
            rim_kernel, "rim", [(velocity.shape, F32), ((2, wr, wc), F32)],
            velocity, oa, ob, ya, yb, mid_rim, drift_rim, spin_rim, total, list_rim, prof_rim, wc_t, ww_t, new_velocity,
            scratch=scratch, any_in=(13,), any_out=(0,), aliases={13: 0},
        )
    return new_spectrum, new_velocity, current


def solution(mesh):
    return jax.shard_map(
        shards,
        mesh=mesh,
        in_specs=(
            P("gx", "gy", None), P(), P("gx", "gy"), P("gx", "gy"), P(), P("gx", "gy", None),
            P("gx", "gy"), P("gx", "gy", None), P("gx", "gy", None), P("gx", "gy", None), P("gx", "gy", None),
        ),
        out_specs=(P("gx", "gy", None), P("gx", "gy", None), P(None, "gx", "gy")),
        check_vma=False,
    )
```

```python
import jax
import jax.numpy as jnp
from jax import lax
from jax.experimental import pallas as pl
from jax.experimental.pallas import tpu as pltpu
from jax.sharding import PartitionSpec as P

K = 4
RX = 2
RY = 4
STEP = 0.5
TALL = 24
RIM = 4
HV, HL = 5, 3
HX, HY = 3, 2
EDGE = 8
BF = jnp.bfloat16
F32 = jnp.float32
ROWS_DOT = (((0,), (0,)), ((), ()))


def partner(i, count, parity):
    return (i ^ 1) if parity == 0 else ((i + 1) ^ 1) - 1


def swap(value, axis, parity):
    nx, ny = lax.axis_size("gx"), lax.axis_size("gy")
    pairs = []
    for x in range(nx):
        for y in range(ny):
            tx, ty = x, y
            if axis == "gx":
                tx = partner(x, nx, parity) % nx
            else:
                ty = partner(y, ny, parity)
                if not 0 <= ty < ny:
                    tx, ty = x ^ 1, y
            pairs.append((x * ny + y, tx * ny + ty))
    return lax.ppermute(value, ("gx", "gy"), pairs)


def exchange(axis, to_a, to_b):
    from_b = swap(to_b, axis, 1)
    from_a = swap(to_a, axis, 0)
    return from_a, from_b


def is_even(axis):
    return lax.axis_index(axis) % 2 == 0


def inside(axis):
    index = lax.axis_index(axis)
    before = jnp.where(index == 0, 0.0, 1.0).astype(F32)
    after = jnp.where(index == lax.axis_size(axis) - 1, 0.0, 1.0).astype(F32)
    return before, after


def pick(cond, one, other):
    return jnp.where(cond, one.astype(F32), other.astype(F32))


def split(value):
    high = value.astype(BF)
    return high, (value - high.astype(F32)).astype(BF)


def split3(value):
    high = value.astype(BF)
    rest = value - high.astype(F32)
    middle = rest.astype(BF)
    return high, middle, (rest - middle.astype(F32)).astype(BF)


def iota(shape, dim):
    return lax.broadcasted_iota(jnp.int32, shape, dim)


def x_rows(cols):
    return (HV - 1) * cols, cols, HL * 16


def edges_kernel(*refs):
    (spec_far, courant_far, source_far, land_far, codes_far, weights_far, coriolis_far, vel_far) = refs[:8]
    (xa, xb, ya, yb, oa, ob, lists, spec, courant, source, land, codes, weights, coriolis, vel, sems) = refs[8:]
    rows, cols, bins = spec.shape
    lanes = vel.shape[-1]
    pairs = [(spec_far, spec)]
    pairs += [(vel_far.at[pl.ds(at, HV)], vel.at[i]) for i, at in ((0, 0), (1, vel_far.shape[0] - HV))]
    pairs += [(codes_far, codes), (weights_far, weights), (coriolis_far, coriolis)]
    pairs += [(courant_far, courant), (source_far, source), (land_far, land)]
    copies = [pltpu.make_async_copy(one, two, sems.at[i]) for i, (one, two) in enumerate(pairs)]
    for copy in copies:
        copy.start()
    even_x, even_y = is_even("gx"), is_even("gy")

    def put(at, last, first):
        n = last.shape[0]
        oa[at : at + n] = jnp.where(even_x, last, first).astype(BF)
        ob[at : at + n] = jnp.where(even_x, first, last).astype(BF)

    at, cell = iota((2 * rows, rows * cols), 0), iota((2 * rows, rows * cols), 1)
    wanted = jnp.where(at < rows, at * cols, (at - rows) * cols + cols - 1)
    chosen = (cell == wanted).astype(F32).astype(BF)
    copies[0].wait()
    sides = jnp.dot(chosen, spec[...].reshape(rows * cols, bins), preferred_element_type=F32)
    first, last = spec[0].astype(F32), spec[rows - 1].astype(F32)
    xa[...] = jnp.where(even_x, last, first).astype(BF)
    xb[...] = jnp.where(even_x, first, last).astype(BF)
    first, last = sides[0:rows], sides[rows:]
    ya[...] = jnp.where(even_y, last, first).astype(BF)
    yb[...] = jnp.where(even_y, first, last).astype(BF)

    for copy in copies[1:]:
        copy.wait()
    listed, wide = codes.shape[0], codes.shape[2]
    is_u = iota((1, lanes), 1) < lanes // 2
    outer = [
        jnp.where(is_u, pltpu.roll(vel[side, one], lanes // 2, 1), vel[side, two])
        for side, one, two in ((1, 0, 1), (0, HV - 1, HV - 2))
    ]
    put(0, *outer)
    for i in range(1, HV - 1):
        put(i * wide, vel[1, i + 1], vel[0, i - 1])
    last, first = vel[1, HV - 1], vel[0, 0]
    put((HV - 1) * wide, last - last.astype(BF).astype(F32), first - first.astype(BF).astype(F32))
    for r in range(listed):
        lists[r] = jnp.zeros((16, lanes), F32)
        weight = weights[r]
        turn = coriolis[r : r + 1, :]
        high = turn.astype(BF).astype(F32)
        lists[r, 0:K, 0:wide] = codes[r].astype(F32)
        lists[r, K : 2 * K, 0:wide] = weight / jnp.sum(weight, axis=0, keepdims=True)
        lists[r, 2 * K : 2 * K + 1, 0:wide] = high
        lists[r, 2 * K + 1 : 2 * K + 2, 0:wide] = turn - high
    for i in range(HL):
        put(HV * wide + i * 16, lists[listed - HL + i], lists[i])


def wave_kernel(spec, xa, xb, ya, yb, courant, source, land, weights_far, vel_far, out, profile, pa, pb, vel, weights, sems):
    rows, cols, bins = spec.shape
    copies = [pltpu.make_async_copy(weights_far, weights, sems.at[0]), pltpu.make_async_copy(vel_far, vel, sems.at[1])]
    for copy in copies:
        copy.start()
    even_x, even_y = is_even("gx"), is_even("gy")
    has_south, has_north = inside("gy")
    west, east = pick(even_x, xb[...], xa[...]), pick(even_x, xa[...], xb[...])
    south = pick(even_y, yb[...], ya[...]) * has_south
    north = pick(even_y, ya[...], yb[...]) * has_north
    cx, cy = courant[0:1, :], courant[1:2, :]
    ax, ay = jnp.abs(cx), jnp.abs(cy)
    from_west, from_south = cx > 0.0, cy > 0.0
    keep = 1.0 - ax - ay
    sub = iota((cols, 1), 0)
    cells, parts = [], []
    for x in range(rows):
        center = spec[x].astype(F32)
        before = spec[x - 1].astype(F32) if x else west
        after = spec[x + 1].astype(F32) if x < rows - 1 else east
        below = jnp.where(sub == 0, south[x : x + 1, :], pltpu.roll(center, 1, 0))
        above = jnp.where(sub == cols - 1, north[x : x + 1, :], pltpu.roll(center, cols - 1, 0))
        advected = (
            keep * center
            + ax * jnp.where(from_west, before, after)
            + ay * jnp.where(from_south, below, above)
        )
        wind = 1.0 + 0.2 * source[:, x : x + 1]
        updated = land[:, x : x + 1] * (advected * (wind - 0.1 * advected))
        updated = updated.astype(BF)
        out[x] = updated
        cells.append(updated)
        if x == 3 * rows // 4 - 1:
            copies[0].wait()
        if x in (3 * rows // 4 - 1, rows - 1):
            part = jnp.dot(jnp.concatenate(cells, axis=0), weights[...], preferred_element_type=F32)
            parts += [part[i * cols : (i + 1) * cols] for i in range(len(cells))]
            cells = []
    for x in range(rows):
        profile[x] = parts[x].astype(BF)
    for i in range(HX):
        first, last = parts[i], parts[rows - HX + i]
        pa[i] = jnp.where(even_x, last, first).astype(BF)
        pb[i] = jnp.where(even_x, first, last).astype(BF)
    copies[1].wait()


def list_place(r, lanes):
    per = lanes // 16
    return r // (4 * per), (r % per) * 16 + RIM * ((r // per) % 4)


def y_rows(rows):
    pairs = (rows + 2 * HV + 1) // 2
    return TALL * HY, (pairs + pairs % 2) * EDGE, -(-(rows + 2) // 16) * 16


def halo_kernel(vel, oa, ob, lists, profile, pa, pb, ya, yb):
    vrow, lanes = vel.shape[0], vel.shape[2]
    rows, cols = vrow - 2 * HV, vel.shape[1] - 2 * EDGE
    even_x, even_y = is_even("gx"), is_even("gy")
    wr, wc = profile.shape[0], profile.shape[1]

    def put(at, last, first):
        n = last.shape[0]
        ya[at : at + n] = jnp.where(even_y, last, first).astype(BF)
        yb[at : at + n] = jnp.where(even_y, first, last).astype(BF)

    before, after = pick(even_x, pb[...], pa[...]), pick(even_x, pa[...], pb[...])
    joined = jnp.concatenate([before.astype(BF), profile[...], after.astype(BF)], axis=0)
    count = (wr + 2 * HX) * wc
    slots = TALL * HY
    at, cell = iota((2 * slots, count), 0), iota((2 * slots, count), 1)
    side, rest = at // slots, at % slots
    column = rest // TALL + jnp.where(side == 0, wc - HY, 0)
    row = rest % TALL
    chosen = ((row < wr + 2 * HX) & (cell == row * wc + column)).astype(F32).astype(BF)
    sides = jnp.dot(chosen, joined.reshape(count, lanes), preferred_element_type=F32)
    put(0, sides[0:slots], sides[slots:])

    sub = iota((EDGE, 1), 0)
    is_u = iota((1, lanes), 1) < lanes // 2
    end = EDGE + cols
    blocks = []
    for r in range(vrow):
        to = RIM * (r % 2)
        one, two = vel[r, end - RIM - to : end + RIM - to, :], vel[r, end - RIM - 1 - to : end + RIM - 1 - to, :]
        last = jnp.where(sub == to, jnp.where(is_u, two, pltpu.roll(one, lanes // 2, 1)), one)
        one, two = vel[r, EDGE - to : 2 * EDGE - to, :], vel[r, EDGE + 1 - to : 2 * EDGE + 1 - to, :]
        first = jnp.where(sub == to + RIM - 1, jnp.where(is_u, one, pltpu.roll(two, lanes // 2, 1)), one)
        blocks.append((last, first))
    pairs = [
        [jnp.where(sub < RIM, blocks[r][i], blocks[r + 1][i]) for i in range(2)] for r in range(0, vrow, 2)
    ]
    pairs += [[jnp.zeros((EDGE, lanes), F32)] * 2] * (len(pairs) % 2)
    for i in range(0, len(pairs), 2):
        put(slots + i * EDGE, *[jnp.concatenate([pairs[i][j], pairs[i + 1][j]], axis=0) for j in range(2)])
    start = slots + len(pairs) * EDGE
    edge = [vel[HV - 1 : HV + rows + 1, at, :] for at in (end - 1, EDGE)]
    spare = jnp.zeros((-(rows + 2) % 16, lanes), F32)
    put(start, *[jnp.concatenate([v - v.astype(BF).astype(F32), spare], axis=0) for v in edge])
    start += rows + 2 + spare.shape[0]

    group = iota((1, lanes), 1) // RIM
    x_start = oa.shape[0] - HL * 16
    tiles = list_place(rows + 2 * HL - 1, lanes)[0] + 1
    acc = [[jnp.zeros((16, lanes), F32)] * 2 for _ in range(tiles)]
    for r in range(rows + 2 * HL):
        if HL <= r < HL + rows:
            own = lists[r - HL]
        else:
            i = r if r < HL else r - HL - rows
            at = x_start + i * 16
            one, two = (ob, oa) if r < HL else (oa, ob)
            own = pick(even_x, one[at : at + 16, :], two[at : at + 16, :])
        tile, to = list_place(r, lanes)
        acc[tile] = [
            jnp.where(group == to // RIM, pltpu.roll(own, (to - where) % lanes, 1), a)
            for a, where in zip(acc[tile], (cols - RIM, 0))
        ]
    for tile in range(tiles):
        put(start + tile * 16, acc[tile][0], acc[tile][1])


def vorticity(ref, r, base, count):
    half = ref.shape[-1] // 2
    is_u = iota((1, 2 * half), 1) < half

    def at(dx, dy):
        return ref[r + dx, base + dy : base + dy + count, :]

    near = jnp.where(is_u, at(0, -1), at(1, 0)) - jnp.where(is_u, at(0, 1), at(-1, 0))
    far = jnp.where(is_u, at(0, -2), at(2, 0)) - jnp.where(is_u, at(0, 2), at(-2, 0))
    part = (8.0 / 12.0) * near - (1.0 / 12.0) * far
    return part + pltpu.roll(part, half, 1)


def averager(lanes):
    at = iota((2 * lanes, lanes), 0)
    to = iota((2 * lanes, lanes), 1)
    half = lanes // 2
    return jnp.where((at % lanes) // half == to % 2, 1.0 / half, 0.0).astype(BF)


def turned(value):
    half = value.shape[-1] // 2
    sign = jnp.where(iota((1, 2 * half), 1) < half, 1.0, -1.0)
    return pltpu.roll(value, half, 1) * sign


def prepare_kernel(own, oa, ob, lists, vel, spin, turn, table, list_rim):
    rows, cols, lanes = own.shape
    wc = cols // RY
    listed = rows + 2 * HL
    unroll = listed // 2
    even_x = is_even("gx")
    lane = iota((1, lanes), 1)

    def from_x(r, halo, start, n):
        one, two = (ob, oa) if r < halo else (oa, ob)
        return pick(even_x, one[start : start + n, :], two[start : start + n, :])

    blank = jnp.zeros((EDGE, lanes), F32)

    def fill(r, _):
        vel[r + HV, EDGE : EDGE + cols, :] = own[r]
        return 0

    lax.fori_loop(0, rows, fill, 0, unroll=8)
    for r in range(rows + 2 * HV):
        vel[r, 0:EDGE, :] = blank
        vel[r, EDGE + cols :, :] = blank
    for i in range(HV - 1):
        near, far = from_x(0, HV, i * cols, cols), from_x(HV, HV, i * cols, cols)
        if i == 0:
            vel[0, EDGE : EDGE + cols, :] = pltpu.roll(near, lanes // 2, 1)
            vel[2 * HV + rows - 1, EDGE : EDGE + cols, :] = pltpu.roll(far, lanes // 2, 1)
            vel[1, EDGE : EDGE + cols, :] = near
            vel[2 * HV + rows - 2, EDGE : EDGE + cols, :] = far
        else:
            if i == HV - 2:
                near = near + from_x(0, HV, (HV - 1) * cols, cols)
            if i == 1:
                far = far + from_x(HV, HV, (HV - 1) * cols, cols)
            vel[i + 1, EDGE : EDGE + cols, :] = near
            vel[HV + rows + i - 1, EDGE : EDGE + cols, :] = far

    sub16 = iota((16, 1), 0)
    place_of = (lane // RY).astype(F32) - 1.0
    per = lanes // 16
    rim = jnp.zeros((16, lanes), F32)
    for r in range(listed):
        if HL <= r < HL + rows:
            full = lists[r - HL]
        else:
            i = r if r < HL else r - HL - rows
            full = from_x(0 if r < HL else HL, HL, HV * cols + i * 16, 16)
        third = jnp.where(full >= 6.0, 2.0, jnp.where(full >= 3.0, 1.0, 0.0))
        table[r] = jnp.where(sub16 < K, third * (wc - 3.0) + full + place_of, full)
        to = (r % per) * 16
        rim = jnp.where(lane // RIM == to // RIM + 1, pltpu.roll(full, (to + RIM) % lanes, 1), rim)
        rim = jnp.where(lane // RIM == to // RIM + 2, pltpu.roll(full, (to + 3 * RIM - cols) % lanes, 1), rim)
        if r % per == per - 1 or r == listed - 1:
            list_rim[r // per] = rim
            rim = jnp.zeros((16, lanes), F32)

    ones = jnp.ones((8, lanes), BF)

    def absolute(m, _):
        for u in range(unroll):
            r = m * unroll + u
            wide = lax.dot_general(table[r, 2 * K :, :].astype(BF), ones, ROWS_DOT, preferred_element_type=F32)
            spin[r] = wide[0:cols]
            turn[r] = wide[0:cols] + vorticity(vel, r + HV - HL, EDGE, cols)
        return 0

    lax.fori_loop(0, listed // unroll, absolute, 0)


def inner_kernel(
    vel, spin, turn, table, profile, pa, pb, codes_far, weights_far, cells,
    out_far, cells_far, mid_rim, drift_rim, spin_rim, total, prof_rim, wave_shares, chosen, spread,
    mid, names, prof, drift, out, codes, weights, sems,
):
    rows, cols, lanes = out.shape
    copies = [
        pltpu.make_async_copy(codes_far, codes, sems.at[0]),
        pltpu.make_async_copy(weights_far, weights, sems.at[1]),
        pltpu.make_async_copy(cells, cells_far, sems.at[2]),
    ]
    for copy in copies:
        copy.start()
    wr, wc = profile.shape[0], profile.shape[1]
    listed = rows + 2 * HL
    prow = wr + 2 * HX
    unroll = listed // 2
    even_x = is_even("gx")
    lane = iota((1, lanes), 1)
    blank = jnp.zeros((EDGE, lanes), F32)
    for x in range(prow):
        if HX <= x < HX + wr:
            part = profile[x - HX].astype(F32)
        elif x < HX:
            part = pick(even_x, pb[x], pa[x])
        else:
            part = pick(even_x, pa[x - HX - wr], pb[x - HX - wr])
        part = turned(part)
        prof[x * wc : (x + 1) * wc, :] = part
        names[x * wc : (x + 1) * wc, :] = part.astype(BF)
    prof_rim[...] = jnp.zeros(prof_rim.shape, F32)
    for c in range(HY):
        prof_rim[0, pl.ds(HY + c, prow, stride=2 * HY), :] = prof[pl.ds(c, prow, stride=wc), :]
        prof_rim[1, pl.ds(c, prow, stride=2 * HY), :] = prof[pl.ds(wc - HY + c, prow, stride=wc), :]

    block = 3 * wc
    place = iota((block, lanes), 0).astype(F32)
    lift = HV - HL

    def first_step(m, _):
        for u in range(unroll):
            r = m * unroll + u
            hot = jnp.where(place == table[r, 0:1, :], table[r, K : K + 1, :], 0.0)
            for k in range(1, K):
                hot = hot + jnp.where(place == table[r, k : k + 1, :], table[r, K + k : K + k + 1, :], 0.0)
            named = names[pl.ds(pl.multiple_of((r + 1) // 2 * wc, wc), block), :]
            stokes = lax.dot_general(hot.astype(BF), named, ROWS_DOT, preferred_element_type=F32)[0:cols]
            drift[r] = stokes
            new = vel[r + lift, EDGE : EDGE + cols, :] + STEP * (turn[r] * stokes)
            mid[r, 0:EDGE, :] = blank
            mid[r, EDGE + cols :, :] = blank
            mid[r, EDGE : EDGE + cols, :] = new
            mid_rim[r, 0] = new[0 : 2 * EDGE]
            mid_rim[r, 1] = new[cols - 2 * EDGE :]
            for where in range(2):
                begin = RIM if where == 0 else cols - RIM - EDGE
                drift_rim[r, where] = drift[r, begin : begin + EDGE, :]
                spin_rim[r, where] = spin[r, begin : begin + EDGE, :]
        return 0

    lax.fori_loop(0, listed // unroll, first_step, 0)

    average = averager(lanes)
    means = jnp.zeros((cols, lanes), F32)
    for n in range(rows + 2):
        r = n + HL - 1
        absolute = spin[r] + vorticity(mid, r, EDGE, cols)
        old = vel[r + lift, EDGE : EDGE + cols, :] + mid[r, EDGE : EDGE + cols, :]
        new = 0.5 * old + (0.5 * STEP) * (absolute * drift[r])
        sums = jnp.dot(jnp.concatenate(split(new), axis=1), average, preferred_element_type=F32)
        means = jnp.where(lane // 2 == n, sums, means)
        if 1 <= n <= rows:
            out[n - 1] = new
            if n % (rows // 4) == 0:
                part = pl.ds(n - rows // 4, rows // 4)
                copies.append(pltpu.make_async_copy(out.at[part], out_far.at[part], sems.at[len(copies)]))
                copies[-1].start()
    total[...] = means

    at, to = iota(chosen.shape, 0), iota(chosen.shape, 1)
    reach = (RY + 2) * wc
    chosen[...] = ((to < reach) & (at == RY * (to % wc) + to // wc + RIM - 1)).astype(F32)
    at, to = iota((lanes, lanes), 0), iota((lanes, lanes), 1)
    spread[...] = ((at < reach) & (at % wc == to)).astype(F32).astype(BF)

    copies[0].wait()
    copies[1].wait()
    at, to = iota((wc, lanes), 0), iota((wc, lanes), 1)
    repeat = ((to < reach) & (to % wc == at)).astype(F32).astype(BF)
    shift = (lane // wc).astype(F32)
    weight = [weights[:, k, :] for k in range(K)]
    whole = sum(weight[1:], weight[0])
    code = [jnp.dot(codes[:, k, :].astype(F32).astype(BF), repeat, preferred_element_type=F32) for k in range(K)]
    share = [
        sum(jnp.dot(p, repeat, preferred_element_type=F32) for p in split3(weight[k] / whole)) for k in range(K)
    ]
    for near in range(RX + 2):
        wave_shares[near] = sum(
            jnp.where(code[k] == near * (RY + 2.0) + shift, share[k], 0.0) for k in range(K)
        )
    for copy in copies[2:]:
        copy.wait()


def rim_kernel(
    wide, ya, yb, mid_rim, drift_rim, spin_rim, total, list_rim, prof_rim, wave_shares, chosen, spread, velocity_in,
    velocity_out, current,
    vel, mid, prof, drift, spin, picked, means, strips, sems,
):
    vrow, lanes = wide.shape[0], wide.shape[2]
    rows, cols = vrow - 2 * HV, wide.shape[1] - 2 * EDGE
    wr, wc = current.shape[1], current.shape[2]
    listed = rows + 2 * HL
    prow = wr + 2 * HX
    even_y = is_even("gy")
    has_south, has_north = inside("gy")
    lane = iota((1, lanes), 1)
    sub = iota((EDGE, 1), 0)
    slots, vel_rows, low_rows = y_rows(rows)

    def from_y(start, n):
        a, b = ya[start : start + n, :], yb[start : start + n, :]
        return pick(even_y, b, a) * has_south, pick(even_y, a, b) * has_north

    blank = jnp.zeros((EDGE, lanes), F32)
    for r in range(vrow):
        vel[0, r, 0:EDGE, :] = blank
        vel[1, r, 2 * EDGE :, :] = blank
        vel[0, r, EDGE:, :] = wide[r, EDGE : 3 * EDGE, :]
        vel[1, r, 0 : 2 * EDGE, :] = wide[r, cols - EDGE : cols + EDGE, :]
    for start in range(0, vel_rows, 2 * EDGE):
        pieces = from_y(slots + start, 2 * EDGE)
        for i in range(2):
            low, high = (p[i * EDGE : i * EDGE + EDGE] for p in pieces)
            low_moved, high_moved = pltpu.roll(low, lanes // 2, 1), pltpu.roll(high, lanes // 2, 1)
            low_in = jnp.where(sub % RIM == 0, low_moved, low)
            for j in range(2):
                r = (start + i * EDGE) // RIM + j
                if r < vrow:
                    at = j * RIM
                    vel[0, r, EDGE - RIM : EDGE, :] = low_in[at : at + RIM]
                    vel[0, r, EDGE - RIM - 1 : EDGE - RIM, :] = low[at : at + 1]
                    vel[1, r, 2 * EDGE : 2 * EDGE + RIM, :] = high[at : at + RIM]
                    vel[1, r, 2 * EDGE + RIM : 2 * EDGE + RIM + 1, :] = high_moved[at + RIM - 1 : at + RIM]

    prof[...] = prof_rim[...]
    south, north = from_y(0, slots)
    south, north = turned(south), turned(north)
    for c in range(HY):
        prof[0, pl.ds(c, TALL, stride=2 * HY), :] = south[TALL * c : TALL * (c + 1)]
        prof[1, pl.ds(HY + c, TALL, stride=2 * HY), :] = north[TALL * c : TALL * (c + 1)]

    per = lanes // 16
    start = slots + vel_rows + low_rows
    span = 2 * per * HY
    place = iota((2 * span, lanes), 0).astype(F32)
    part = lane % 16
    offset = (part // EDGE) * span + ((lane // 16 + 1) // 2) * (2 * HY) + (part % EDGE) // RIM
    sub16 = iota((16, 1), 0)
    ones = jnp.ones((8, lanes), F32)
    none = jnp.zeros((2 * span, lanes), F32)
    for g in range(-(-listed // per)):
        tile, to = list_place(g * per, lanes)
        south, north = from_y(start + tile * 16, 16)
        full = list_rim[g]
        full = jnp.where(part // RIM == 0, pltpu.roll(south, (-to) % lanes, 1), full)
        full = jnp.where(part // RIM == 3, pltpu.roll(north, (3 * RIM - to) % lanes, 1), full)
        third = jnp.where(full >= 6.0, 2.0, jnp.where(full >= 3.0, 1.0, 0.0))
        full = jnp.where(sub16 < K, third + full + offset.astype(F32), full)
        hot = jnp.zeros((2 * span, lanes), F32)
        for k in range(K):
            hot = hot + jnp.where(place == full[k : k + 1], full[K + k : K + k + 1], 0.0)
        left = jnp.concatenate([hot, full[2 * K :], blank], axis=0).astype(BF)
        begin = g * (per // 2) * 2 * HY
        named = jnp.concatenate([prof[0, begin : begin + span, :], prof[1, begin : begin + span, :]], axis=0)
        right = jnp.concatenate([
            jnp.concatenate([named, blank, blank], axis=0),
            jnp.concatenate([none, ones, blank], axis=0),
        ], axis=1).astype(BF)
        both = lax.dot_general(left, right, ROWS_DOT, preferred_element_type=F32)
        for i in range(min(per, listed - g * per)):
            for side in range(2):
                at = i * 16 + side * EDGE
                drift[side, g * per + i] = both[at : at + EDGE, 0:lanes]
                spin[side, g * per + i] = both[at : at + EDGE, lanes:]

    lift = HV - HL
    for r in range(listed):
        for side in range(2):
            base = RIM + side * EDGE
            mid[side, r, 2 * EDGE * side : 2 * EDGE * side + EDGE, :] = blank
            mid[side, r, EDGE - side * EDGE : 3 * EDGE - side * EDGE, :] = mid_rim[r, side]
            absolute = spin[side, r] + vorticity(vel.at[side], r + lift, base, EDGE)
            new = vel[side, r + lift, base : base + EDGE, :] + STEP * (absolute * drift[side, r])
            mid[side, r, base : base + EDGE, :] = new

    average = averager(lanes)
    acc = jnp.zeros((4 * EDGE, lanes), F32)
    for n in range(rows + 2):
        r = n + HL - 1
        both = []
        for side in range(2):
            turns, drifts = (spin[side, r], spin_rim[r, side]), (drift[side, r], drift_rim[r, side])
            order = 1 - 2 * side
            absolute = jnp.concatenate(turns[::order], axis=0) + vorticity(mid.at[side], r, RIM, 2 * EDGE)
            tile = slice(RIM, RIM + 2 * EDGE)
            old = vel[side, r + lift, tile, :] + mid[side, r, tile, :]
            new = 0.5 * old + (0.5 * STEP) * (absolute * jnp.concatenate(drifts[::order], axis=0))
            both.append(new)
            if 1 <= n <= rows:
                strips[side, n - 1] = new[RIM : RIM + EDGE]
        sums = jnp.dot(
            jnp.concatenate(split(jnp.concatenate(both, axis=0)), axis=1), average, preferred_element_type=F32
        )
        acc = jnp.where(lane // 2 == n, sums, acc)
    where = iota((4 * EDGE, 1), 0)
    own_lane = lane // 2 == iota((low_rows, 1), 0)
    for low, at in zip(from_y(slots + vel_rows, low_rows), (RIM - 1, 4 * EDGE - RIM)):
        sums = jnp.dot(low.astype(BF), average[0:lanes], preferred_element_type=F32)
        acc = acc + jnp.where(where == at, jnp.sum(jnp.where(own_lane, sums, 0.0), axis=0, keepdims=True), 0.0)
    copies = [
        pltpu.make_async_copy(strips.at[side], velocity_out.at[:, pl.ds(at, EDGE), :], sems.at[side])
        for side, at in ((0, 0), (1, cols - EDGE))
    ]
    for copy in copies:
        copy.start()
    means[0 : 2 * EDGE] = acc[0 : 2 * EDGE]
    means[2 * EDGE : 2 * RIM + cols - 2 * EDGE] = total[2 * EDGE - RIM : cols - 2 * EDGE + RIM, :]
    means[2 * RIM + cols - 2 * EDGE :] = acc[2 * EDGE :]

    named = chosen[...].astype(BF)
    picked[...] = sum(
        lax.dot_general(p, named, ROWS_DOT, preferred_element_type=F32) for p in split3(means[...])
    )
    summed = [
        sum(wave_shares[near] * picked[pl.ds(2 * near + c, wr, stride=2 * RX), :] for near in range(RX + 2))
        for c in range(2)
    ]
    sums = sum(
        jnp.dot(p, spread[...], preferred_element_type=F32) for p in split3(jnp.concatenate(summed, axis=0))
    )
    current[0] = sums[0:wr, 0:wc]
    current[1] = sums[wr:, 0:wc]
    for copy in copies:
        copy.wait()


VMEM = pl.BlockSpec(memory_space=pltpu.VMEM)
ANY = pl.BlockSpec(memory_space=pltpu.HBM)


def call(kernel, name, outs, *args, scratch=(), any_in=(), any_out=(), aliases=None):
    args = [pltpu.with_memory_space_constraint(v, pltpu.HBM) if i in any_in else v for i, v in enumerate(args)]
    return pl.pallas_call(
        kernel,
        out_shape=tuple(jax.ShapeDtypeStruct(shape, dtype) for shape, dtype in outs),
        in_specs=[ANY if i in any_in else VMEM for i in range(len(args))],
        out_specs=tuple(ANY if i in any_out else VMEM for i in range(len(outs))),
        scratch_shapes=list(scratch),
        input_output_aliases=aliases or {},
        compiler_params=pltpu.CompilerParams(vmem_limit_bytes=14 << 20),
        name=name,
    )(*args)


def shards(
    spectrum, courant, source, wave_land, stokes_kernel, velocity, coriolis,
    ocean_codes, ocean_weights, wave_codes, wave_weights,
):
    wr, wc, bins = spectrum.shape
    rows, cols, lanes = velocity.shape
    listed = rows + 2 * HL
    prow = wr + 2 * HX

    with jax.named_scope("spectrum_edges"):
        codes, weights = jnp.transpose(ocean_codes, (0, 2, 1)), jnp.transpose(ocean_weights, (0, 2, 1))
        size = sum(x_rows(cols))
        outs = [((wc, bins), BF)] * 2 + [((wr, bins), BF)] * 2 + [((size, lanes), BF)] * 2 + [((rows, 16, lanes), F32)]
        kept = [spectrum, courant, source, wave_land]
        xa, xb, ya, yb, oa, ob, lists, spectrum, courant, source, wave_land = call(
            edges_kernel, "edges", outs + [(v.shape, v.dtype) for v in kept],
            *kept, codes, weights, coriolis, velocity, any_in=range(8),
            scratch=[
                pltpu.VMEM(codes.shape, codes.dtype),
                pltpu.VMEM(weights.shape, F32),
                pltpu.VMEM(coriolis.shape, F32),
                pltpu.VMEM((2, HV, cols, lanes), F32),
                pltpu.SemaphoreType.DMA((9,)),
            ],
        )
        xa, xb = exchange("gx", xa, xb)
        ya, yb = exchange("gy", ya, yb)
        oa, ob = exchange("gx", oa, ob)

    with jax.named_scope("wave"):
        new_spectrum, profiles, pa, pb, velocity = call(
            wave_kernel, "wave",
            [(spectrum.shape, BF), ((wr, wc, lanes), BF), ((HX, wc, lanes), BF), ((HX, wc, lanes), BF), (velocity.shape, F32)],
            spectrum, xa, xb, ya, yb, courant, source.T, wave_land.T.astype(F32),
            stokes_kernel, velocity,
            any_in=(8, 9), scratch=[pltpu.VMEM(stokes_kernel.shape, BF), pltpu.SemaphoreType.DMA((2,))],
        )
        pa, pb = exchange("gx", pa, pb)

    with jax.named_scope("prepare"):
        wide = cols + 2 * EDGE
        groups = -(-listed // (lanes // 16))
        vel, spin, turn, table, list_rim = call(
            prepare_kernel, "prepare",
            [
                ((rows + 2 * HV, wide, lanes), F32),
                ((listed, cols, lanes), F32),
                ((listed, cols, lanes), F32),
                ((listed, 16, lanes), F32),
                ((groups, 16, lanes), F32),
            ],
            velocity, oa, ob, lists,
        )

    with jax.named_scope("halo"):
        size = sum(y_rows(rows)) + (list_place(listed - 1, lanes)[0] + 1) * 16
        ya, yb = call(
            halo_kernel, "halo", [((size, lanes), BF)] * 2, vel, oa, ob, lists, profiles, pa, pb
        )
        ya, yb = exchange("gy", ya, yb)

    with jax.named_scope("inner"):
        scratch = [
            pltpu.VMEM((listed, wide, lanes), F32),
            pltpu.VMEM((prow * wc, lanes), BF),
            pltpu.VMEM((prow * wc, lanes), F32),
            pltpu.VMEM((listed, cols, lanes), F32),
            pltpu.VMEM(velocity.shape, F32),
            pltpu.VMEM((wr, K, wc), jnp.int32),
            pltpu.VMEM((wr, K, wc), F32),
            pltpu.SemaphoreType.DMA((7,)),
        ]
        new_velocity, new_spectrum, mid_rim, drift_rim, spin_rim, total, prof_rim, wave_shares, chosen, spread = call(
            inner_kernel, "inner",
            [
                (velocity.shape, F32),
                (spectrum.shape, BF),
                ((listed, 2, 2 * EDGE, lanes), F32),
                ((listed, 2, EDGE, lanes), F32),
                ((listed, 2, EDGE, lanes), F32),
                ((cols, lanes), F32),
                ((2, 2 * HY * (TALL + 4), lanes), F32),
                ((RX + 2, wr, lanes), F32),
                ((cols + 2 * RIM, lanes), F32),
                ((lanes, lanes), BF),
            ],
            vel, spin, turn, table, profiles, pa, pb,
            jnp.transpose(wave_codes, (0, 2, 1)), jnp.transpose(wave_weights, (0, 2, 1)),
            new_spectrum, scratch=scratch, any_in=(7, 8), any_out=(0, 1),
        )

    with jax.named_scope("rim"):
        scratch = [
            pltpu.VMEM((2, rows + 2 * HV, 3 * EDGE, lanes), F32),
            pltpu.VMEM((2, listed, 3 * EDGE, lanes), F32),
            pltpu.VMEM((2, 2 * HY * (TALL + 4), lanes), F32),
            pltpu.VMEM((2, listed, EDGE, lanes), F32),
            pltpu.VMEM((2, listed, EDGE, lanes), F32),
            pltpu.VMEM((lanes, lanes), F32),
            pltpu.VMEM((cols + 2 * RIM, lanes), F32),
            pltpu.VMEM((2, rows, EDGE, lanes), F32),
            pltpu.SemaphoreType.DMA((2,)),
        ]
        new_velocity, current = call(
            rim_kernel, "rim", [(velocity.shape, F32), ((2, wr, wc), F32)],
            vel, ya, yb, mid_rim, drift_rim, spin_rim, total, list_rim, prof_rim, wave_shares, chosen, spread,
            new_velocity, scratch=scratch, any_in=(12,), any_out=(0,), aliases={12: 0},
        )
    return new_spectrum, new_velocity, current


def solution(mesh):
    return jax.shard_map(
        shards,
        mesh=mesh,
        in_specs=(
            P("gx", "gy", None), P(), P("gx", "gy"), P("gx", "gy"), P(), P("gx", "gy", None),
            P("gx", "gy"), P("gx", "gy", None), P("gx", "gy", None), P("gx", "gy", None), P("gx", "gy", None),
        ),
        out_specs=(P("gx", "gy", None), P("gx", "gy", None), P(None, "gx", "gy")),
        check_vma=False,
    )
```

```python
import jax
import jax.numpy as jnp
from jax import lax
from jax.experimental import pallas as pl
from jax.experimental.pallas import tpu as pltpu
from jax.sharding import PartitionSpec as P

K = 4
RX = 2
RY = 4
STEP = 0.5
PARTS = 1
TALL = 24
RIM = 4
HV, HL = 5, 3
HX, HY = 3, 2
EDGE = 8
BF = jnp.bfloat16
F32 = jnp.float32
ROWS_DOT = (((0,), (0,)), ((), ()))


def partner(i, count, parity):
    return (i ^ 1) if parity == 0 else ((i + 1) ^ 1) - 1


def swap(value, axis, parity):
    nx, ny = lax.axis_size("gx"), lax.axis_size("gy")
    pairs = []
    for x in range(nx):
        for y in range(ny):
            tx, ty = x, y
            if axis == "gx":
                tx = partner(x, nx, parity) % nx
            else:
                ty = partner(y, ny, parity)
                if not 0 <= ty < ny:
                    tx, ty = x ^ 1, y
            pairs.append((x * ny + y, tx * ny + ty))
    return lax.ppermute(value, ("gx", "gy"), pairs)


def exchange(axis, to_a, to_b):
    from_b = swap(to_b, axis, 1)
    from_a = swap(to_a, axis, 0)
    return from_a, from_b


def is_even(axis):
    return lax.axis_index(axis) % 2 == 0


def inside(axis):
    index = lax.axis_index(axis)
    before = jnp.where(index == 0, 0.0, 1.0).astype(F32)
    after = jnp.where(index == lax.axis_size(axis) - 1, 0.0, 1.0).astype(F32)
    return before, after


def pick(cond, one, other):
    return jnp.where(cond, one.astype(F32), other.astype(F32))


def split(value):
    high = value.astype(BF)
    return high, (value - high.astype(F32)).astype(BF)


def split3(value):
    high = value.astype(BF)
    rest = value - high.astype(F32)
    middle = rest.astype(BF)
    return high, middle, (rest - middle.astype(F32)).astype(BF)


def iota(shape, dim):
    return lax.broadcasted_iota(jnp.int32, shape, dim)


def x_rows(cols):
    return (HV - 1) * cols, HL * 16


def cut_rows(one, two):
    step = one.shape[0] // PARTS
    return [(one.at[pl.ds(i * step, step)], two.at[pl.ds(i * step, step)]) for i in range(PARTS)]


def edges_kernel(*refs):
    (spec_far, courant_far, source_far, land_far, basis_far, codes_far, weights_far, coriolis_far, vel_far) = refs[:9]
    (xa, xb, ya, yb, oa, ob, lists, spec, courant, source, land, basis) = refs[9:21]
    (codes, weights, coriolis, vel, sems) = refs[21:]
    rows, cols, bins = spec.shape
    lanes = vel.shape[-1]
    pairs = cut_rows(spec_far, spec)
    pairs += [(vel_far.at[pl.ds(at, HV)], vel.at[i]) for i, at in ((0, 0), (1, vel_far.shape[0] - HV))]
    pairs += [(codes_far, codes), (weights_far, weights), (coriolis_far, coriolis)]
    pairs += [(courant_far, courant), (source_far, source), (land_far, land), (basis_far, basis)]
    copies = [pltpu.make_async_copy(one, two, sems.at[i]) for i, (one, two) in enumerate(pairs)]
    for copy in copies:
        copy.start()
    even_x, even_y = is_even("gx"), is_even("gy")

    def put(at, last, first):
        n = last.shape[0]
        oa[at : at + n] = jnp.where(even_x, last, first).astype(BF)
        ob[at : at + n] = jnp.where(even_x, first, last).astype(BF)

    at, cell = iota((2 * rows, rows * cols), 0), iota((2 * rows, rows * cols), 1)
    wanted = jnp.where(at < rows, at * cols, (at - rows) * cols + cols - 1)
    chosen = (cell == wanted).astype(F32).astype(BF)
    for copy in copies[:PARTS]:
        copy.wait()
    sides = jnp.dot(chosen, spec[...].reshape(rows * cols, bins), preferred_element_type=F32)
    first, last = spec[0].astype(F32), spec[rows - 1].astype(F32)
    xa[...] = jnp.where(even_x, last, first).astype(BF)
    xb[...] = jnp.where(even_x, first, last).astype(BF)
    first, last = sides[0:rows], sides[rows:]
    ya[...] = jnp.where(even_y, last, first).astype(BF)
    yb[...] = jnp.where(even_y, first, last).astype(BF)

    for copy in copies[PARTS:]:
        copy.wait()
    listed, wide = codes.shape[0], codes.shape[2]
    is_u = iota((1, lanes), 1) < lanes // 2
    outer = [
        jnp.where(is_u, pltpu.roll(vel[side, one], lanes // 2, 1), vel[side, two])
        for side, one, two in ((1, 0, 1), (0, HV - 1, HV - 2))
    ]
    put(0, *outer)
    for i in range(1, HV - 1):
        put(i * wide, vel[1, i + 1], vel[0, i - 1])
    for r in range(listed):
        lists[r] = jnp.zeros((16, lanes), F32)
        weight = weights[r]
        turn = coriolis[r : r + 1, :]
        high = turn.astype(BF).astype(F32)
        lists[r, 0:K, 0:wide] = codes[r].astype(F32)
        lists[r, K : 2 * K, 0:wide] = weight / jnp.sum(weight, axis=0, keepdims=True)
        lists[r, 2 * K : 2 * K + 1, 0:wide] = high
        lists[r, 2 * K + 1 : 2 * K + 2, 0:wide] = turn - high
    for i in range(HL):
        put((HV - 1) * wide + i * 16, lists[listed - HL + i], lists[i])


def advance(chosen, spec, sides, ya, yb, courant, source, land, weights, at_once, put):
    rows, cols, _ = spec.shape
    even_y = is_even("gy")
    has_south, has_north = inside("gy")
    south = pick(even_y, yb[...], ya[...]) * has_south
    north = pick(even_y, ya[...], yb[...]) * has_north
    cx, cy = courant[0:1, :], courant[1:2, :]
    ax, ay = jnp.abs(cx), jnp.abs(cy)
    from_west, from_south = cx > 0.0, cy > 0.0
    keep = 1.0 - ax - ay
    sub = iota((cols, 1), 0)
    cells = []
    for x in chosen:
        center = spec[x].astype(F32)
        before = spec[x - 1].astype(F32) if x else sides[0]
        after = spec[x + 1].astype(F32) if x < rows - 1 else sides[1]
        below = jnp.where(sub == 0, south[x : x + 1, :], pltpu.roll(center, 1, 0))
        above = jnp.where(sub == cols - 1, north[x : x + 1, :], pltpu.roll(center, cols - 1, 0))
        advected = (
            keep * center
            + ax * jnp.where(from_west, before, after)
            + ay * jnp.where(from_south, below, above)
        )
        wind = 1.0 + 0.2 * source[:, x : x + 1]
        updated = land[:, x : x + 1] * (advected * (wind - 0.1 * advected))
        cells.append(updated.astype(BF))
        if len(cells) == at_once:
            parts = jnp.dot(jnp.concatenate(cells, axis=0), weights[...], preferred_element_type=F32)
            for i, value in enumerate(cells):
                put(x - at_once + 1 + i, value, parts[i * cols : (i + 1) * cols])
            cells = []


def wave_ends_kernel(spec, xa, xb, ya, yb, courant, source, land, weights, out, profile, pa, pb):
    rows, cols, bins = spec.shape
    even_x = is_even("gx")
    west, east = pick(even_x, xb[...], xa[...]), pick(even_x, xa[...], xb[...])

    parts = []

    def put(x, value, part):
        i = len(parts)
        out[i], profile[i] = value, part.astype(BF)
        parts.append(part)

    ends = list(range(HX)) + list(range(rows - HX, rows))
    advance(ends, spec, (west, east), ya, yb, courant, source, land, weights, HX, put)
    for i in range(HX):
        first, last = parts[i], parts[HX + i]
        pa[i] = jnp.where(even_x, last, first).astype(BF)
        pb[i] = jnp.where(even_x, first, last).astype(BF)


def wave_rest_kernel(spec, ya, yb, courant, source, land, weights, ends, out, profile):
    rows = spec.shape[0]

    def put(x, value, part):
        out[x - HX], profile[x - HX] = value, part.astype(BF)

    advance(range(HX, rows - HX), spec, None, ya, yb, courant, source, land, weights, (rows - 2 * HX) // 2, put)


def list_place(r, lanes):
    per = lanes // 16
    return r // (4 * per), (r % per) * 16 + RIM * ((r // per) % 4)


def y_rows(rows):
    pairs = (rows + 2 * HV + 1) // 2
    return TALL * HY, (pairs + pairs % 2) * EDGE


def halo_kernel(vel, oa, ob, lists, ends, rest, pa, pb, ya, yb):
    vrow, lanes = vel.shape[0], vel.shape[2]
    rows, cols = vrow - 2 * HV, vel.shape[1] - 2 * EDGE
    even_x, even_y = is_even("gx"), is_even("gy")
    wr, wc = rest.shape[0] + 2 * HX, rest.shape[1]

    def put(at, last, first):
        n = last.shape[0]
        ya[at : at + n] = jnp.where(even_y, last, first).astype(BF)
        yb[at : at + n] = jnp.where(even_y, first, last).astype(BF)

    before, after = pick(even_x, pb[...], pa[...]), pick(even_x, pa[...], pb[...])
    joined = jnp.concatenate([before.astype(BF), ends[0:HX], rest[...], ends[HX:], after.astype(BF)], axis=0)
    count = (wr + 2 * HX) * wc
    slots = TALL * HY
    at, cell = iota((2 * slots, count), 0), iota((2 * slots, count), 1)
    side, rest = at // slots, at % slots
    column = rest // TALL + jnp.where(side == 0, wc - HY, 0)
    row = rest % TALL
    chosen = ((row < wr + 2 * HX) & (cell == row * wc + column)).astype(F32).astype(BF)
    sides = jnp.dot(chosen, joined.reshape(count, lanes), preferred_element_type=F32)
    put(0, sides[0:slots], sides[slots:])

    sub = iota((EDGE, 1), 0)
    is_u = iota((1, lanes), 1) < lanes // 2
    end = EDGE + cols
    blocks = []
    for r in range(vrow):
        to = RIM * (r % 2)
        one, two = vel[r, end - RIM - to : end + RIM - to, :], vel[r, end - RIM - 1 - to : end + RIM - 1 - to, :]
        last = jnp.where(sub == to, jnp.where(is_u, two, pltpu.roll(one, lanes // 2, 1)), one)
        one, two = vel[r, EDGE - to : 2 * EDGE - to, :], vel[r, EDGE + 1 - to : 2 * EDGE + 1 - to, :]
        first = jnp.where(sub == to + RIM - 1, jnp.where(is_u, one, pltpu.roll(two, lanes // 2, 1)), one)
        blocks.append((last, first))
    pairs = [
        [jnp.where(sub < RIM, blocks[r][i], blocks[r + 1][i]) for i in range(2)] for r in range(0, vrow, 2)
    ]
    pairs += [[jnp.zeros((EDGE, lanes), F32)] * 2] * (len(pairs) % 2)
    for i in range(0, len(pairs), 2):
        put(slots + i * EDGE, *[jnp.concatenate([pairs[i][j], pairs[i + 1][j]], axis=0) for j in range(2)])
    start = slots + len(pairs) * EDGE

    group = iota((1, lanes), 1) // RIM
    x_start = oa.shape[0] - HL * 16
    tiles = list_place(rows + 2 * HL - 1, lanes)[0] + 1
    acc = [[jnp.zeros((16, lanes), F32)] * 2 for _ in range(tiles)]
    for r in range(rows + 2 * HL):
        if HL <= r < HL + rows:
            own = lists[r - HL]
        else:
            i = r if r < HL else r - HL - rows
            at = x_start + i * 16
            one, two = (ob, oa) if r < HL else (oa, ob)
            own = pick(even_x, one[at : at + 16, :], two[at : at + 16, :])
        tile, to = list_place(r, lanes)
        acc[tile] = [
            jnp.where(group == to // RIM, pltpu.roll(own, (to - where) % lanes, 1), a)
            for a, where in zip(acc[tile], (cols - RIM, 0))
        ]
    for tile in range(tiles):
        put(start + tile * 16, acc[tile][0], acc[tile][1])


def vorticity(ref, r, base, count):
    half = ref.shape[-1] // 2
    is_u = iota((1, 2 * half), 1) < half

    def at(dx, dy):
        return ref[r + dx, base + dy : base + dy + count, :]

    near = jnp.where(is_u, at(0, -1), at(1, 0)) - jnp.where(is_u, at(0, 1), at(-1, 0))
    far = jnp.where(is_u, at(0, -2), at(2, 0)) - jnp.where(is_u, at(0, 2), at(-2, 0))
    part = (8.0 / 12.0) * near - (1.0 / 12.0) * far
    return part + pltpu.roll(part, half, 1)


def averager(lanes):
    at = iota((2 * lanes, lanes), 0)
    to = iota((2 * lanes, lanes), 1)
    half = lanes // 2
    return jnp.where((at % lanes) // half == to % 2, 1.0 / half, 0.0).astype(BF)


def turned(value):
    half = value.shape[-1] // 2
    sign = jnp.where(iota((1, 2 * half), 1) < half, 1.0, -1.0)
    return pltpu.roll(value, half, 1) * sign


def prepare_kernel(own, oa, ob, lists, vel, spin, turn, table, list_rim):
    rows, cols, lanes = own.shape
    wc = cols // RY
    listed = rows + 2 * HL
    unroll = listed // 2
    even_x = is_even("gx")
    lane = iota((1, lanes), 1)

    def from_x(r, halo, start, n):
        one, two = (ob, oa) if r < halo else (oa, ob)
        return pick(even_x, one[start : start + n, :], two[start : start + n, :])

    blank = jnp.zeros((EDGE, lanes), F32)

    def fill(r, _):
        vel[r + HV, EDGE : EDGE + cols, :] = own[r]
        return 0

    lax.fori_loop(0, rows, fill, 0, unroll=8)
    for r in range(rows + 2 * HV):
        vel[r, 0:EDGE, :] = blank
        vel[r, EDGE + cols :, :] = blank
    for i in range(HV - 1):
        near, far = from_x(0, HV, i * cols, cols), from_x(HV, HV, i * cols, cols)
        if i == 0:
            vel[0, EDGE : EDGE + cols, :] = pltpu.roll(near, lanes // 2, 1)
            vel[2 * HV + rows - 1, EDGE : EDGE + cols, :] = pltpu.roll(far, lanes // 2, 1)
            vel[1, EDGE : EDGE + cols, :] = near
            vel[2 * HV + rows - 2, EDGE : EDGE + cols, :] = far
        else:
            vel[i + 1, EDGE : EDGE + cols, :] = near
            vel[HV + rows + i - 1, EDGE : EDGE + cols, :] = far

    sub16 = iota((16, 1), 0)
    place_of = (lane // RY).astype(F32) - 1.0
    per = lanes // 16
    rim = jnp.zeros((16, lanes), F32)
    for r in range(listed):
        if HL <= r < HL + rows:
            full = lists[r - HL]
        else:
            i = r if r < HL else r - HL - rows
            full = from_x(0 if r < HL else HL, HL, (HV - 1) * cols + i * 16, 16)
        third = jnp.where(full >= 6.0, 2.0, jnp.where(full >= 3.0, 1.0, 0.0))
        table[r] = jnp.where(sub16 < K, third * (wc - 3.0) + full + place_of, full)
        to = (r % per) * 16
        rim = jnp.where(lane // RIM == to // RIM + 1, pltpu.roll(full, (to + RIM) % lanes, 1), rim)
        rim = jnp.where(lane // RIM == to // RIM + 2, pltpu.roll(full, (to + 3 * RIM - cols) % lanes, 1), rim)
        if r % per == per - 1 or r == listed - 1:
            list_rim[r // per] = rim
            rim = jnp.zeros((16, lanes), F32)

    ones = jnp.ones((8, lanes), BF)

    def absolute(m, _):
        for u in range(unroll):
            r = m * unroll + u
            wide = lax.dot_general(table[r, 2 * K :, :].astype(BF), ones, ROWS_DOT, preferred_element_type=F32)
            spin[r] = wide[0:cols]
            turn[r] = wide[0:cols] + vorticity(vel, r + HV - HL, EDGE, cols)
        return 0

    lax.fori_loop(0, listed // unroll, absolute, 0)


def inner_kernel(
    vel, spin, turn, table, ends, rest, pa, pb, codes_far, weights_far, cells_ends, cells_rest,
    out_far, cells_far, mid_rim, drift_rim, spin_rim, total, prof_rim, wave_shares, chosen, spread,
    mid, names, prof, drift, out, codes, weights, sems,
):
    rows, cols, lanes = out.shape
    copies = [
        pltpu.make_async_copy(codes_far, codes, sems.at[0]),
        pltpu.make_async_copy(weights_far, weights, sems.at[1]),
    ]
    wr, wc = rest.shape[0] + 2 * HX, rest.shape[1]
    for part, to in (
        (cells_ends.at[pl.ds(0, HX)], cells_far.at[pl.ds(0, HX)]),
        (cells_rest, cells_far.at[pl.ds(HX, wr - 2 * HX)]),
        (cells_ends.at[pl.ds(HX, HX)], cells_far.at[pl.ds(wr - HX, HX)]),
    ):
        copies.append(pltpu.make_async_copy(part, to, sems.at[len(copies)]))
    for copy in copies:
        copy.start()
    listed = rows + 2 * HL
    prow = wr + 2 * HX
    unroll = listed // 2
    even_x = is_even("gx")
    lane = iota((1, lanes), 1)
    blank = jnp.zeros((EDGE, lanes), F32)
    for x in range(prow):
        if HX <= x < HX + wr:
            i = x - HX
            own = ends[i] if i < HX else rest[i - HX] if i < wr - HX else ends[i - wr + 2 * HX]
            part = own.astype(F32)
        elif x < HX:
            part = pick(even_x, pb[x], pa[x])
        else:
            part = pick(even_x, pa[x - HX - wr], pb[x - HX - wr])
        part = turned(part)
        prof[x * wc : (x + 1) * wc, :] = part
        names[x * wc : (x + 1) * wc, :] = part.astype(BF)
    prof_rim[...] = jnp.zeros(prof_rim.shape, F32)
    for c in range(HY):
        prof_rim[0, pl.ds(HY + c, prow, stride=2 * HY), :] = prof[pl.ds(c, prow, stride=wc), :]
        prof_rim[1, pl.ds(c, prow, stride=2 * HY), :] = prof[pl.ds(wc - HY + c, prow, stride=wc), :]

    block = 3 * wc
    place = iota((block, lanes), 0).astype(F32)
    lift = HV - HL

    def first_step(m, _):
        for u in range(unroll):
            r = m * unroll + u
            hot = jnp.where(place == table[r, 0:1, :], table[r, K : K + 1, :], 0.0)
            for k in range(1, K):
                hot = hot + jnp.where(place == table[r, k : k + 1, :], table[r, K + k : K + k + 1, :], 0.0)
            named = names[pl.ds(pl.multiple_of((r + 1) // 2 * wc, wc), block), :]
            stokes = lax.dot_general(hot.astype(BF), named, ROWS_DOT, preferred_element_type=F32)[0:cols]
            drift[r] = stokes
            new = vel[r + lift, EDGE : EDGE + cols, :] + STEP * (turn[r] * stokes)
            mid[r, 0:EDGE, :] = blank
            mid[r, EDGE + cols :, :] = blank
            mid[r, EDGE : EDGE + cols, :] = new
            mid_rim[r, 0] = new[0 : 2 * EDGE]
            mid_rim[r, 1] = new[cols - 2 * EDGE :]
            for where in range(2):
                begin = RIM if where == 0 else cols - RIM - EDGE
                drift_rim[r, where] = drift[r, begin : begin + EDGE, :]
                spin_rim[r, where] = spin[r, begin : begin + EDGE, :]
        return 0

    lax.fori_loop(0, listed // unroll, first_step, 0)

    average = averager(lanes)
    means = jnp.zeros((cols, lanes), F32)
    for n in range(rows + 2):
        r = n + HL - 1
        absolute = spin[r] + vorticity(mid, r, EDGE, cols)
        old = vel[r + lift, EDGE : EDGE + cols, :] + mid[r, EDGE : EDGE + cols, :]
        new = 0.5 * old + (0.5 * STEP) * (absolute * drift[r])
        sums = jnp.dot(jnp.concatenate(split(new), axis=1), average, preferred_element_type=F32)
        means = jnp.where(lane // 2 == n, sums, means)
        if 1 <= n <= rows:
            out[n - 1] = new
            if n % (rows // 4) == 0:
                part = pl.ds(n - rows // 4, rows // 4)
                copies.append(pltpu.make_async_copy(out.at[part], out_far.at[part], sems.at[len(copies)]))
                copies[-1].start()
    total[...] = means

    at, to = iota(chosen.shape, 0), iota(chosen.shape, 1)
    reach = (RY + 2) * wc
    chosen[...] = ((to < reach) & (at == RY * (to % wc) + to // wc + RIM - 1)).astype(F32)
    at, to = iota((lanes, lanes), 0), iota((lanes, lanes), 1)
    spread[...] = ((at < reach) & (at % wc == to)).astype(F32).astype(BF)

    copies[0].wait()
    copies[1].wait()
    at, to = iota((wc, lanes), 0), iota((wc, lanes), 1)
    repeat = ((to < reach) & (to % wc == at)).astype(F32).astype(BF)
    shift = (lane // wc).astype(F32)
    weight = [weights[:, k, :] for k in range(K)]
    whole = sum(weight[1:], weight[0])
    code = [jnp.dot(codes[:, k, :].astype(F32).astype(BF), repeat, preferred_element_type=F32) for k in range(K)]
    share = [
        sum(jnp.dot(p, repeat, preferred_element_type=F32) for p in split3(weight[k] / whole)) for k in range(K)
    ]
    for near in range(RX + 2):
        wave_shares[near] = sum(
            jnp.where(code[k] == near * (RY + 2.0) + shift, share[k], 0.0) for k in range(K)
        )
    for copy in copies[2:]:
        copy.wait()


def rim_kernel(
    wide, ya, yb, mid_rim, drift_rim, spin_rim, total, list_rim, prof_rim, wave_shares, chosen, spread, velocity_in,
    velocity_out, current,
    vel, mid, prof, drift, spin, picked, means, strips, sems,
):
    vrow, lanes = wide.shape[0], wide.shape[2]
    rows, cols = vrow - 2 * HV, wide.shape[1] - 2 * EDGE
    wr, wc = current.shape[1], current.shape[2]
    listed = rows + 2 * HL
    prow = wr + 2 * HX
    even_y = is_even("gy")
    has_south, has_north = inside("gy")
    lane = iota((1, lanes), 1)
    sub = iota((EDGE, 1), 0)
    slots, vel_rows = y_rows(rows)

    def from_y(start, n):
        a, b = ya[start : start + n, :], yb[start : start + n, :]
        return pick(even_y, b, a) * has_south, pick(even_y, a, b) * has_north

    blank = jnp.zeros((EDGE, lanes), F32)
    for r in range(vrow):
        vel[0, r, 0:EDGE, :] = blank
        vel[1, r, 2 * EDGE :, :] = blank
        vel[0, r, EDGE:, :] = wide[r, EDGE : 3 * EDGE, :]
        vel[1, r, 0 : 2 * EDGE, :] = wide[r, cols - EDGE : cols + EDGE, :]
    for start in range(0, vel_rows, 2 * EDGE):
        pieces = from_y(slots + start, 2 * EDGE)
        for i in range(2):
            low, high = (p[i * EDGE : i * EDGE + EDGE] for p in pieces)
            low_moved, high_moved = pltpu.roll(low, lanes // 2, 1), pltpu.roll(high, lanes // 2, 1)
            low_in = jnp.where(sub % RIM == 0, low_moved, low)
            for j in range(2):
                r = (start + i * EDGE) // RIM + j
                if r < vrow:
                    at = j * RIM
                    vel[0, r, EDGE - RIM : EDGE, :] = low_in[at : at + RIM]
                    vel[0, r, EDGE - RIM - 1 : EDGE - RIM, :] = low[at : at + 1]
                    vel[1, r, 2 * EDGE : 2 * EDGE + RIM, :] = high[at : at + RIM]
                    vel[1, r, 2 * EDGE + RIM : 2 * EDGE + RIM + 1, :] = high_moved[at + RIM - 1 : at + RIM]

    prof[...] = prof_rim[...]
    south, north = from_y(0, slots)
    south, north = turned(south), turned(north)
    for c in range(HY):
        prof[0, pl.ds(c, TALL, stride=2 * HY), :] = south[TALL * c : TALL * (c + 1)]
        prof[1, pl.ds(HY + c, TALL, stride=2 * HY), :] = north[TALL * c : TALL * (c + 1)]

    per = lanes // 16
    start = slots + vel_rows
    span = 2 * per * HY
    place = iota((2 * span, lanes), 0).astype(F32)
    part = lane % 16
    offset = (part // EDGE) * span + ((lane // 16 + 1) // 2) * (2 * HY) + (part % EDGE) // RIM
    sub16 = iota((16, 1), 0)
    ones = jnp.ones((8, lanes), F32)
    none = jnp.zeros((2 * span, lanes), F32)
    for g in range(-(-listed // per)):
        tile, to = list_place(g * per, lanes)
        south, north = from_y(start + tile * 16, 16)
        full = list_rim[g]
        full = jnp.where(part // RIM == 0, pltpu.roll(south, (-to) % lanes, 1), full)
        full = jnp.where(part // RIM == 3, pltpu.roll(north, (3 * RIM - to) % lanes, 1), full)
        third = jnp.where(full >= 6.0, 2.0, jnp.where(full >= 3.0, 1.0, 0.0))
        full = jnp.where(sub16 < K, third + full + offset.astype(F32), full)
        hot = jnp.zeros((2 * span, lanes), F32)
        for k in range(K):
            hot = hot + jnp.where(place == full[k : k + 1], full[K + k : K + k + 1], 0.0)
        left = jnp.concatenate([hot, full[2 * K :], blank], axis=0).astype(BF)
        begin = g * (per // 2) * 2 * HY
        named = jnp.concatenate([prof[0, begin : begin + span, :], prof[1, begin : begin + span, :]], axis=0)
        right = jnp.concatenate([
            jnp.concatenate([named, blank, blank], axis=0),
            jnp.concatenate([none, ones, blank], axis=0),
        ], axis=1).astype(BF)
        both = lax.dot_general(left, right, ROWS_DOT, preferred_element_type=F32)
        for i in range(min(per, listed - g * per)):
            for side in range(2):
                at = i * 16 + side * EDGE
                drift[side, g * per + i] = both[at : at + EDGE, 0:lanes]
                spin[side, g * per + i] = both[at : at + EDGE, lanes:]

    lift = HV - HL
    for r in range(listed):
        for side in range(2):
            base = RIM + side * EDGE
            mid[side, r, 2 * EDGE * side : 2 * EDGE * side + EDGE, :] = blank
            mid[side, r, EDGE - side * EDGE : 3 * EDGE - side * EDGE, :] = mid_rim[r, side]
            absolute = spin[side, r] + vorticity(vel.at[side], r + lift, base, EDGE)
            new = vel[side, r + lift, base : base + EDGE, :] + STEP * (absolute * drift[side, r])
            mid[side, r, base : base + EDGE, :] = new

    average = averager(lanes)
    acc = jnp.zeros((4 * EDGE, lanes), F32)
    for n in range(rows + 2):
        r = n + HL - 1
        both = []
        for side in range(2):
            turns, drifts = (spin[side, r], spin_rim[r, side]), (drift[side, r], drift_rim[r, side])
            order = 1 - 2 * side
            absolute = jnp.concatenate(turns[::order], axis=0) + vorticity(mid.at[side], r, RIM, 2 * EDGE)
            tile = slice(RIM, RIM + 2 * EDGE)
            old = vel[side, r + lift, tile, :] + mid[side, r, tile, :]
            new = 0.5 * old + (0.5 * STEP) * (absolute * jnp.concatenate(drifts[::order], axis=0))
            both.append(new)
            if 1 <= n <= rows:
                strips[side, n - 1] = new[RIM : RIM + EDGE]
        sums = jnp.dot(
            jnp.concatenate(split(jnp.concatenate(both, axis=0)), axis=1), average, preferred_element_type=F32
        )
        acc = jnp.where(lane // 2 == n, sums, acc)
    copies = [
        pltpu.make_async_copy(strips.at[side], velocity_out.at[:, pl.ds(at, EDGE), :], sems.at[side])
        for side, at in ((0, 0), (1, cols - EDGE))
    ]
    for copy in copies:
        copy.start()
    means[0 : 2 * EDGE] = acc[0 : 2 * EDGE]
    means[2 * EDGE : 2 * RIM + cols - 2 * EDGE] = total[2 * EDGE - RIM : cols - 2 * EDGE + RIM, :]
    means[2 * RIM + cols - 2 * EDGE :] = acc[2 * EDGE :]

    named = chosen[...].astype(BF)
    picked[...] = sum(
        lax.dot_general(p, named, ROWS_DOT, preferred_element_type=F32) for p in split3(means[...])
    )
    summed = [
        sum(wave_shares[near] * picked[pl.ds(2 * near + c, wr, stride=2 * RX), :] for near in range(RX + 2))
        for c in range(2)
    ]
    sums = sum(
        jnp.dot(p, spread[...], preferred_element_type=F32) for p in split3(jnp.concatenate(summed, axis=0))
    )
    current[0] = sums[0:wr, 0:wc]
    current[1] = sums[wr:, 0:wc]
    for copy in copies:
        copy.wait()


VMEM = pl.BlockSpec(memory_space=pltpu.VMEM)
ANY = pl.BlockSpec(memory_space=pltpu.HBM)


def call(kernel, name, outs, *args, scratch=(), any_in=(), any_out=(), aliases=None):
    args = [pltpu.with_memory_space_constraint(v, pltpu.HBM) if i in any_in else v for i, v in enumerate(args)]
    return pl.pallas_call(
        kernel,
        out_shape=tuple(jax.ShapeDtypeStruct(shape, dtype) for shape, dtype in outs),
        in_specs=[ANY if i in any_in else VMEM for i in range(len(args))],
        out_specs=tuple(ANY if i in any_out else VMEM for i in range(len(outs))),
        scratch_shapes=list(scratch),
        input_output_aliases=aliases or {},
        compiler_params=pltpu.CompilerParams(vmem_limit_bytes=14 << 20),
        name=name,
    )(*args)


def shards(
    spectrum, courant, source, wave_land, stokes_kernel, velocity, coriolis,
    ocean_codes, ocean_weights, wave_codes, wave_weights,
):
    wr, wc, bins = spectrum.shape
    rows, cols, lanes = velocity.shape
    listed = rows + 2 * HL
    prow = wr + 2 * HX

    with jax.named_scope("spectrum_edges"):
        codes, weights = jnp.transpose(ocean_codes, (0, 2, 1)), jnp.transpose(ocean_weights, (0, 2, 1))
        size = sum(x_rows(cols))
        outs = [((wc, bins), BF)] * 2 + [((wr, bins), BF)] * 2 + [((size, lanes), BF)] * 2 + [((rows, 16, lanes), F32)]
        kept = [spectrum, courant, source, wave_land, stokes_kernel]
        xa, xb, ya, yb, oa, ob, lists, spectrum, courant, source, wave_land, stokes_kernel = call(
            edges_kernel, "edges", outs + [(v.shape, v.dtype) for v in kept],
            *kept, codes, weights, coriolis, velocity, any_in=range(9),
            scratch=[
                pltpu.VMEM(codes.shape, codes.dtype),
                pltpu.VMEM(weights.shape, F32),
                pltpu.VMEM(coriolis.shape, F32),
                pltpu.VMEM((2, HV, cols, lanes), F32),
                pltpu.SemaphoreType.DMA((9 + PARTS,)),
            ],
        )
        xa, xb = exchange("gx", xa, xb)
        ya, yb = exchange("gy", ya, yb)
        oa, ob = exchange("gx", oa, ob)

    with jax.named_scope("wave"):
        source, land = source.T, wave_land.T.astype(F32)
        edge = (HX, wc, lanes)
        cells_ends, ends, pa, pb = call(
            wave_ends_kernel, "wave_ends",
            [((2 * HX, wc, bins), BF), ((2 * HX, wc, lanes), BF), (edge, BF), (edge, BF)],
            spectrum, xa, xb, ya, yb, courant, source, land, stokes_kernel,
        )
        pa, pb = exchange("gx", pa, pb)
        cells_rest, rest = call(
            wave_rest_kernel, "wave_rest",
            [((wr - 2 * HX, wc, bins), BF), ((wr - 2 * HX, wc, lanes), BF)],
            spectrum, ya, yb, courant, source, land, stokes_kernel, ends,
        )

    with jax.named_scope("prepare"):
        wide = cols + 2 * EDGE
        groups = -(-listed // (lanes // 16))
        vel, spin, turn, table, list_rim = call(
            prepare_kernel, "prepare",
            [
                ((rows + 2 * HV, wide, lanes), F32),
                ((listed, cols, lanes), F32),
                ((listed, cols, lanes), F32),
                ((listed, 16, lanes), F32),
                ((groups, 16, lanes), F32),
            ],
            velocity, oa, ob, lists,
        )

    with jax.named_scope("halo"):
        size = sum(y_rows(rows)) + (list_place(listed - 1, lanes)[0] + 1) * 16
        ya, yb = call(
            halo_kernel, "halo", [((size, lanes), BF)] * 2, vel, oa, ob, lists, ends, rest, pa, pb
        )
        ya, yb = exchange("gy", ya, yb)

    with jax.named_scope("inner"):
        scratch = [
            pltpu.VMEM((listed, wide, lanes), F32),
            pltpu.VMEM((prow * wc, lanes), BF),
            pltpu.VMEM((prow * wc, lanes), F32),
            pltpu.VMEM((listed, cols, lanes), F32),
            pltpu.VMEM(velocity.shape, F32),
            pltpu.VMEM((wr, K, wc), jnp.int32),
            pltpu.VMEM((wr, K, wc), F32),
            pltpu.SemaphoreType.DMA((9,)),
        ]
        new_velocity, new_spectrum, mid_rim, drift_rim, spin_rim, total, prof_rim, wave_shares, chosen, spread = call(
            inner_kernel, "inner",
            [
                (velocity.shape, F32),
                (spectrum.shape, BF),
                ((listed, 2, 2 * EDGE, lanes), F32),
                ((listed, 2, EDGE, lanes), F32),
                ((listed, 2, EDGE, lanes), F32),
                ((cols, lanes), F32),
                ((2, 2 * HY * (TALL + 4), lanes), F32),
                ((RX + 2, wr, lanes), F32),
                ((cols + 2 * RIM, lanes), F32),
                ((lanes, lanes), BF),
            ],
            vel, spin, turn, table, ends, rest, pa, pb,
            jnp.transpose(wave_codes, (0, 2, 1)), jnp.transpose(wave_weights, (0, 2, 1)),
            cells_ends, cells_rest, scratch=scratch, any_in=(8, 9), any_out=(0, 1),
        )

    with jax.named_scope("rim"):
        scratch = [
            pltpu.VMEM((2, rows + 2 * HV, 3 * EDGE, lanes), F32),
            pltpu.VMEM((2, listed, 3 * EDGE, lanes), F32),
            pltpu.VMEM((2, 2 * HY * (TALL + 4), lanes), F32),
            pltpu.VMEM((2, listed, EDGE, lanes), F32),
            pltpu.VMEM((2, listed, EDGE, lanes), F32),
            pltpu.VMEM((lanes, lanes), F32),
            pltpu.VMEM((cols + 2 * RIM, lanes), F32),
            pltpu.VMEM((2, rows, EDGE, lanes), F32),
            pltpu.SemaphoreType.DMA((2,)),
        ]
        new_velocity, current = call(
            rim_kernel, "rim", [(velocity.shape, F32), ((2, wr, wc), F32)],
            vel, ya, yb, mid_rim, drift_rim, spin_rim, total, list_rim, prof_rim, wave_shares, chosen, spread,
            new_velocity, scratch=scratch, any_in=(12,), any_out=(0,), aliases={12: 0},
        )
    return new_spectrum, new_velocity, current


def solution(mesh):
    return jax.shard_map(
        shards,
        mesh=mesh,
        in_specs=(
            P("gx", "gy", None), P(), P("gx", "gy"), P("gx", "gy"), P(), P("gx", "gy", None),
            P("gx", "gy"), P("gx", "gy", None), P("gx", "gy", None), P("gx", "gy", None), P("gx", "gy", None),
        ),
        out_specs=(P("gx", "gy", None), P("gx", "gy", None), P(None, "gx", "gy")),
        check_vma=False,
    )
```

```python
import jax
import jax.numpy as jnp
from jax import lax
from jax.experimental import pallas as pl
from jax.experimental.pallas import tpu as pltpu
from jax.sharding import PartitionSpec as P

K = 4
RX = 2
RY = 4
STEP = 0.5
PARTS = 4
TALL = 24
RIM = 4
HV, HL = 5, 3
HX, HY = 3, 2
EDGE = 8
BF = jnp.bfloat16
F32 = jnp.float32
ROWS_DOT = (((0,), (0,)), ((), ()))


def partner(i, count, parity):
    return (i ^ 1) if parity == 0 else ((i + 1) ^ 1) - 1


def swap(value, axis, parity):
    nx, ny = lax.axis_size("gx"), lax.axis_size("gy")
    pairs = []
    for x in range(nx):
        for y in range(ny):
            tx, ty = x, y
            if axis == "gx":
                tx = partner(x, nx, parity) % nx
            else:
                ty = partner(y, ny, parity)
                if not 0 <= ty < ny:
                    tx, ty = x ^ 1, y
            pairs.append((x * ny + y, tx * ny + ty))
    return lax.ppermute(value, ("gx", "gy"), pairs)


def exchange(axis, to_a, to_b):
    from_a = swap(to_a, axis, 0)
    from_b = swap(to_b, axis, 1)
    return from_a, from_b


def is_even(axis):
    return lax.axis_index(axis) % 2 == 0


def inside(axis):
    index = lax.axis_index(axis)
    before = jnp.where(index == 0, 0.0, 1.0).astype(F32)
    after = jnp.where(index == lax.axis_size(axis) - 1, 0.0, 1.0).astype(F32)
    return before, after


def pick(cond, one, other):
    return jnp.where(cond, one.astype(F32), other.astype(F32))


def split(value):
    high = value.astype(BF)
    return high, (value - high.astype(F32)).astype(BF)


def split3(value):
    high = value.astype(BF)
    rest = value - high.astype(F32)
    middle = rest.astype(BF)
    return high, middle, (rest - middle.astype(F32)).astype(BF)


def iota(shape, dim):
    return lax.broadcasted_iota(jnp.int32, shape, dim)


def x_rows(cols):
    return (HV - 1) * cols, HL * 16


def edges_kernel(*refs):
    (spec_far, courant_far, source_far, land_far, codes_far, weights_far, coriolis_far, vel_far, basis_far) = refs[:9]
    (wave_codes_far, wave_weights_far) = refs[9:11]
    (oa, ob, ya, yb, lists, spec, courant, source_t, land_t, basis, wave_codes, wave_weights) = refs[11:23]
    (source, land, codes, weights, coriolis, vel, sems) = refs[23:]
    rows, cols, bins = spec.shape
    lanes = vel.shape[-1]
    pairs = [(spec_far, spec)]
    pairs += [(vel_far.at[pl.ds(at, HV)], vel.at[i]) for i, at in ((0, 0), (1, vel_far.shape[0] - HV))]
    pairs += [(codes_far, codes), (weights_far, weights), (coriolis_far, coriolis)]
    pairs += [(courant_far, courant), (source_far, source), (land_far, land), (basis_far, basis)]
    pairs += [(wave_codes_far, wave_codes), (wave_weights_far, wave_weights)]
    copies = [pltpu.make_async_copy(one, two, sems.at[i]) for i, (one, two) in enumerate(pairs)]
    for copy in copies:
        copy.start()
    even_x, even_y = is_even("gx"), is_even("gy")

    def put(at, last, first):
        n = last.shape[0]
        oa[at : at + n] = jnp.where(even_x, last, first).astype(BF)
        ob[at : at + n] = jnp.where(even_x, first, last).astype(BF)

    at, cell = iota((2 * rows, rows * cols), 0), iota((2 * rows, rows * cols), 1)
    wanted = jnp.where(at < rows, at * cols, (at - rows) * cols + cols - 1)
    chosen = (cell == wanted).astype(F32).astype(BF)
    copies[0].wait()
    sides = jnp.dot(chosen, spec[...].reshape(rows * cols, bins), preferred_element_type=F32)
    start = sum(x_rows(codes.shape[2]))
    for i in range(bins // lanes):
        part = slice(i * lanes, (i + 1) * lanes)
        put(start + i * cols, spec[rows - 1, :, part].astype(F32), spec[0, :, part].astype(F32))
    first, last = sides[0:rows], sides[rows:]
    ya[...] = jnp.where(even_y, last, first).astype(BF)
    yb[...] = jnp.where(even_y, first, last).astype(BF)

    for copy in copies[1:]:
        copy.wait()
    source_t[...] = source[...].T
    land_t[...] = land[...].astype(F32).T
    listed, wide = codes.shape[0], codes.shape[2]
    is_u = iota((1, lanes), 1) < lanes // 2
    outer = [
        jnp.where(is_u, pltpu.roll(vel[side, one], lanes // 2, 1), vel[side, two])
        for side, one, two in ((1, 0, 1), (0, HV - 1, HV - 2))
    ]
    put(0, *outer)
    for i in range(1, HV - 1):
        put(i * wide, vel[1, i + 1], vel[0, i - 1])
    for r in range(listed):
        lists[r] = jnp.zeros((16, lanes), F32)
        weight = weights[r]
        turn = coriolis[r : r + 1, :]
        high = turn.astype(BF).astype(F32)
        lists[r, 0:K, 0:wide] = codes[r].astype(F32)
        lists[r, K : 2 * K, 0:wide] = weight / jnp.sum(weight, axis=0, keepdims=True)
        lists[r, 2 * K : 2 * K + 1, 0:wide] = high
        lists[r, 2 * K + 1 : 2 * K + 2, 0:wide] = turn - high
    for i in range(HL):
        put((HV - 1) * wide + i * 16, lists[listed - HL + i], lists[i])


def advance(chosen, spec, sides, ya, yb, courant, source, land, weights, at_once, put):
    rows, cols, _ = spec.shape
    even_y = is_even("gy")
    has_south, has_north = inside("gy")
    south = pick(even_y, yb[...], ya[...]) * has_south
    north = pick(even_y, ya[...], yb[...]) * has_north
    cx, cy = courant[0:1, :], courant[1:2, :]
    ax, ay = jnp.abs(cx), jnp.abs(cy)
    from_west, from_south = cx > 0.0, cy > 0.0
    keep = 1.0 - ax - ay
    sub = iota((cols, 1), 0)
    cells = []
    for x in chosen:
        center = spec[x].astype(F32)
        before = spec[x - 1].astype(F32) if x else sides[0]
        after = spec[x + 1].astype(F32) if x < rows - 1 else sides[1]
        below = jnp.where(sub == 0, south[x : x + 1, :], pltpu.roll(center, 1, 0))
        above = jnp.where(sub == cols - 1, north[x : x + 1, :], pltpu.roll(center, cols - 1, 0))
        advected = (
            keep * center
            + ax * jnp.where(from_west, before, after)
            + ay * jnp.where(from_south, below, above)
        )
        wind = 1.0 + 0.2 * source[:, x : x + 1]
        updated = land[:, x : x + 1] * (advected * (wind - 0.1 * advected))
        cells.append(updated.astype(BF))
        if len(cells) == at_once:
            parts = jnp.dot(jnp.concatenate(cells, axis=0), weights[...], preferred_element_type=F32)
            for i, value in enumerate(cells):
                put(x - at_once + 1 + i, value, parts[i * cols : (i + 1) * cols])
            cells = []


def sides_kernel(xb, xa, after, sides):
    even_x = is_even("gx")
    cols, bins = sides.shape[1], sides.shape[2]
    lanes = xa.shape[1]
    start = xa.shape[0] - cols * bins // lanes
    for i in range(bins // lanes):
        a, b = (ref[start + i * cols : start + (i + 1) * cols, :] for ref in (xa, xb))
        part = slice(i * lanes, (i + 1) * lanes)
        sides[0, :, part], sides[1, :, part] = pick(even_x, b, a).astype(BF), pick(even_x, a, b).astype(BF)


def wave_ends_kernel(spec, sides, yb, ya, courant, source, land, weights, out, profile, pa, pb):
    rows, cols, bins = spec.shape
    even_x = is_even("gx")
    parts = []

    def put(x, value, part):
        i = len(parts)
        out[i], profile[i] = value, part.astype(BF)
        parts.append(part)

    ends = list(range(HX)) + list(range(rows - HX, rows))
    advance(ends, spec, [sides[i].astype(F32) for i in range(2)], ya, yb, courant, source, land, weights, HX, put)
    for i in range(HX):
        first, last = parts[i], parts[HX + i]
        pa[i] = jnp.where(even_x, last, first).astype(BF)
        pb[i] = jnp.where(even_x, first, last).astype(BF)


def wave_rest_kernel(spec, yb, ya, courant, source, land, weights, ends, out, profile):
    rows = spec.shape[0]

    def put(x, value, part):
        out[x - HX], profile[x - HX] = value, part.astype(BF)

    advance(range(HX, rows - HX), spec, None, ya, yb, courant, source, land, weights, (rows - 2 * HX) // 2, put)


def list_place(r, lanes):
    per = lanes // 16
    return r // (4 * per), (r % per) * 16 + RIM * ((r // per) % 4)


def y_rows(rows):
    pairs = (rows + 2 * HV + 1) // 2
    return TALL * HY, (pairs + pairs % 2) * EDGE


def row_of(i, rows, own, ends, reach):
    return own[i] if 0 <= i < rows else ends[i + reach if i < 0 else i - rows + reach]


def halo_kernel(vel, vel_halo, ob, oa, lists, ends, rest, pb, pa, ya, yb):
    rows, cols, lanes = vel.shape
    vrow = rows + 2 * HV
    even_x, even_y = is_even("gx"), is_even("gy")
    wr, wc = rest.shape[0] + 2 * HX, rest.shape[1]

    def put(at, last, first):
        n = last.shape[0]
        ya[at : at + n] = jnp.where(even_y, last, first).astype(BF)
        yb[at : at + n] = jnp.where(even_y, first, last).astype(BF)

    before, after = pick(even_x, pb[...], pa[...]), pick(even_x, pa[...], pb[...])
    joined = jnp.concatenate([before.astype(BF), ends[0:HX], rest[...], ends[HX:], after.astype(BF)], axis=0)
    count = (wr + 2 * HX) * wc
    slots = TALL * HY
    at, cell = iota((2 * slots, count), 0), iota((2 * slots, count), 1)
    side, rest = at // slots, at % slots
    column = rest // TALL + jnp.where(side == 0, wc - HY, 0)
    row = rest % TALL
    chosen = ((row < wr + 2 * HX) & (cell == row * wc + column)).astype(F32).astype(BF)
    sides = jnp.dot(chosen, joined.reshape(count, lanes), preferred_element_type=F32)
    put(0, sides[0:slots], sides[slots:])

    sub = iota((EDGE, 1), 0)
    is_u = iota((1, lanes), 1) < lanes // 2
    blocks = []
    for r in range(vrow):
        to = RIM * (r % 2)

        def ends_of(ref, k):
            return ref[k, cols - EDGE : cols, :], ref[k, 0:EDGE, :]

        i = r - HV
        if 0 <= i < rows:
            last, first = ends_of(vel, i)
        else:
            last, first = ends_of(vel_halo, r if i < 0 else r - rows)

        def moved(value, one, two):
            return pltpu.roll(value, (two - one) % EDGE, 0) if one != two else value

        one, two = moved(last, EDGE - RIM, to), moved(last, EDGE - RIM - 1, to)
        last = jnp.where(sub == to, jnp.where(is_u, two, pltpu.roll(one, lanes // 2, 1)), one)
        one, two = moved(first, 0, to), moved(first, RIM, to + RIM - 1)
        first = jnp.where(sub == to + RIM - 1, jnp.where(is_u, one, pltpu.roll(two, lanes // 2, 1)), one)
        blocks.append((last, first))
    pairs = [
        [jnp.where(sub < RIM, blocks[r][i], blocks[r + 1][i]) for i in range(2)] for r in range(0, vrow, 2)
    ]
    pairs += [[jnp.zeros((EDGE, lanes), F32)] * 2] * (len(pairs) % 2)
    for i in range(0, len(pairs), 2):
        put(slots + i * EDGE, *[jnp.concatenate([pairs[i][j], pairs[i + 1][j]], axis=0) for j in range(2)])
    start = slots + len(pairs) * EDGE

    group = iota((1, lanes), 1) // RIM
    x_start = (HV - 1) * cols
    tiles = list_place(rows + 2 * HL - 1, lanes)[0] + 1
    acc = [[jnp.zeros((16, lanes), F32)] * 2 for _ in range(tiles)]
    for r in range(rows + 2 * HL):
        if HL <= r < HL + rows:
            own = lists[r - HL]
        else:
            i = r if r < HL else r - HL - rows
            at = x_start + i * 16
            one, two = (ob, oa) if r < HL else (oa, ob)
            own = pick(even_x, one[at : at + 16, :], two[at : at + 16, :])
        tile, to = list_place(r, lanes)
        acc[tile] = [
            jnp.where(group == to // RIM, pltpu.roll(own, (to - where) % lanes, 1), a)
            for a, where in zip(acc[tile], (cols - RIM, 0))
        ]
    for tile in range(tiles):
        put(start + tile * 16, acc[tile][0], acc[tile][1])


def vorticity(ref, r, base, count):
    half = ref.shape[-1] // 2
    is_u = iota((1, 2 * half), 1) < half

    def at(dx, dy):
        return ref[r + dx, base + dy : base + dy + count, :]

    near = jnp.where(is_u, at(0, -1), at(1, 0)) - jnp.where(is_u, at(0, 1), at(-1, 0))
    far = jnp.where(is_u, at(0, -2), at(2, 0)) - jnp.where(is_u, at(0, 2), at(-2, 0))
    part = (8.0 / 12.0) * near - (1.0 / 12.0) * far
    return part + pltpu.roll(part, half, 1)


def averager(lanes):
    at = iota((2 * lanes, lanes), 0)
    to = iota((2 * lanes, lanes), 1)
    half = lanes // 2
    return jnp.where((at % lanes) // half == to % 2, 1.0 / half, 0.0).astype(BF)


def turned(value):
    half = value.shape[-1] // 2
    sign = jnp.where(iota((1, 2 * half), 1) < half, 1.0, -1.0)
    return pltpu.roll(value, half, 1) * sign


def one_hot(full, cols):
    lanes = full.shape[1]
    wave_cols = cols // RY
    codes = full[0:EDGE]
    third = jnp.where(codes >= 6.0, 2.0, jnp.where(codes >= 3.0, 1.0, 0.0))
    slot = third * (wave_cols - 3.0) + codes + (iota((1, lanes), 1) // RY).astype(F32) - 1.0
    place = iota((3 * wave_cols, lanes), 0).astype(F32)
    hot = jnp.where(place == slot[0:1], full[K : K + 1], 0.0)
    for k in range(1, K):
        hot = hot + jnp.where(place == slot[k : k + 1], full[K + k : K + k + 1], 0.0)
    return hot.astype(BF)


def rim_lists(full, rim, r, cols):
    lanes = full.shape[1]
    lane = iota((1, lanes), 1)
    to = (r % (lanes // 16)) * 16
    rim = jnp.where(lane // RIM == to // RIM + 1, pltpu.roll(full, (to + RIM) % lanes, 1), rim)
    return jnp.where(lane // RIM == to // RIM + 2, pltpu.roll(full, (to + 3 * RIM - cols) % lanes, 1), rim)


def prepare_own_kernel(
    own, lists, codes, weights, spin, turn, table, list_rim, wave_shares, chosen, spread, vel
):
    rows, cols, lanes = own.shape
    per = lanes // 16
    blank = jnp.zeros((EDGE, lanes), F32)

    def fill(i, _):
        vel[i, 0:EDGE, :] = blank
        vel[i, EDGE + cols :, :] = blank
        vel[i, EDGE : EDGE + cols, :] = own[i]
        return 0

    lax.fori_loop(0, rows, fill, 0, unroll=8)
    rim = [jnp.zeros((16, lanes), F32)] * list_rim.shape[0]
    for i in range(rows):
        g = (i + HL) // per
        full = lists[i]
        table[i], rim[g] = one_hot(full, cols), rim_lists(full, rim[g], i + HL, cols)
    for g, value in enumerate(rim):
        list_rim[g] = value

    ones = jnp.ones((8, lanes), BF)

    def widened(i):
        return lax.dot_general(lists[i, 2 * K :, :].astype(BF), ones, ROWS_DOT, preferred_element_type=F32)[0:cols]

    for i in (0, 1, rows - 2, rows - 1):
        spin[i] = widened(i)
    half = (rows - 4) // 2

    def absolute(m, _):
        for u in range(half):
            i = m * half + u + 2
            wide = widened(i)
            spin[i] = wide
            turn[i - 2] = wide + vorticity(vel, i, EDGE, cols)
        return 0

    lax.fori_loop(0, 2, absolute, 0)

    wc = cols // RY
    lane = iota((1, lanes), 1)
    at, to = iota(chosen.shape, 0), iota(chosen.shape, 1)
    reach = (RY + 2) * wc
    chosen[...] = ((to < reach) & (at == RY * (to % wc) + to // wc + RIM - 1)).astype(F32)
    at, to = iota((lanes, lanes), 0), iota((lanes, lanes), 1)
    spread[...] = ((at < reach) & (at % wc == to)).astype(F32).astype(BF)

    at, to = iota((wc, lanes), 0), iota((wc, lanes), 1)
    repeat = ((to < reach) & (to % wc == at)).astype(F32).astype(BF)
    shift = (lane // wc).astype(F32)
    weight = [weights[:, k, :] for k in range(K)]
    whole = sum(weight[1:], weight[0])
    code = [jnp.dot(codes[:, k, :].astype(F32).astype(BF), repeat, preferred_element_type=F32) for k in range(K)]
    share = [
        sum(jnp.dot(p, repeat, preferred_element_type=F32) for p in split3(weight[k] / whole)) for k in range(K)
    ]
    for near in range(RX + 2):
        wave_shares[near] = sum(
            jnp.where(code[k] == near * (RY + 2.0) + shift, share[k], 0.0) for k in range(K)
        )


def prepare_ends_kernel(own, ob, oa, spin_own, list_own, vel_halo, spin, turn, table, list_rim, vel):
    rows, cols, lanes = own.shape
    per = lanes // 16
    even_x = is_even("gx")
    blank = jnp.zeros((EDGE, lanes), F32)
    list_rim[...] = list_own[...]
    ones = jnp.ones((8, lanes), BF)
    for side in range(2):
        one, two = (oa, ob) if side else (ob, oa)

        def from_x(start, n):
            return pick(even_x, one[start : start + n, :], two[start : start + n, :])

        parts = [from_x(i * cols, cols) for i in range(HV - 1)]
        outer = pltpu.roll(parts[0], lanes // 2, 1)
        parts = parts[1:] + [parts[0], outer] if side else [outer] + parts
        for k in range(HV):
            vel_halo[side * HV + k] = parts[k]
        near = [own[i] for i in (range(rows - HV + 1, rows) if side else range(HV - 1))]
        for k, value in enumerate(near + parts if side else parts + near):
            vel[side, k, 0:EDGE, :] = blank
            vel[side, k, EDGE + cols :, :] = blank
            vel[side, k, EDGE : EDGE + cols, :] = value
        for k in range(HL):
            at = side * HL + k
            r = k + side * (rows + HL)
            full = from_x((HV - 1) * cols + k * 16, 16)
            table[at], list_rim[r // per] = one_hot(full, cols), rim_lists(full, list_rim[r // per], r, cols)
            spin[at] = lax.dot_general(full[2 * K :].astype(BF), ones, ROWS_DOT, preferred_element_type=F32)[0:cols]
        for k in range(HL + 2):
            i = k + (rows - 2 if side else -HL)
            turn[side * (HL + 2) + k] = row_of(i, rows, spin_own, spin, HL) + vorticity(vel.at[side], k + 2, EDGE, cols)


def inner_kernel(
    vel, vel_halo, spin_own, spin_ends, turn_own, turn_ends, table_own, table_ends,
    ends, rest, pb, pa, cells_ends, cells_rest,
    out, cells_far, mid_rim, drift_rim, spin_rim, total, prof_rim,
    mid, names, prof, drift, sems,
):
    rows, cols, lanes = out.shape
    copies = []
    wr, wc = rest.shape[0] + 2 * HX, rest.shape[1]
    for part, to in (
        (cells_ends.at[pl.ds(0, HX)], cells_far.at[pl.ds(0, HX)]),
        (cells_rest, cells_far.at[pl.ds(HX, wr - 2 * HX)]),
        (cells_ends.at[pl.ds(HX, HX)], cells_far.at[pl.ds(wr - HX, HX)]),
    ):
        copies.append(pltpu.make_async_copy(part, to, sems.at[len(copies)]))
    for copy in copies:
        copy.start()
    listed = rows + 2 * HL
    prow = wr + 2 * HX
    even_x = is_even("gx")
    lane = iota((1, lanes), 1)
    blank = jnp.zeros((EDGE, lanes), F32)
    for x in range(prow):
        if HX <= x < HX + wr:
            i = x - HX
            own = ends[i] if i < HX else rest[i - HX] if i < wr - HX else ends[i - wr + 2 * HX]
            part = own.astype(F32)
        elif x < HX:
            part = pick(even_x, pb[x], pa[x])
        else:
            part = pick(even_x, pa[x - HX - wr], pb[x - HX - wr])
        part = turned(part)
        prof[x * wc : (x + 1) * wc, :] = part
        names[x * wc : (x + 1) * wc, :] = part.astype(BF)
    prof_rim[...] = jnp.zeros(prof_rim.shape, F32)
    for c in range(HY):
        prof_rim[0, pl.ds(HY + c, prow, stride=2 * HY), :] = prof[pl.ds(c, prow, stride=wc), :]
        prof_rim[1, pl.ds(c, prow, stride=2 * HY), :] = prof[pl.ds(wc - HY + c, prow, stride=wc), :]

    block = 3 * wc

    def first(r, vel_ref, table_ref, turn_ref, spin_ref, vk, tk, uk):
        named = names[pl.ds(pl.multiple_of((r + 1) // 2 * wc, wc), block), :]
        stokes = lax.dot_general(table_ref[tk], named, ROWS_DOT, preferred_element_type=F32)[0:cols]
        drift[r] = stokes
        new = vel_ref[vk] + STEP * (turn_ref[uk] * stokes)
        mid[r, 0:EDGE, :] = blank
        mid[r, EDGE + cols :, :] = blank
        mid[r, EDGE : EDGE + cols, :] = new
        mid_rim[r, 0] = new[0 : 2 * EDGE]
        mid_rim[r, 1] = new[cols - 2 * EDGE :]
        for where in range(2):
            begin = RIM if where == 0 else cols - RIM - EDGE
            drift_rim[r, where] = drift[r, begin : begin + EDGE, :]
            spin_rim[r, where] = spin_ref[tk, begin : begin + EDGE, :]

    for i in [*range(-HL, 2), *range(rows - 2, rows + HL)]:
        end = i + HL if i < 2 else i - rows + HL + 4
        if 0 <= i < rows:
            first(i + HL, vel, table_own, turn_ends, spin_own, i, i, end)
        else:
            far = 0 if i < 0 else rows
            first(i + HL, vel_halo, table_ends, turn_ends, spin_ends, i - far + HV, i - far + HL, end)
    unroll = (rows - 4) // 2

    def first_step(m, _):
        for u in range(unroll):
            i = m * unroll + u + 2
            first(i + HL, vel, table_own, turn_own, spin_own, i, i, i - 2)
        return 0

    lax.fori_loop(0, 2, first_step, 0)

    average = averager(lanes)
    means = jnp.zeros((cols, lanes), F32)
    for n in range(rows + 2):
        r = n + HL - 1
        absolute = row_of(n - 1, rows, spin_own, spin_ends, HL) + vorticity(mid, r, EDGE, cols)
        old = row_of(n - 1, rows, vel, vel_halo, HV) + mid[r, EDGE : EDGE + cols, :]
        new = 0.5 * old + (0.5 * STEP) * (absolute * drift[r])
        sums = jnp.dot(jnp.concatenate(split(new), axis=1), average, preferred_element_type=F32)
        means = jnp.where(lane // 2 == n, sums, means)
        if 1 <= n <= rows:
            out[n - 1] = new
    total[...] = means

    for copy in copies:
        copy.wait()


def rim_kernel(
    own, vel_halo, yb, ya, mid_rim, drift_rim, spin_rim, total, list_rim, prof_rim, wave_shares, chosen, spread, inner,
    out, current,
    vel, mid, prof, drift, spin, picked, means, strips, sems,
):
    rows, cols, lanes = own.shape
    vrow = rows + 2 * HV
    wr, wc = current.shape[1], current.shape[2]
    listed = rows + 2 * HL
    prow = wr + 2 * HX
    even_y = is_even("gy")
    has_south, has_north = inside("gy")
    lane = iota((1, lanes), 1)
    sub = iota((EDGE, 1), 0)
    slots, vel_rows = y_rows(rows)

    def from_y(start, n):
        a, b = ya[start : start + n, :], yb[start : start + n, :]
        return pick(even_y, b, a) * has_south, pick(even_y, a, b) * has_north

    middle = pl.ds(EDGE, cols - 2 * EDGE)
    copies = [pltpu.make_async_copy(inner.at[:, middle, :], out.at[:, middle, :], sems.at[0])]
    copies[0].start()

    blank = jnp.zeros((EDGE, lanes), F32)
    for r in range(vrow):
        vel[0, r, 0:EDGE, :] = blank
        vel[1, r, 2 * EDGE :, :] = blank
        ref, k = (own, r - HV) if HV <= r < HV + rows else (vel_halo, r if r < HV else r - rows)
        vel[0, r, EDGE:, :] = ref[k, 0 : 2 * EDGE, :]
        vel[1, r, 0 : 2 * EDGE, :] = ref[k, cols - 2 * EDGE : cols, :]
    for start in range(0, vel_rows, 2 * EDGE):
        pieces = from_y(slots + start, 2 * EDGE)
        for i in range(2):
            low, high = (p[i * EDGE : i * EDGE + EDGE] for p in pieces)
            low_moved, high_moved = pltpu.roll(low, lanes // 2, 1), pltpu.roll(high, lanes // 2, 1)
            low_in = jnp.where(sub % RIM == 0, low_moved, low)
            for j in range(2):
                r = (start + i * EDGE) // RIM + j
                if r < vrow:
                    at = j * RIM
                    vel[0, r, EDGE - RIM : EDGE, :] = low_in[at : at + RIM]
                    vel[0, r, EDGE - RIM - 1 : EDGE - RIM, :] = low[at : at + 1]
                    vel[1, r, 2 * EDGE : 2 * EDGE + RIM, :] = high[at : at + RIM]
                    vel[1, r, 2 * EDGE + RIM : 2 * EDGE + RIM + 1, :] = high_moved[at + RIM - 1 : at + RIM]

    prof[...] = prof_rim[...]
    south, north = from_y(0, slots)
    south, north = turned(south), turned(north)
    for c in range(HY):
        prof[0, pl.ds(c, TALL, stride=2 * HY), :] = south[TALL * c : TALL * (c + 1)]
        prof[1, pl.ds(HY + c, TALL, stride=2 * HY), :] = north[TALL * c : TALL * (c + 1)]

    per = lanes // 16
    start = slots + vel_rows
    span = 2 * per * HY
    place = iota((2 * span, lanes), 0).astype(F32)
    part = lane % 16
    offset = (part // EDGE) * span + ((lane // 16 + 1) // 2) * (2 * HY) + (part % EDGE) // RIM
    sub16 = iota((16, 1), 0)
    ones = jnp.ones((8, lanes), F32)
    none = jnp.zeros((2 * span, lanes), F32)
    for g in range(-(-listed // per)):
        tile, to = list_place(g * per, lanes)
        south, north = from_y(start + tile * 16, 16)
        full = list_rim[g]
        full = jnp.where(part // RIM == 0, pltpu.roll(south, (-to) % lanes, 1), full)
        full = jnp.where(part // RIM == 3, pltpu.roll(north, (3 * RIM - to) % lanes, 1), full)
        third = jnp.where(full >= 6.0, 2.0, jnp.where(full >= 3.0, 1.0, 0.0))
        full = jnp.where(sub16 < K, third + full + offset.astype(F32), full)
        hot = jnp.zeros((2 * span, lanes), F32)
        for k in range(K):
            hot = hot + jnp.where(place == full[k : k + 1], full[K + k : K + k + 1], 0.0)
        left = jnp.concatenate([hot, full[2 * K :], blank], axis=0).astype(BF)
        begin = g * (per // 2) * 2 * HY
        named = jnp.concatenate([prof[0, begin : begin + span, :], prof[1, begin : begin + span, :]], axis=0)
        right = jnp.concatenate([
            jnp.concatenate([named, blank, blank], axis=0),
            jnp.concatenate([none, ones, blank], axis=0),
        ], axis=1).astype(BF)
        both = lax.dot_general(left, right, ROWS_DOT, preferred_element_type=F32)
        for i in range(min(per, listed - g * per)):
            for side in range(2):
                at = i * 16 + side * EDGE
                drift[side, g * per + i] = both[at : at + EDGE, 0:lanes]
                spin[side, g * per + i] = both[at : at + EDGE, lanes:]

    lift = HV - HL
    for r in range(listed):
        for side in range(2):
            base = RIM + side * EDGE
            mid[side, r, 2 * EDGE * side : 2 * EDGE * side + EDGE, :] = blank
            mid[side, r, EDGE - side * EDGE : 3 * EDGE - side * EDGE, :] = mid_rim[r, side]
            absolute = spin[side, r] + vorticity(vel.at[side], r + lift, base, EDGE)
            new = vel[side, r + lift, base : base + EDGE, :] + STEP * (absolute * drift[side, r])
            mid[side, r, base : base + EDGE, :] = new

    average = averager(lanes)
    acc = jnp.zeros((4 * EDGE, lanes), F32)
    step = rows // PARTS
    for n in range(rows + 2):
        r = n + HL - 1
        both = []
        for side in range(2):
            turns, drifts = (spin[side, r], spin_rim[r, side]), (drift[side, r], drift_rim[r, side])
            order = 1 - 2 * side
            absolute = jnp.concatenate(turns[::order], axis=0) + vorticity(mid.at[side], r, RIM, 2 * EDGE)
            tile = slice(RIM, RIM + 2 * EDGE)
            old = vel[side, r + lift, tile, :] + mid[side, r, tile, :]
            new = 0.5 * old + (0.5 * STEP) * (absolute * jnp.concatenate(drifts[::order], axis=0))
            both.append(new)
            if 1 <= n <= rows:
                strips[side, n - 1] = new[RIM : RIM + EDGE]
        sums = jnp.dot(
            jnp.concatenate(split(jnp.concatenate(both, axis=0)), axis=1), average, preferred_element_type=F32
        )
        acc = jnp.where(lane // 2 == n, sums, acc)
        if n and n % step == 0:
            part = pl.ds(n - step, step)
            for side, at in ((0, 0), (1, cols - EDGE)):
                one, two = strips.at[side, part], out.at[part, pl.ds(at, EDGE), :]
                copies.append(pltpu.make_async_copy(one, two, sems.at[len(copies)]))
                copies[-1].start()
    means[0 : 2 * EDGE] = acc[0 : 2 * EDGE]
    means[2 * EDGE : 2 * RIM + cols - 2 * EDGE] = total[2 * EDGE - RIM : cols - 2 * EDGE + RIM, :]
    means[2 * RIM + cols - 2 * EDGE :] = acc[2 * EDGE :]

    named = chosen[...].astype(BF)
    picked[...] = sum(
        lax.dot_general(p, named, ROWS_DOT, preferred_element_type=F32) for p in split3(means[...])
    )
    summed = [
        sum(wave_shares[near] * picked[pl.ds(2 * near + c, wr, stride=2 * RX), :] for near in range(RX + 2))
        for c in range(2)
    ]
    sums = sum(
        jnp.dot(p, spread[...], preferred_element_type=F32) for p in split3(jnp.concatenate(summed, axis=0))
    )
    current[0] = sums[0:wr, 0:wc]
    current[1] = sums[wr:, 0:wc]
    for copy in copies:
        copy.wait()


VMEM = pl.BlockSpec(memory_space=pltpu.VMEM)
ANY = pl.BlockSpec(memory_space=pltpu.HBM)


def call(kernel, name, outs, *args, scratch=(), any_in=(), any_out=()):
    args = [pltpu.with_memory_space_constraint(v, pltpu.HBM) if i in any_in else v for i, v in enumerate(args)]
    return pl.pallas_call(
        kernel,
        out_shape=tuple(jax.ShapeDtypeStruct(shape, dtype) for shape, dtype in outs),
        in_specs=[ANY if i in any_in else VMEM for i in range(len(args))],
        out_specs=tuple(ANY if i in any_out else VMEM for i in range(len(outs))),
        scratch_shapes=list(scratch),
        compiler_params=pltpu.CompilerParams(vmem_limit_bytes=14 << 20),
        name=name,
    )(*args)


def shards(
    spectrum, courant, source, wave_land, stokes_kernel, velocity, coriolis,
    ocean_codes, ocean_weights, wave_codes, wave_weights,
):
    wr, wc, bins = spectrum.shape
    rows, cols, lanes = velocity.shape
    listed = rows + 2 * HL
    prow = wr + 2 * HX

    with jax.named_scope("spectrum_edges"):
        codes, weights = jnp.transpose(ocean_codes, (0, 2, 1)), jnp.transpose(ocean_weights, (0, 2, 1))
        size = sum(x_rows(cols)) + wc * bins // lanes
        outs = [((size, lanes), BF)] * 2 + [((wr, bins), BF)] * 2 + [((rows, 16, lanes), F32)]
        outs += [(spectrum.shape, BF), (courant.shape, F32), ((wc, wr), F32), ((wc, wr), F32), (stokes_kernel.shape, BF)]
        outs += [((wr, K, wc), wave_codes.dtype), ((wr, K, wc), F32)]
        oa, ob, ya, yb, lists, spectrum, courant, source, land, stokes_kernel, wave_codes, wave_weights = call(
            edges_kernel, "edges", outs,
            spectrum, courant, source, wave_land, codes, weights, coriolis, velocity, stokes_kernel,
            jnp.transpose(wave_codes, (0, 2, 1)), jnp.transpose(wave_weights, (0, 2, 1)), any_in=range(11),
            scratch=[
                pltpu.VMEM(source.shape, F32),
                pltpu.VMEM(wave_land.shape, wave_land.dtype),
                pltpu.VMEM(codes.shape, codes.dtype),
                pltpu.VMEM(weights.shape, F32),
                pltpu.VMEM(coriolis.shape, F32),
                pltpu.VMEM((2, HV, cols, lanes), F32),
                pltpu.SemaphoreType.DMA((12,)),
            ],
        )
        oa, ob = exchange("gx", oa, ob)
        ya, yb = exchange("gy", ya, yb)

    with jax.named_scope("prepare_own"):
        groups = -(-listed // (lanes // 16))
        level = (cols, lanes)
        spin_own, turn_own, table_own, list_own, wave_shares, chosen, spread = call(
            prepare_own_kernel, "prepare_own",
            [
                ((rows, *level), F32), ((rows - 4, *level), F32), ((rows, 3 * wc, lanes), BF), ((groups, 16, lanes), F32),
                ((RX + 2, wr, lanes), F32), ((cols + 2 * RIM, lanes), F32), ((lanes, lanes), BF),
            ],
            velocity, lists, wave_codes, wave_weights, scratch=[pltpu.VMEM((rows, cols + 2 * EDGE, lanes), F32)],
        )

    with jax.named_scope("wave"):
        edge = (HX, wc, lanes)
        sides = call(sides_kernel, "sides", [((2, wc, bins), BF)], ob, oa, list_own)[0]
        cells_ends, ends, pa, pb = call(
            wave_ends_kernel, "wave_ends",
            [((2 * HX, wc, bins), BF), ((2 * HX, wc, lanes), BF), (edge, BF), (edge, BF)],
            spectrum, sides, yb, ya, courant, source, land, stokes_kernel,
        )
        pa, pb = exchange("gx", pa, pb)
        cells_rest, rest = call(
            wave_rest_kernel, "wave_rest",
            [((wr - 2 * HX, wc, bins), BF), ((wr - 2 * HX, wc, lanes), BF)],
            spectrum, yb, ya, courant, source, land, stokes_kernel, ends,
        )

    with jax.named_scope("prepare_ends"):
        vel_halo, spin_ends, turn_ends, table_ends, list_rim = call(
            prepare_ends_kernel, "prepare_ends",
            [
                ((2 * HV, *level), F32), ((2 * HL, *level), F32), ((2 * HL + 4, *level), F32),
                ((2 * HL, 3 * wc, lanes), BF), ((groups, 16, lanes), F32),
            ],
            velocity, ob, oa, spin_own, list_own,
            scratch=[pltpu.VMEM((2, 2 * HV - 1, cols + 2 * EDGE, lanes), F32)],
        )

    with jax.named_scope("halo"):
        size = sum(y_rows(rows)) + (list_place(listed - 1, lanes)[0] + 1) * 16
        ya, yb = call(
            halo_kernel, "halo", [((size, lanes), BF)] * 2,
            velocity, vel_halo, ob, oa, lists, ends, rest, pb, pa,
        )
        ya, yb = exchange("gy", ya, yb)

    with jax.named_scope("inner"):
        scratch = [
            pltpu.VMEM((listed, cols + 2 * EDGE, lanes), F32),
            pltpu.VMEM((prow * wc, lanes), BF),
            pltpu.VMEM((prow * wc, lanes), F32),
            pltpu.VMEM((listed, cols, lanes), F32),
            pltpu.SemaphoreType.DMA((3,)),
        ]
        result, new_spectrum, mid_rim, drift_rim, spin_rim, total, prof_rim = call(
            inner_kernel, "inner",
            [
                (velocity.shape, F32),
                (spectrum.shape, BF),
                ((listed, 2, 2 * EDGE, lanes), F32),
                ((listed, 2, EDGE, lanes), F32),
                ((listed, 2, EDGE, lanes), F32),
                ((cols, lanes), F32),
                ((2, 2 * HY * (TALL + 4), lanes), F32),
            ],
            velocity, vel_halo, spin_own, spin_ends, turn_own, turn_ends, table_own, table_ends,
            ends, rest, pb, pa,
            cells_ends, cells_rest, scratch=scratch, any_out=(1,),
        )

    with jax.named_scope("rim"):
        scratch = [
            pltpu.VMEM((2, rows + 2 * HV, 3 * EDGE, lanes), F32),
            pltpu.VMEM((2, listed, 3 * EDGE, lanes), F32),
            pltpu.VMEM((2, 2 * HY * (TALL + 4), lanes), F32),
            pltpu.VMEM((2, listed, EDGE, lanes), F32),
            pltpu.VMEM((2, listed, EDGE, lanes), F32),
            pltpu.VMEM((lanes, lanes), F32),
            pltpu.VMEM((cols + 2 * RIM, lanes), F32),
            pltpu.VMEM((2, rows, EDGE, lanes), F32),
            pltpu.SemaphoreType.DMA((1 + 2 * PARTS,)),
        ]
        new_velocity, current = call(
            rim_kernel, "rim", [(velocity.shape, F32), ((2, wr, wc), F32)],
            velocity, vel_halo, yb, ya, mid_rim, drift_rim, spin_rim, total, list_rim, prof_rim, wave_shares, chosen, spread,
            result, scratch=scratch, any_out=(0,),
        )
    return new_spectrum, new_velocity, current


def solution(mesh):
    return jax.shard_map(
        shards,
        mesh=mesh,
        in_specs=(
            P("gx", "gy", None), P(), P("gx", "gy"), P("gx", "gy"), P(), P("gx", "gy", None),
            P("gx", "gy"), P("gx", "gy", None), P("gx", "gy", None), P("gx", "gy", None), P("gx", "gy", None),
        ),
        out_specs=(P("gx", "gy", None), P("gx", "gy", None), P(None, "gx", "gy")),
        check_vma=False,
    )
```

```python
import jax
import jax.numpy as jnp
from jax import lax
from jax.experimental import pallas as pl
from jax.experimental.pallas import tpu as pltpu
from jax.sharding import PartitionSpec as P

K = 4
RX = 2
RY = 4
STEP = 0.5
PARTS = 4
TALL = 24
RIM = 4
HV, HL = 5, 3
HX, HY = 3, 2
EDGE = 8
BF = jnp.bfloat16
F32 = jnp.float32
ROWS_DOT = (((0,), (0,)), ((), ()))


def partner(i, count, parity):
    return (i ^ 1) if parity == 0 else ((i + 1) ^ 1) - 1


def swap(value, axis, parity):
    nx, ny = lax.axis_size("gx"), lax.axis_size("gy")
    pairs = []
    for x in range(nx):
        for y in range(ny):
            tx, ty = x, y
            if axis == "gx":
                tx = partner(x, nx, parity) % nx
            else:
                ty = partner(y, ny, parity)
                if not 0 <= ty < ny:
                    tx, ty = x ^ 1, y
            pairs.append((x * ny + y, tx * ny + ty))
    return lax.ppermute(value, ("gx", "gy"), pairs)


def exchange(axis, to_a, to_b):
    from_a = swap(to_a, axis, 0)
    from_b = swap(to_b, axis, 1)
    return from_a, from_b


def is_even(axis):
    return lax.axis_index(axis) % 2 == 0


def inside(axis):
    index = lax.axis_index(axis)
    before = jnp.where(index == 0, 0.0, 1.0).astype(F32)
    after = jnp.where(index == lax.axis_size(axis) - 1, 0.0, 1.0).astype(F32)
    return before, after


def pick(cond, one, other):
    return jnp.where(cond, one.astype(F32), other.astype(F32))


def split(value):
    high = value.astype(BF)
    return high, (value - high.astype(F32)).astype(BF)


def split3(value):
    high = value.astype(BF)
    rest = value - high.astype(F32)
    middle = rest.astype(BF)
    return high, middle, (rest - middle.astype(F32)).astype(BF)


def iota(shape, dim):
    return lax.broadcasted_iota(jnp.int32, shape, dim)


def x_rows(cols):
    return (HV - 1) * cols, HL * 16


def edges_kernel(*refs):
    (spec_far, courant_far, source_far, land_far, codes_far, weights_far, coriolis_far, vel_far, basis_far) = refs[:9]
    (wave_codes_far, wave_weights_far) = refs[9:11]
    (oa, ob, ya, yb, lists, spec, courant, source_t, land_t, basis, wave_codes, wave_weights) = refs[11:23]
    (source, land, codes, weights, coriolis, vel, sems) = refs[23:]
    rows, cols, bins = spec.shape
    lanes = vel.shape[-1]
    pairs = [(spec_far, spec)]
    pairs += [(vel_far.at[pl.ds(at, HV)], vel.at[i]) for i, at in ((0, 0), (1, vel_far.shape[0] - HV))]
    pairs += [(codes_far, codes), (weights_far, weights), (coriolis_far, coriolis)]
    pairs += [(courant_far, courant), (source_far, source), (land_far, land), (basis_far, basis)]
    pairs += [(wave_codes_far, wave_codes), (wave_weights_far, wave_weights)]
    copies = [pltpu.make_async_copy(one, two, sems.at[i]) for i, (one, two) in enumerate(pairs)]
    for copy in copies:
        copy.start()
    even_x, even_y = is_even("gx"), is_even("gy")

    def put(at, last, first):
        n = last.shape[0]
        oa[at : at + n] = jnp.where(even_x, last, first).astype(BF)
        ob[at : at + n] = jnp.where(even_x, first, last).astype(BF)

    at, cell = iota((2 * rows, rows * cols), 0), iota((2 * rows, rows * cols), 1)
    wanted = jnp.where(at < rows, at * cols, (at - rows) * cols + cols - 1)
    chosen = (cell == wanted).astype(F32).astype(BF)
    copies[0].wait()
    sides = jnp.dot(chosen, spec[...].reshape(rows * cols, bins), preferred_element_type=F32)
    start = sum(x_rows(codes.shape[2]))
    for i in range(bins // lanes):
        part = slice(i * lanes, (i + 1) * lanes)
        put(start + i * cols, spec[rows - 1, :, part].astype(F32), spec[0, :, part].astype(F32))
    first, last = sides[0:rows], sides[rows:]
    ya[...] = jnp.where(even_y, last, first).astype(BF)
    yb[...] = jnp.where(even_y, first, last).astype(BF)

    for copy in copies[1:]:
        copy.wait()
    source_t[...] = source[...].T
    land_t[...] = land[...].astype(F32).T
    listed, wide = codes.shape[0], codes.shape[2]
    is_u = iota((1, lanes), 1) < lanes // 2
    outer = [
        jnp.where(is_u, pltpu.roll(vel[side, one], lanes // 2, 1), vel[side, two])
        for side, one, two in ((1, 0, 1), (0, HV - 1, HV - 2))
    ]
    put(0, *outer)
    for i in range(1, HV - 1):
        put(i * wide, vel[1, i + 1], vel[0, i - 1])
    for r in range(listed):
        lists[r] = jnp.zeros((16, lanes), F32)
        weight = weights[r]
        turn = coriolis[r : r + 1, :]
        high = turn.astype(BF).astype(F32)
        lists[r, 0:K, 0:wide] = codes[r].astype(F32)
        lists[r, K : 2 * K, 0:wide] = weight / jnp.sum(weight, axis=0, keepdims=True)
        lists[r, 2 * K : 2 * K + 1, 0:wide] = high
        lists[r, 2 * K + 1 : 2 * K + 2, 0:wide] = turn - high
    for i in range(HL):
        put((HV - 1) * wide + i * 16, lists[listed - HL + i], lists[i])


def advance(chosen, spec, sides, ya, yb, courant, source, land, weights, at_once, put):
    rows, cols, _ = spec.shape
    even_y = is_even("gy")
    has_south, has_north = inside("gy")
    south = pick(even_y, yb[...], ya[...]) * has_south
    north = pick(even_y, ya[...], yb[...]) * has_north
    cx, cy = courant[0:1, :], courant[1:2, :]
    ax, ay = jnp.abs(cx), jnp.abs(cy)
    from_west, from_south = cx > 0.0, cy > 0.0
    keep = 1.0 - ax - ay
    sub = iota((cols, 1), 0)
    cells = []
    for x in chosen:
        center = spec[x].astype(F32)
        before = spec[x - 1].astype(F32) if x else sides[0]
        after = spec[x + 1].astype(F32) if x < rows - 1 else sides[1]
        below = jnp.where(sub == 0, south[x : x + 1, :], pltpu.roll(center, 1, 0))
        above = jnp.where(sub == cols - 1, north[x : x + 1, :], pltpu.roll(center, cols - 1, 0))
        advected = (
            keep * center
            + ax * jnp.where(from_west, before, after)
            + ay * jnp.where(from_south, below, above)
        )
        wind = 1.0 + 0.2 * source[:, x : x + 1]
        updated = land[:, x : x + 1] * (advected * (wind - 0.1 * advected))
        cells.append(updated.astype(BF))
        if len(cells) == at_once:
            parts = jnp.dot(jnp.concatenate(cells, axis=0), weights[...], preferred_element_type=F32)
            for i, value in enumerate(cells):
                put(x - at_once + 1 + i, value, parts[i * cols : (i + 1) * cols])
            cells = []


def sides_kernel(xb, xa, after, sides):
    even_x = is_even("gx")
    cols, bins = sides.shape[1], sides.shape[2]
    lanes = xa.shape[1]
    start = xa.shape[0] - cols * bins // lanes
    for i in range(bins // lanes):
        a, b = (ref[start + i * cols : start + (i + 1) * cols, :] for ref in (xa, xb))
        part = slice(i * lanes, (i + 1) * lanes)
        sides[0, :, part], sides[1, :, part] = pick(even_x, b, a).astype(BF), pick(even_x, a, b).astype(BF)


def wave_ends_kernel(spec, sides, ya, yb, courant, source, land, weights, out, profile, pa, pb):
    rows, cols, bins = spec.shape
    even_x = is_even("gx")
    parts = []

    def put(x, value, part):
        i = len(parts)
        out[i], profile[i] = value, part.astype(BF)
        parts.append(part)

    ends = list(range(HX)) + list(range(rows - HX, rows))
    advance(ends, spec, [sides[i].astype(F32) for i in range(2)], ya, yb, courant, source, land, weights, HX, put)
    for i in range(HX):
        first, last = parts[i], parts[HX + i]
        pa[i] = jnp.where(even_x, last, first).astype(BF)
        pb[i] = jnp.where(even_x, first, last).astype(BF)


def wave_rest_kernel(spec, ya, yb, courant, source, land, weights, ends, out, profile):
    rows = spec.shape[0]

    def put(x, value, part):
        out[x - HX], profile[x - HX] = value, part.astype(BF)

    advance(range(HX, rows - HX), spec, None, ya, yb, courant, source, land, weights, (rows - 2 * HX) // 2, put)


def list_place(r, lanes):
    per = lanes // 16
    return r // (4 * per), (r % per) * 16 + RIM * ((r // per) % 4)


def y_rows(rows):
    pairs = (rows + 2 * HV + 1) // 2
    return TALL * HY, (pairs + pairs % 2) * EDGE


def row_of(i, rows, own, ends, reach):
    return own[i] if 0 <= i < rows else ends[i + reach if i < 0 else i - rows + reach]


def pack_rows(vel, vel_halo, ob, oa, lists, ya, yb):
    rows, cols, lanes = vel.shape
    vrow = rows + 2 * HV
    slots = 0
    even_x, even_y = is_even("gx"), is_even("gy")

    def put(at, last, first):
        n = last.shape[0]
        ya[at : at + n] = jnp.where(even_y, last, first).astype(BF)
        yb[at : at + n] = jnp.where(even_y, first, last).astype(BF)

    sub = iota((EDGE, 1), 0)
    is_u = iota((1, lanes), 1) < lanes // 2
    blocks = []
    for r in range(vrow):
        to = RIM * (r % 2)

        def ends_of(ref, k):
            return ref[k, cols - EDGE : cols, :], ref[k, 0:EDGE, :]

        i = r - HV
        if 0 <= i < rows:
            last, first = ends_of(vel, i)
        else:
            last, first = ends_of(vel_halo, r if i < 0 else r - rows)

        def moved(value, one, two):
            return pltpu.roll(value, (two - one) % EDGE, 0) if one != two else value

        one, two = moved(last, EDGE - RIM, to), moved(last, EDGE - RIM - 1, to)
        last = jnp.where(sub == to, jnp.where(is_u, two, pltpu.roll(one, lanes // 2, 1)), one)
        one, two = moved(first, 0, to), moved(first, RIM, to + RIM - 1)
        first = jnp.where(sub == to + RIM - 1, jnp.where(is_u, one, pltpu.roll(two, lanes // 2, 1)), one)
        blocks.append((last, first))
    pairs = [
        [jnp.where(sub < RIM, blocks[r][i], blocks[r + 1][i]) for i in range(2)] for r in range(0, vrow, 2)
    ]
    pairs += [[jnp.zeros((EDGE, lanes), F32)] * 2] * (len(pairs) % 2)
    for i in range(0, len(pairs), 2):
        put(slots + i * EDGE, *[jnp.concatenate([pairs[i][j], pairs[i + 1][j]], axis=0) for j in range(2)])
    start = slots + len(pairs) * EDGE

    group = iota((1, lanes), 1) // RIM
    x_start = (HV - 1) * cols
    tiles = list_place(rows + 2 * HL - 1, lanes)[0] + 1
    acc = [[jnp.zeros((16, lanes), F32)] * 2 for _ in range(tiles)]
    for r in range(rows + 2 * HL):
        if HL <= r < HL + rows:
            own = lists[r - HL]
        else:
            i = r if r < HL else r - HL - rows
            at = x_start + i * 16
            one, two = (ob, oa) if r < HL else (oa, ob)
            own = pick(even_x, one[at : at + 16, :], two[at : at + 16, :])
        tile, to = list_place(r, lanes)
        acc[tile] = [
            jnp.where(group == to // RIM, pltpu.roll(own, (to - where) % lanes, 1), a)
            for a, where in zip(acc[tile], (cols - RIM, 0))
        ]
    for tile in range(tiles):
        put(start + tile * 16, acc[tile][0], acc[tile][1])


def halo_kernel(fixed_a, fixed_b, ends, rest, pb, pa, ya, yb):
    lanes = rest.shape[2]
    even_x, even_y = is_even("gx"), is_even("gy")
    wr, wc = rest.shape[0] + 2 * HX, rest.shape[1]

    def put(at, last, first):
        n = last.shape[0]
        ya[at : at + n] = jnp.where(even_y, last, first).astype(BF)
        yb[at : at + n] = jnp.where(even_y, first, last).astype(BF)

    before, after = pick(even_x, pb[...], pa[...]), pick(even_x, pa[...], pb[...])
    joined = jnp.concatenate([before.astype(BF), ends[0:HX], rest[...], ends[HX:], after.astype(BF)], axis=0)
    count = (wr + 2 * HX) * wc
    slots = TALL * HY
    at, cell = iota((2 * slots, count), 0), iota((2 * slots, count), 1)
    side, rest = at // slots, at % slots
    column = rest // TALL + jnp.where(side == 0, wc - HY, 0)
    row = rest % TALL
    chosen = ((row < wr + 2 * HX) & (cell == row * wc + column)).astype(F32).astype(BF)
    sides = jnp.dot(chosen, joined.reshape(count, lanes), preferred_element_type=F32)
    put(0, sides[0:slots], sides[slots:])
    ya[slots:], yb[slots:] = fixed_a[...], fixed_b[...]


def vorticity(ref, r, base, count):
    half = ref.shape[-1] // 2
    is_u = iota((1, 2 * half), 1) < half

    def at(dx, dy):
        return ref[r + dx, base + dy : base + dy + count, :]

    near = jnp.where(is_u, at(0, -1), at(1, 0)) - jnp.where(is_u, at(0, 1), at(-1, 0))
    far = jnp.where(is_u, at(0, -2), at(2, 0)) - jnp.where(is_u, at(0, 2), at(-2, 0))
    part = (8.0 / 12.0) * near - (1.0 / 12.0) * far
    return part + pltpu.roll(part, half, 1)


def averager(lanes):
    at = iota((2 * lanes, lanes), 0)
    to = iota((2 * lanes, lanes), 1)
    half = lanes // 2
    return jnp.where((at % lanes) // half == to % 2, 1.0 / half, 0.0).astype(BF)


def turned(value):
    half = value.shape[-1] // 2
    sign = jnp.where(iota((1, 2 * half), 1) < half, 1.0, -1.0)
    return pltpu.roll(value, half, 1) * sign


def one_hot(full, cols):
    lanes = full.shape[1]
    wave_cols = cols // RY
    codes = full[0:EDGE]
    third = jnp.where(codes >= 6.0, 2.0, jnp.where(codes >= 3.0, 1.0, 0.0))
    slot = third * (wave_cols - 3.0) + codes + (iota((1, lanes), 1) // RY).astype(F32) - 1.0
    place = iota((3 * wave_cols, lanes), 0).astype(F32)
    hot = jnp.where(place == slot[0:1], full[K : K + 1], 0.0)
    for k in range(1, K):
        hot = hot + jnp.where(place == slot[k : k + 1], full[K + k : K + k + 1], 0.0)
    return hot.astype(BF)


def rim_lists(full, rim, r, cols):
    lanes = full.shape[1]
    lane = iota((1, lanes), 1)
    to = (r % (lanes // 16)) * 16
    rim = jnp.where(lane // RIM == to // RIM + 1, pltpu.roll(full, (to + RIM) % lanes, 1), rim)
    return jnp.where(lane // RIM == to // RIM + 2, pltpu.roll(full, (to + 3 * RIM - cols) % lanes, 1), rim)


def prepare_own_kernel(
    own, lists, codes, weights, spin, turn, table, list_rim, wave_shares, chosen, spread, vel
):
    rows, cols, lanes = own.shape
    per = lanes // 16
    blank = jnp.zeros((EDGE, lanes), F32)

    def fill(i, _):
        vel[i, 0:EDGE, :] = blank
        vel[i, EDGE + cols :, :] = blank
        vel[i, EDGE : EDGE + cols, :] = own[i]
        return 0

    lax.fori_loop(0, rows, fill, 0, unroll=8)
    rim = [jnp.zeros((16, lanes), F32)] * list_rim.shape[0]
    for i in range(rows):
        g = (i + HL) // per
        full = lists[i]
        table[i], rim[g] = one_hot(full, cols), rim_lists(full, rim[g], i + HL, cols)
    for g, value in enumerate(rim):
        list_rim[g] = value

    ones = jnp.ones((8, lanes), BF)

    def widened(i):
        return lax.dot_general(lists[i, 2 * K :, :].astype(BF), ones, ROWS_DOT, preferred_element_type=F32)[0:cols]

    for i in (0, 1, rows - 2, rows - 1):
        spin[i] = widened(i)
    half = (rows - 4) // 2

    def absolute(m, _):
        for u in range(half):
            i = m * half + u + 2
            wide = widened(i)
            spin[i] = wide
            turn[i - 2] = wide + vorticity(vel, i, EDGE, cols)
        return 0

    lax.fori_loop(0, 2, absolute, 0)

    wc = cols // RY
    lane = iota((1, lanes), 1)
    at, to = iota(chosen.shape, 0), iota(chosen.shape, 1)
    reach = (RY + 2) * wc
    chosen[...] = ((to < reach) & (at == RY * (to % wc) + to // wc + RIM - 1)).astype(F32)
    at, to = iota((lanes, lanes), 0), iota((lanes, lanes), 1)
    spread[...] = ((at < reach) & (at % wc == to)).astype(F32).astype(BF)

    at, to = iota((wc, lanes), 0), iota((wc, lanes), 1)
    repeat = ((to < reach) & (to % wc == at)).astype(F32).astype(BF)
    shift = (lane // wc).astype(F32)
    weight = [weights[:, k, :] for k in range(K)]
    whole = sum(weight[1:], weight[0])
    code = [jnp.dot(codes[:, k, :].astype(F32).astype(BF), repeat, preferred_element_type=F32) for k in range(K)]
    share = [
        sum(jnp.dot(p, repeat, preferred_element_type=F32) for p in split3(weight[k] / whole)) for k in range(K)
    ]
    for near in range(RX + 2):
        wave_shares[near] = sum(
            jnp.where(code[k] == near * (RY + 2.0) + shift, share[k], 0.0) for k in range(K)
        )


def prepare_ends_kernel(
    own, ob, oa, lists, spin_own, list_own, vel_halo, spin, turn, table, list_rim, fixed_a, fixed_b, vel
):
    rows, cols, lanes = own.shape
    per = lanes // 16
    even_x = is_even("gx")
    blank = jnp.zeros((EDGE, lanes), F32)
    list_rim[...] = list_own[...]
    ones = jnp.ones((8, lanes), BF)
    for side in range(2):
        one, two = (oa, ob) if side else (ob, oa)

        def from_x(start, n):
            return pick(even_x, one[start : start + n, :], two[start : start + n, :])

        parts = [from_x(i * cols, cols) for i in range(HV - 1)]
        outer = pltpu.roll(parts[0], lanes // 2, 1)
        parts = parts[1:] + [parts[0], outer] if side else [outer] + parts
        for k in range(HV):
            vel_halo[side * HV + k] = parts[k]
        near = [own[i] for i in (range(rows - HV + 1, rows) if side else range(HV - 1))]
        for k, value in enumerate(near + parts if side else parts + near):
            vel[side, k, 0:EDGE, :] = blank
            vel[side, k, EDGE + cols :, :] = blank
            vel[side, k, EDGE : EDGE + cols, :] = value
        for k in range(HL):
            at = side * HL + k
            r = k + side * (rows + HL)
            full = from_x((HV - 1) * cols + k * 16, 16)
            table[at], list_rim[r // per] = one_hot(full, cols), rim_lists(full, list_rim[r // per], r, cols)
            spin[at] = lax.dot_general(full[2 * K :].astype(BF), ones, ROWS_DOT, preferred_element_type=F32)[0:cols]
        for k in range(HL + 2):
            i = k + (rows - 2 if side else -HL)
            turn[side * (HL + 2) + k] = row_of(i, rows, spin_own, spin, HL) + vorticity(vel.at[side], k + 2, EDGE, cols)
    pack_rows(own, vel_halo, ob, oa, lists, fixed_a, fixed_b)


def inner_kernel(
    vel, vel_halo, spin_own, spin_ends, turn_own, turn_ends, table_own, table_ends,
    ends, rest, pb, pa, cells_ends, cells_rest,
    out, cells_far, mid_rim, drift_rim, spin_rim, total, prof_rim,
    mid, names, prof, drift, sems,
):
    rows, cols, lanes = out.shape
    copies = []
    wr, wc = rest.shape[0] + 2 * HX, rest.shape[1]
    for part, to in (
        (cells_ends.at[pl.ds(0, HX)], cells_far.at[pl.ds(0, HX)]),
        (cells_rest, cells_far.at[pl.ds(HX, wr - 2 * HX)]),
        (cells_ends.at[pl.ds(HX, HX)], cells_far.at[pl.ds(wr - HX, HX)]),
    ):
        copies.append(pltpu.make_async_copy(part, to, sems.at[len(copies)]))
    for copy in copies:
        copy.start()
    listed = rows + 2 * HL
    prow = wr + 2 * HX
    even_x = is_even("gx")
    lane = iota((1, lanes), 1)
    blank = jnp.zeros((EDGE, lanes), F32)
    for x in range(prow):
        if HX <= x < HX + wr:
            i = x - HX
            own = ends[i] if i < HX else rest[i - HX] if i < wr - HX else ends[i - wr + 2 * HX]
            part = own.astype(F32)
        elif x < HX:
            part = pick(even_x, pb[x], pa[x])
        else:
            part = pick(even_x, pa[x - HX - wr], pb[x - HX - wr])
        part = turned(part)
        prof[x * wc : (x + 1) * wc, :] = part
        names[x * wc : (x + 1) * wc, :] = part.astype(BF)
    prof_rim[...] = jnp.zeros(prof_rim.shape, F32)
    for c in range(HY):
        prof_rim[0, pl.ds(HY + c, prow, stride=2 * HY), :] = prof[pl.ds(c, prow, stride=wc), :]
        prof_rim[1, pl.ds(c, prow, stride=2 * HY), :] = prof[pl.ds(wc - HY + c, prow, stride=wc), :]

    block = 3 * wc

    def first(r, vel_ref, table_ref, turn_ref, spin_ref, vk, tk, uk):
        named = names[pl.ds(pl.multiple_of((r + 1) // 2 * wc, wc), block), :]
        stokes = lax.dot_general(table_ref[tk], named, ROWS_DOT, preferred_element_type=F32)[0:cols]
        drift[r] = stokes
        new = vel_ref[vk] + STEP * (turn_ref[uk] * stokes)
        mid[r, 0:EDGE, :] = blank
        mid[r, EDGE + cols :, :] = blank
        mid[r, EDGE : EDGE + cols, :] = new
        mid_rim[r, 0] = new[0 : 2 * EDGE]
        mid_rim[r, 1] = new[cols - 2 * EDGE :]
        for where in range(2):
            begin = RIM if where == 0 else cols - RIM - EDGE
            drift_rim[r, where] = drift[r, begin : begin + EDGE, :]
            spin_rim[r, where] = spin_ref[tk, begin : begin + EDGE, :]

    for i in [*range(-HL, 2), *range(rows - 2, rows + HL)]:
        end = i + HL if i < 2 else i - rows + HL + 4
        if 0 <= i < rows:
            first(i + HL, vel, table_own, turn_ends, spin_own, i, i, end)
        else:
            far = 0 if i < 0 else rows
            first(i + HL, vel_halo, table_ends, turn_ends, spin_ends, i - far + HV, i - far + HL, end)
    unroll = (rows - 4) // 2

    def first_step(m, _):
        for u in range(unroll):
            i = m * unroll + u + 2
            first(i + HL, vel, table_own, turn_own, spin_own, i, i, i - 2)
        return 0

    lax.fori_loop(0, 2, first_step, 0)

    average = averager(lanes)
    means = jnp.zeros((cols, lanes), F32)
    for n in range(rows + 2):
        r = n + HL - 1
        absolute = row_of(n - 1, rows, spin_own, spin_ends, HL) + vorticity(mid, r, EDGE, cols)
        old = row_of(n - 1, rows, vel, vel_halo, HV) + mid[r, EDGE : EDGE + cols, :]
        new = 0.5 * old + (0.5 * STEP) * (absolute * drift[r])
        sums = jnp.dot(jnp.concatenate(split(new), axis=1), average, preferred_element_type=F32)
        means = jnp.where(lane // 2 == n, sums, means)
        if 1 <= n <= rows:
            out[n - 1] = new
    total[...] = means

    for copy in copies:
        copy.wait()


def rim_kernel(
    own, vel_halo, ya, yb, mid_rim, drift_rim, spin_rim, total, list_rim, prof_rim, wave_shares, chosen, spread, inner,
    out, current,
    vel, mid, prof, drift, spin, picked, means, strips, sems,
):
    rows, cols, lanes = own.shape
    vrow = rows + 2 * HV
    wr, wc = current.shape[1], current.shape[2]
    listed = rows + 2 * HL
    prow = wr + 2 * HX
    even_y = is_even("gy")
    has_south, has_north = inside("gy")
    lane = iota((1, lanes), 1)
    sub = iota((EDGE, 1), 0)
    slots, vel_rows = y_rows(rows)

    def from_y(start, n):
        a, b = ya[start : start + n, :], yb[start : start + n, :]
        return pick(even_y, b, a) * has_south, pick(even_y, a, b) * has_north

    middle = pl.ds(EDGE, cols - 2 * EDGE)
    copies = [pltpu.make_async_copy(inner.at[:, middle, :], out.at[:, middle, :], sems.at[0])]
    copies[0].start()

    blank = jnp.zeros((EDGE, lanes), F32)
    for r in range(vrow):
        vel[0, r, 0:EDGE, :] = blank
        vel[1, r, 2 * EDGE :, :] = blank
        ref, k = (own, r - HV) if HV <= r < HV + rows else (vel_halo, r if r < HV else r - rows)
        vel[0, r, EDGE:, :] = ref[k, 0 : 2 * EDGE, :]
        vel[1, r, 0 : 2 * EDGE, :] = ref[k, cols - 2 * EDGE : cols, :]
    for start in range(0, vel_rows, 2 * EDGE):
        pieces = from_y(slots + start, 2 * EDGE)
        for i in range(2):
            low, high = (p[i * EDGE : i * EDGE + EDGE] for p in pieces)
            low_moved, high_moved = pltpu.roll(low, lanes // 2, 1), pltpu.roll(high, lanes // 2, 1)
            low_in = jnp.where(sub % RIM == 0, low_moved, low)
            for j in range(2):
                r = (start + i * EDGE) // RIM + j
                if r < vrow:
                    at = j * RIM
                    vel[0, r, EDGE - RIM : EDGE, :] = low_in[at : at + RIM]
                    vel[0, r, EDGE - RIM - 1 : EDGE - RIM, :] = low[at : at + 1]
                    vel[1, r, 2 * EDGE : 2 * EDGE + RIM, :] = high[at : at + RIM]
                    vel[1, r, 2 * EDGE + RIM : 2 * EDGE + RIM + 1, :] = high_moved[at + RIM - 1 : at + RIM]

    prof[...] = prof_rim[...]
    south, north = from_y(0, slots)
    south, north = turned(south), turned(north)
    for c in range(HY):
        prof[0, pl.ds(c, TALL, stride=2 * HY), :] = south[TALL * c : TALL * (c + 1)]
        prof[1, pl.ds(HY + c, TALL, stride=2 * HY), :] = north[TALL * c : TALL * (c + 1)]

    per = lanes // 16
    start = slots + vel_rows
    span = 2 * per * HY
    place = iota((2 * span, lanes), 0).astype(F32)
    part = lane % 16
    offset = (part // EDGE) * span + ((lane // 16 + 1) // 2) * (2 * HY) + (part % EDGE) // RIM
    sub16 = iota((16, 1), 0)
    ones = jnp.ones((8, lanes), F32)
    none = jnp.zeros((2 * span, lanes), F32)
    for g in range(-(-listed // per)):
        tile, to = list_place(g * per, lanes)
        south, north = from_y(start + tile * 16, 16)
        full = list_rim[g]
        full = jnp.where(part // RIM == 0, pltpu.roll(south, (-to) % lanes, 1), full)
        full = jnp.where(part // RIM == 3, pltpu.roll(north, (3 * RIM - to) % lanes, 1), full)
        third = jnp.where(full >= 6.0, 2.0, jnp.where(full >= 3.0, 1.0, 0.0))
        full = jnp.where(sub16 < K, third + full + offset.astype(F32), full)
        hot = jnp.zeros((2 * span, lanes), F32)
        for k in range(K):
            hot = hot + jnp.where(place == full[k : k + 1], full[K + k : K + k + 1], 0.0)
        left = jnp.concatenate([hot, full[2 * K :], blank], axis=0).astype(BF)
        begin = g * (per // 2) * 2 * HY
        named = jnp.concatenate([prof[0, begin : begin + span, :], prof[1, begin : begin + span, :]], axis=0)
        right = jnp.concatenate([
            jnp.concatenate([named, blank, blank], axis=0),
            jnp.concatenate([none, ones, blank], axis=0),
        ], axis=1).astype(BF)
        both = lax.dot_general(left, right, ROWS_DOT, preferred_element_type=F32)
        for i in range(min(per, listed - g * per)):
            for side in range(2):
                at = i * 16 + side * EDGE
                drift[side, g * per + i] = both[at : at + EDGE, 0:lanes]
                spin[side, g * per + i] = both[at : at + EDGE, lanes:]

    lift = HV - HL
    for r in range(listed):
        for side in range(2):
            base = RIM + side * EDGE
            mid[side, r, 2 * EDGE * side : 2 * EDGE * side + EDGE, :] = blank
            mid[side, r, EDGE - side * EDGE : 3 * EDGE - side * EDGE, :] = mid_rim[r, side]
            absolute = spin[side, r] + vorticity(vel.at[side], r + lift, base, EDGE)
            new = vel[side, r + lift, base : base + EDGE, :] + STEP * (absolute * drift[side, r])
            mid[side, r, base : base + EDGE, :] = new

    average = averager(lanes)
    acc = jnp.zeros((2 * EDGE, lanes), F32)
    step = rows // PARTS
    begins = (EDGE - 1, EDGE + 1)
    for n in range(rows + 2):
        r = n + HL - 1
        both = []
        for side, begin in enumerate(begins):
            order = 1 - 2 * side

            def joined(here, there):
                return jnp.concatenate([here, there][::order], axis=0)[begin - RIM : begin - RIM + EDGE]

            absolute = joined(spin[side, r], spin_rim[r, side]) + vorticity(mid.at[side], r, begin, EDGE)
            old = vel[side, r + lift, begin : begin + EDGE, :] + mid[side, r, begin : begin + EDGE, :]
            new = 0.5 * old + (0.5 * STEP) * (absolute * joined(drift[side, r], drift_rim[r, side]))
            both.append(new)
            if 1 <= n <= rows:
                kept = inner[n - 1, side * (cols - EDGE) : side * (cols - EDGE) + EDGE, :]
                moved = pltpu.roll(new, EDGE - 1 if side == 0 else 1, 0)
                strips[side, n - 1] = jnp.where(sub == (EDGE - 1 if side == 0 else 0), kept, moved)
        sums = jnp.dot(
            jnp.concatenate(split(jnp.concatenate(both, axis=0)), axis=1), average, preferred_element_type=F32
        )
        acc = jnp.where(lane // 2 == n, sums, acc)
        if n and n % step == 0:
            part = pl.ds(n - step, step)
            for side, at in ((0, 0), (1, cols - EDGE)):
                one, two = strips.at[side, part], out.at[part, pl.ds(at, EDGE), :]
                copies.append(pltpu.make_async_copy(one, two, sems.at[len(copies)]))
                copies[-1].start()
    count = cols + 2 * RIM
    means[0:EDGE] = blank
    means[count - EDGE :] = blank
    means[RIM - 1 : RIM - 1 + EDGE] = acc[0:EDGE]
    means[RIM - 1 + EDGE : count - RIM + 1 - EDGE] = total[EDGE - 1 : cols - EDGE + 1, :]
    means[count - RIM + 1 - EDGE : count - RIM + 1] = acc[EDGE:]

    named = chosen[...].astype(BF)
    picked[...] = sum(
        lax.dot_general(p, named, ROWS_DOT, preferred_element_type=F32) for p in split3(means[...])
    )
    summed = [
        sum(wave_shares[near] * picked[pl.ds(2 * near + c, wr, stride=2 * RX), :] for near in range(RX + 2))
        for c in range(2)
    ]
    sums = sum(
        jnp.dot(p, spread[...], preferred_element_type=F32) for p in split3(jnp.concatenate(summed, axis=0))
    )
    current[0] = sums[0:wr, 0:wc]
    current[1] = sums[wr:, 0:wc]
    for copy in copies:
        copy.wait()


VMEM = pl.BlockSpec(memory_space=pltpu.VMEM)
ANY = pl.BlockSpec(memory_space=pltpu.HBM)


def call(kernel, name, outs, *args, scratch=(), any_in=(), any_out=()):
    args = [pltpu.with_memory_space_constraint(v, pltpu.HBM) if i in any_in else v for i, v in enumerate(args)]
    return pl.pallas_call(
        kernel,
        out_shape=tuple(jax.ShapeDtypeStruct(shape, dtype) for shape, dtype in outs),
        in_specs=[ANY if i in any_in else VMEM for i in range(len(args))],
        out_specs=tuple(ANY if i in any_out else VMEM for i in range(len(outs))),
        scratch_shapes=list(scratch),
        compiler_params=pltpu.CompilerParams(vmem_limit_bytes=14 << 20),
        name=name,
    )(*args)


def shards(
    spectrum, courant, source, wave_land, stokes_kernel, velocity, coriolis,
    ocean_codes, ocean_weights, wave_codes, wave_weights,
):
    wr, wc, bins = spectrum.shape
    rows, cols, lanes = velocity.shape
    listed = rows + 2 * HL
    prow = wr + 2 * HX

    with jax.named_scope("spectrum_edges"):
        codes, weights = jnp.transpose(ocean_codes, (0, 2, 1)), jnp.transpose(ocean_weights, (0, 2, 1))
        size = sum(x_rows(cols)) + wc * bins // lanes
        outs = [((size, lanes), BF)] * 2 + [((wr, bins), BF)] * 2 + [((rows, 16, lanes), F32)]
        outs += [(spectrum.shape, BF), (courant.shape, F32), ((wc, wr), F32), ((wc, wr), F32), (stokes_kernel.shape, BF)]
        outs += [((wr, K, wc), wave_codes.dtype), ((wr, K, wc), F32)]
        oa, ob, ya, yb, lists, spectrum, courant, source, land, stokes_kernel, wave_codes, wave_weights = call(
            edges_kernel, "edges", outs,
            spectrum, courant, source, wave_land, codes, weights, coriolis, velocity, stokes_kernel,
            jnp.transpose(wave_codes, (0, 2, 1)), jnp.transpose(wave_weights, (0, 2, 1)), any_in=range(11),
            scratch=[
                pltpu.VMEM(source.shape, F32),
                pltpu.VMEM(wave_land.shape, wave_land.dtype),
                pltpu.VMEM(codes.shape, codes.dtype),
                pltpu.VMEM(weights.shape, F32),
                pltpu.VMEM(coriolis.shape, F32),
                pltpu.VMEM((2, HV, cols, lanes), F32),
                pltpu.SemaphoreType.DMA((12,)),
            ],
        )
        oa, ob = exchange("gx", oa, ob)
        ya, yb = exchange("gy", ya, yb)

    with jax.named_scope("prepare_own"):
        groups = -(-listed // (lanes // 16))
        level = (cols, lanes)
        spin_own, turn_own, table_own, list_own, wave_shares, chosen, spread = call(
            prepare_own_kernel, "prepare_own",
            [
                ((rows, *level), F32), ((rows - 4, *level), F32), ((rows, 3 * wc, lanes), BF), ((groups, 16, lanes), F32),
                ((RX + 2, wr, lanes), F32), ((cols + 2 * RIM, lanes), F32), ((lanes, lanes), BF),
            ],
            velocity, lists, wave_codes, wave_weights, scratch=[pltpu.VMEM((rows, cols + 2 * EDGE, lanes), F32)],
        )

    with jax.named_scope("wave"):
        edge = (HX, wc, lanes)
        sides = call(sides_kernel, "sides", [((2, wc, bins), BF)], ob, oa, list_own)[0]
        cells_ends, ends, pa, pb = call(
            wave_ends_kernel, "wave_ends",
            [((2 * HX, wc, bins), BF), ((2 * HX, wc, lanes), BF), (edge, BF), (edge, BF)],
            spectrum, sides, ya, yb, courant, source, land, stokes_kernel,
        )
        pa, pb = exchange("gx", pa, pb)
        cells_rest, rest = call(
            wave_rest_kernel, "wave_rest",
            [((wr - 2 * HX, wc, bins), BF), ((wr - 2 * HX, wc, lanes), BF)],
            spectrum, ya, yb, courant, source, land, stokes_kernel, ends,
        )

    with jax.named_scope("prepare_ends"):
        size = y_rows(rows)[1] + (list_place(listed - 1, lanes)[0] + 1) * 16
        vel_halo, spin_ends, turn_ends, table_ends, list_rim, fixed_a, fixed_b = call(
            prepare_ends_kernel, "prepare_ends",
            [
                ((2 * HV, *level), F32), ((2 * HL, *level), F32), ((2 * HL + 4, *level), F32),
                ((2 * HL, 3 * wc, lanes), BF), ((groups, 16, lanes), F32),
                ((size, lanes), BF), ((size, lanes), BF),
            ],
            velocity, ob, oa, lists, spin_own, list_own,
            scratch=[pltpu.VMEM((2, 2 * HV - 1, cols + 2 * EDGE, lanes), F32)],
        )

    with jax.named_scope("halo"):
        size += y_rows(rows)[0]
        ya, yb = call(
            halo_kernel, "halo", [((size, lanes), BF)] * 2, fixed_a, fixed_b, ends, rest, pb, pa
        )
        ya, yb = exchange("gy", ya, yb)

    with jax.named_scope("inner"):
        scratch = [
            pltpu.VMEM((listed, cols + 2 * EDGE, lanes), F32),
            pltpu.VMEM((prow * wc, lanes), BF),
            pltpu.VMEM((prow * wc, lanes), F32),
            pltpu.VMEM((listed, cols, lanes), F32),
            pltpu.SemaphoreType.DMA((3,)),
        ]
        result, new_spectrum, mid_rim, drift_rim, spin_rim, total, prof_rim = call(
            inner_kernel, "inner",
            [
                (velocity.shape, F32),
                (spectrum.shape, BF),
                ((listed, 2, 2 * EDGE, lanes), F32),
                ((listed, 2, EDGE, lanes), F32),
                ((listed, 2, EDGE, lanes), F32),
                ((cols, lanes), F32),
                ((2, 2 * HY * (TALL + 4), lanes), F32),
            ],
            velocity, vel_halo, spin_own, spin_ends, turn_own, turn_ends, table_own, table_ends,
            ends, rest, pb, pa,
            cells_ends, cells_rest, scratch=scratch, any_out=(1,),
        )

    with jax.named_scope("rim"):
        scratch = [
            pltpu.VMEM((2, rows + 2 * HV, 3 * EDGE, lanes), F32),
            pltpu.VMEM((2, listed, 3 * EDGE, lanes), F32),
            pltpu.VMEM((2, 2 * HY * (TALL + 4), lanes), F32),
            pltpu.VMEM((2, listed, EDGE, lanes), F32),
            pltpu.VMEM((2, listed, EDGE, lanes), F32),
            pltpu.VMEM((lanes, lanes), F32),
            pltpu.VMEM((cols + 2 * RIM, lanes), F32),
            pltpu.VMEM((2, rows, EDGE, lanes), F32),
            pltpu.SemaphoreType.DMA((1 + 2 * PARTS,)),
        ]
        new_velocity, current = call(
            rim_kernel, "rim", [(velocity.shape, F32), ((2, wr, wc), F32)],
            velocity, vel_halo, ya, yb, mid_rim, drift_rim, spin_rim, total, list_rim, prof_rim, wave_shares, chosen, spread,
            result, scratch=scratch, any_out=(0,),
        )
    return new_spectrum, new_velocity, current


def solution(mesh):
    return jax.shard_map(
        shards,
        mesh=mesh,
        in_specs=(
            P("gx", "gy", None), P(), P("gx", "gy"), P("gx", "gy"), P(), P("gx", "gy", None),
            P("gx", "gy"), P("gx", "gy", None), P("gx", "gy", None), P("gx", "gy", None), P("gx", "gy", None),
        ),
        out_specs=(P("gx", "gy", None), P("gx", "gy", None), P(None, "gx", "gy")),
        check_vma=False,
    )
```

```python
import jax
import jax.numpy as jnp
from jax import lax
from jax.experimental import pallas as pl
from jax.experimental.pallas import tpu as pltpu
from jax.sharding import PartitionSpec as P

K = 4
RX = 2
RY = 4
STEP = 0.5
PARTS = 4
TALL = 24
RIM = 4
HV, HL = 5, 3
HX, HY = 3, 2
EDGE = 8
BF = jnp.bfloat16
F32 = jnp.float32
ROWS_DOT = (((0,), (0,)), ((), ()))


def partner(i, count, parity):
    return (i ^ 1) if parity == 0 else ((i + 1) ^ 1) - 1


def swap(value, axis, parity):
    nx, ny = lax.axis_size("gx"), lax.axis_size("gy")
    pairs = []
    for x in range(nx):
        for y in range(ny):
            tx, ty = x, y
            if axis == "gx":
                tx = partner(x, nx, parity) % nx
            else:
                ty = partner(y, ny, parity)
                if not 0 <= ty < ny:
                    tx, ty = x ^ 1, y
            pairs.append((x * ny + y, tx * ny + ty))
    return lax.ppermute(value, ("gx", "gy"), pairs)


def exchange(axis, to_a, to_b):
    from_a = swap(to_a, axis, 0)
    from_b = swap(to_b, axis, 1)
    return from_a, from_b


def is_even(axis):
    return lax.axis_index(axis) % 2 == 0


def inside(axis):
    index = lax.axis_index(axis)
    before = jnp.where(index == 0, 0.0, 1.0).astype(F32)
    after = jnp.where(index == lax.axis_size(axis) - 1, 0.0, 1.0).astype(F32)
    return before, after


def pick(cond, one, other):
    return jnp.where(cond, one.astype(F32), other.astype(F32))


def split(value):
    high = value.astype(BF)
    return high, (value - high.astype(F32)).astype(BF)


def split3(value):
    high = value.astype(BF)
    rest = value - high.astype(F32)
    middle = rest.astype(BF)
    return high, middle, (rest - middle.astype(F32)).astype(BF)


def iota(shape, dim):
    return lax.broadcasted_iota(jnp.int32, shape, dim)


def x_rows(cols):
    return (HV - 1) * cols, HL * 16


def edges_kernel(*refs):
    (spec_far, courant_far, source_far, land_far, codes_far, weights_far, coriolis_far, vel_far) = refs[:8]
    (oa, ob, ya, yb, lists, spec, courant, source_t, land_t) = refs[8:17]
    (source, land, codes, weights, coriolis, vel, sems) = refs[17:]
    rows, cols, bins = spec.shape
    lanes = vel.shape[-1]
    pairs = [(spec_far, spec)]
    pairs += [(vel_far.at[pl.ds(at, HV)], vel.at[i]) for i, at in ((0, 0), (1, vel_far.shape[0] - HV))]
    pairs += [(codes_far, codes), (weights_far, weights), (coriolis_far, coriolis)]
    pairs += [(courant_far, courant), (source_far, source), (land_far, land)]
    copies = [pltpu.make_async_copy(one, two, sems.at[i]) for i, (one, two) in enumerate(pairs)]
    for copy in copies:
        copy.start()
    even_x, even_y = is_even("gx"), is_even("gy")

    def put(at, last, first):
        n = last.shape[0]
        oa[at : at + n] = jnp.where(even_x, last, first).astype(BF)
        ob[at : at + n] = jnp.where(even_x, first, last).astype(BF)

    at, cell = iota((2 * rows, rows * cols), 0), iota((2 * rows, rows * cols), 1)
    wanted = jnp.where(at < rows, at * cols, (at - rows) * cols + cols - 1)
    chosen = (cell == wanted).astype(F32).astype(BF)
    copies[0].wait()
    sides = jnp.dot(chosen, spec[...].reshape(rows * cols, bins), preferred_element_type=F32)
    start = sum(x_rows(codes.shape[2]))
    for i in range(bins // lanes):
        part = slice(i * lanes, (i + 1) * lanes)
        put(start + i * cols, spec[rows - 1, :, part].astype(F32), spec[0, :, part].astype(F32))
    first, last = sides[0:rows], sides[rows:]
    ya[...] = jnp.where(even_y, last, first).astype(BF)
    yb[...] = jnp.where(even_y, first, last).astype(BF)

    for copy in copies[1:]:
        copy.wait()
    source_t[...] = source[...].T
    land_t[...] = land[...].astype(F32).T
    listed, wide = codes.shape[0], codes.shape[2]
    is_u = iota((1, lanes), 1) < lanes // 2
    outer = [
        jnp.where(is_u, pltpu.roll(vel[side, one], lanes // 2, 1), vel[side, two])
        for side, one, two in ((1, 0, 1), (0, HV - 1, HV - 2))
    ]
    put(0, *outer)
    for i in range(1, HV - 1):
        put(i * wide, vel[1, i + 1], vel[0, i - 1])
    for r in range(listed):
        lists[r] = jnp.zeros((16, lanes), F32)
        weight = weights[r]
        turn = coriolis[r : r + 1, :]
        high = turn.astype(BF).astype(F32)
        lists[r, 0:K, 0:wide] = codes[r].astype(F32)
        lists[r, K : 2 * K, 0:wide] = weight / jnp.sum(weight, axis=0, keepdims=True)
        lists[r, 2 * K : 2 * K + 1, 0:wide] = high
        lists[r, 2 * K + 1 : 2 * K + 2, 0:wide] = turn - high
    for i in range(HL):
        put((HV - 1) * wide + i * 16, lists[listed - HL + i], lists[i])


def advance(chosen, spec, sides, ya, yb, courant, source, land, weights, at_once, put):
    rows, cols, _ = spec.shape
    even_y = is_even("gy")
    has_south, has_north = inside("gy")
    south = pick(even_y, yb[...], ya[...]) * has_south
    north = pick(even_y, ya[...], yb[...]) * has_north
    cx, cy = courant[0:1, :], courant[1:2, :]
    ax, ay = jnp.abs(cx), jnp.abs(cy)
    from_west, from_south = cx > 0.0, cy > 0.0
    keep = 1.0 - ax - ay
    sub = iota((cols, 1), 0)
    cells = []
    for x in chosen:
        center = spec[x].astype(F32)
        before = spec[x - 1].astype(F32) if x else sides[0]
        after = spec[x + 1].astype(F32) if x < rows - 1 else sides[1]
        below = jnp.where(sub == 0, south[x : x + 1, :], pltpu.roll(center, 1, 0))
        above = jnp.where(sub == cols - 1, north[x : x + 1, :], pltpu.roll(center, cols - 1, 0))
        advected = (
            keep * center
            + ax * jnp.where(from_west, before, after)
            + ay * jnp.where(from_south, below, above)
        )
        wind = 1.0 + 0.2 * source[:, x : x + 1]
        updated = land[:, x : x + 1] * (advected * (wind - 0.1 * advected))
        cells.append(updated.astype(BF))
        if len(cells) == at_once:
            parts = jnp.dot(jnp.concatenate(cells, axis=0), weights[...], preferred_element_type=F32)
            for i, value in enumerate(cells):
                put(x - at_once + 1 + i, value, parts[i * cols : (i + 1) * cols])
            cells = []


def sides_kernel(xb, xa, after, sides):
    even_x = is_even("gx")
    cols, bins = sides.shape[1], sides.shape[2]
    lanes = xa.shape[1]
    start = xa.shape[0] - cols * bins // lanes
    for i in range(bins // lanes):
        a, b = (ref[start + i * cols : start + (i + 1) * cols, :] for ref in (xa, xb))
        part = slice(i * lanes, (i + 1) * lanes)
        sides[0, :, part], sides[1, :, part] = pick(even_x, b, a).astype(BF), pick(even_x, a, b).astype(BF)


def wave_ends_kernel(spec, sides, ya, yb, courant, source, land, weights, out, profile, pa, pb):
    rows, cols, bins = spec.shape
    even_x = is_even("gx")
    parts = []

    def put(x, value, part):
        i = len(parts)
        out[i], profile[i] = value, part.astype(BF)
        parts.append(part)

    ends = list(range(HX)) + list(range(rows - HX, rows))
    advance(ends, spec, [sides[i].astype(F32) for i in range(2)], ya, yb, courant, source, land, weights, HX, put)
    for i in range(HX):
        first, last = parts[i], parts[HX + i]
        pa[i] = jnp.where(even_x, last, first).astype(BF)
        pb[i] = jnp.where(even_x, first, last).astype(BF)


def wave_rest_kernel(spec, ya, yb, courant, source, land, weights, ends, out, profile):
    rows = spec.shape[0]

    def put(x, value, part):
        out[x - HX], profile[x - HX] = value, part.astype(BF)

    advance(range(HX, rows - HX), spec, None, ya, yb, courant, source, land, weights, (rows - 2 * HX) // 2, put)


def list_place(r, lanes):
    per = lanes // 16
    return r // (4 * per), (r % per) * 16 + RIM * ((r // per) % 4)


def y_rows(rows):
    pairs = (rows + 2 * HV + 1) // 2
    return TALL * HY, (pairs + pairs % 2) * EDGE


def row_of(i, rows, own, ends, reach):
    return own[i] if 0 <= i < rows else ends[i + reach if i < 0 else i - rows + reach]


def pack_rows(vel, vel_halo, ob, oa, lists, ya, yb):
    rows, cols, lanes = vel.shape
    vrow = rows + 2 * HV
    slots = 0
    even_x, even_y = is_even("gx"), is_even("gy")

    def put(at, last, first):
        n = last.shape[0]
        ya[at : at + n] = jnp.where(even_y, last, first).astype(BF)
        yb[at : at + n] = jnp.where(even_y, first, last).astype(BF)

    sub = iota((EDGE, 1), 0)
    is_u = iota((1, lanes), 1) < lanes // 2
    blocks = []
    for r in range(vrow):
        to = RIM * (r % 2)

        def ends_of(ref, k):
            return ref[k, cols - EDGE : cols, :], ref[k, 0:EDGE, :]

        i = r - HV
        if 0 <= i < rows:
            last, first = ends_of(vel, i)
        else:
            last, first = ends_of(vel_halo, r if i < 0 else r - rows)

        def moved(value, one, two):
            return pltpu.roll(value, (two - one) % EDGE, 0) if one != two else value

        one, two = moved(last, EDGE - RIM, to), moved(last, EDGE - RIM - 1, to)
        last = jnp.where(sub == to, jnp.where(is_u, two, pltpu.roll(one, lanes // 2, 1)), one)
        one, two = moved(first, 0, to), moved(first, RIM, to + RIM - 1)
        first = jnp.where(sub == to + RIM - 1, jnp.where(is_u, one, pltpu.roll(two, lanes // 2, 1)), one)
        blocks.append((last, first))
    pairs = [
        [jnp.where(sub < RIM, blocks[r][i], blocks[r + 1][i]) for i in range(2)] for r in range(0, vrow, 2)
    ]
    pairs += [[jnp.zeros((EDGE, lanes), F32)] * 2] * (len(pairs) % 2)
    for i in range(0, len(pairs), 2):
        put(slots + i * EDGE, *[jnp.concatenate([pairs[i][j], pairs[i + 1][j]], axis=0) for j in range(2)])
    start = slots + len(pairs) * EDGE

    group = iota((1, lanes), 1) // RIM
    x_start = (HV - 1) * cols
    tiles = list_place(rows + 2 * HL - 1, lanes)[0] + 1
    acc = [[jnp.zeros((16, lanes), F32)] * 2 for _ in range(tiles)]
    for r in range(rows + 2 * HL):
        if HL <= r < HL + rows:
            own = lists[r - HL]
        else:
            i = r if r < HL else r - HL - rows
            at = x_start + i * 16
            one, two = (ob, oa) if r < HL else (oa, ob)
            own = pick(even_x, one[at : at + 16, :], two[at : at + 16, :])
        tile, to = list_place(r, lanes)
        acc[tile] = [
            jnp.where(group == to // RIM, pltpu.roll(own, (to - where) % lanes, 1), a)
            for a, where in zip(acc[tile], (cols - RIM, 0))
        ]
    for tile in range(tiles):
        put(start + tile * 16, acc[tile][0], acc[tile][1])


def halo_kernel(fixed_a, fixed_b, ends, rest, pb, pa, ya, yb):
    lanes = rest.shape[2]
    even_x, even_y = is_even("gx"), is_even("gy")
    wr, wc = rest.shape[0] + 2 * HX, rest.shape[1]

    def put(at, last, first):
        n = last.shape[0]
        ya[at : at + n] = jnp.where(even_y, last, first).astype(BF)
        yb[at : at + n] = jnp.where(even_y, first, last).astype(BF)

    before, after = pick(even_x, pb[...], pa[...]), pick(even_x, pa[...], pb[...])
    joined = jnp.concatenate([before.astype(BF), ends[0:HX], rest[...], ends[HX:], after.astype(BF)], axis=0)
    count = (wr + 2 * HX) * wc
    slots = TALL * HY
    at, cell = iota((2 * slots, count), 0), iota((2 * slots, count), 1)
    side, rest = at // slots, at % slots
    column = rest // TALL + jnp.where(side == 0, wc - HY, 0)
    row = rest % TALL
    chosen = ((row < wr + 2 * HX) & (cell == row * wc + column)).astype(F32).astype(BF)
    sides = jnp.dot(chosen, joined.reshape(count, lanes), preferred_element_type=F32)
    put(0, sides[0:slots], sides[slots:])
    ya[slots:], yb[slots:] = fixed_a[...], fixed_b[...]


def vorticity(ref, r, base, count):
    half = ref.shape[-1] // 2
    is_u = iota((1, 2 * half), 1) < half

    def at(dx, dy):
        return ref[r + dx, base + dy : base + dy + count, :]

    near = jnp.where(is_u, at(0, -1), at(1, 0)) - jnp.where(is_u, at(0, 1), at(-1, 0))
    far = jnp.where(is_u, at(0, -2), at(2, 0)) - jnp.where(is_u, at(0, 2), at(-2, 0))
    part = (8.0 / 12.0) * near - (1.0 / 12.0) * far
    return part + pltpu.roll(part, half, 1)


def averager(lanes):
    at = iota((2 * lanes, lanes), 0)
    to = iota((2 * lanes, lanes), 1)
    half = lanes // 2
    return jnp.where((at % lanes) // half == to % 2, 1.0 / half, 0.0).astype(BF)


def add_means(acc, first, values, average):
    size, lanes = values[0].shape
    parts = jnp.concatenate([jnp.concatenate(split(v), axis=1) for v in values], axis=0)
    sums = jnp.dot(parts, average, preferred_element_type=F32)
    place = iota((1, lanes), 1) // 2
    for i in range(len(values)):
        acc = jnp.where(place == first + i, sums[i * size : (i + 1) * size], acc)
    return acc


def turned(value):
    half = value.shape[-1] // 2
    sign = jnp.where(iota((1, 2 * half), 1) < half, 1.0, -1.0)
    return pltpu.roll(value, half, 1) * sign


def one_hot(full, cols):
    lanes = full.shape[1]
    wave_cols = cols // RY
    codes = full[0:EDGE]
    third = jnp.where(codes >= 6.0, 2.0, jnp.where(codes >= 3.0, 1.0, 0.0))
    slot = third * (wave_cols - 3.0) + codes + (iota((1, lanes), 1) // RY).astype(F32) - 1.0
    place = iota((3 * wave_cols, lanes), 0).astype(F32)
    hot = jnp.where(place == slot[0:1], full[K : K + 1], 0.0)
    for k in range(1, K):
        hot = hot + jnp.where(place == slot[k : k + 1], full[K + k : K + k + 1], 0.0)
    return hot.astype(BF)


def rim_lists(full, rim, r, cols):
    lanes = full.shape[1]
    lane = iota((1, lanes), 1)
    to = (r % (lanes // 16)) * 16
    rim = jnp.where(lane // RIM == to // RIM + 1, pltpu.roll(full, (to + RIM) % lanes, 1), rim)
    return jnp.where(lane // RIM == to // RIM + 2, pltpu.roll(full, (to + 3 * RIM - cols) % lanes, 1), rim)


def prepare_own_kernel(
    own, lists, codes_far, weights_far, basis_far,
    spin, turn, table, list_rim, wave_shares, chosen, spread, basis,
    vel, codes, weights, sems,
):
    rows, cols, lanes = own.shape
    pairs = ((codes_far, codes), (weights_far, weights), (basis_far, basis))
    copies = [pltpu.make_async_copy(one, two, sems.at[i]) for i, (one, two) in enumerate(pairs)]
    for copy in copies:
        copy.start()
    per = lanes // 16
    blank = jnp.zeros((EDGE, lanes), F32)

    def fill(i, _):
        vel[i, 0:EDGE, :] = blank
        vel[i, EDGE + cols :, :] = blank
        vel[i, EDGE : EDGE + cols, :] = own[i]
        return 0

    lax.fori_loop(0, rows, fill, 0, unroll=8)
    rim = [jnp.zeros((16, lanes), F32)] * list_rim.shape[0]
    for i in range(rows):
        g = (i + HL) // per
        full = lists[i]
        table[i], rim[g] = one_hot(full, cols), rim_lists(full, rim[g], i + HL, cols)
    for g, value in enumerate(rim):
        list_rim[g] = value

    ones = jnp.ones((8, lanes), BF)

    def widened(i):
        return lax.dot_general(lists[i, 2 * K :, :].astype(BF), ones, ROWS_DOT, preferred_element_type=F32)[0:cols]

    for i in (0, 1, rows - 2, rows - 1):
        spin[i] = widened(i)
    half = (rows - 4) // 2

    def absolute(m, _):
        for u in range(half):
            i = m * half + u + 2
            wide = widened(i)
            spin[i] = wide
            turn[i - 2] = wide + vorticity(vel, i, EDGE, cols)
        return 0

    lax.fori_loop(0, 2, absolute, 0)

    wc = cols // RY
    lane = iota((1, lanes), 1)
    at, to = iota(chosen.shape, 0), iota(chosen.shape, 1)
    reach = (RY + 2) * wc
    chosen[...] = ((to < reach) & (at == RY * (to % wc) + to // wc + RIM - 1)).astype(F32)
    at, to = iota((lanes, lanes), 0), iota((lanes, lanes), 1)
    spread[...] = ((at < reach) & (at % wc == to)).astype(F32).astype(BF)

    for copy in copies:
        copy.wait()
    at, to = iota((wc, lanes), 0), iota((wc, lanes), 1)
    repeat = ((to < reach) & (to % wc == at)).astype(F32).astype(BF)
    shift = (lane // wc).astype(F32)
    weight = [weights[:, k, :] for k in range(K)]
    whole = sum(weight[1:], weight[0])
    code = [jnp.dot(codes[:, k, :].astype(F32).astype(BF), repeat, preferred_element_type=F32) for k in range(K)]
    share = [
        sum(jnp.dot(p, repeat, preferred_element_type=F32) for p in split3(weight[k] / whole)) for k in range(K)
    ]
    for near in range(RX + 2):
        wave_shares[near] = sum(
            jnp.where(code[k] == near * (RY + 2.0) + shift, share[k], 0.0) for k in range(K)
        )


def prepare_ends_kernel(
    own, ob, oa, lists, spin_own, list_own, vel_halo, spin, turn, table, list_rim, fixed_a, fixed_b, vel
):
    rows, cols, lanes = own.shape
    per = lanes // 16
    even_x = is_even("gx")
    blank = jnp.zeros((EDGE, lanes), F32)
    list_rim[...] = list_own[...]
    ones = jnp.ones((8, lanes), BF)
    for side in range(2):
        one, two = (oa, ob) if side else (ob, oa)

        def from_x(start, n):
            return pick(even_x, one[start : start + n, :], two[start : start + n, :])

        parts = [from_x(i * cols, cols) for i in range(HV - 1)]
        outer = pltpu.roll(parts[0], lanes // 2, 1)
        parts = parts[1:] + [parts[0], outer] if side else [outer] + parts
        for k in range(HV):
            vel_halo[side * HV + k] = parts[k]
        near = [own[i] for i in (range(rows - HV + 1, rows) if side else range(HV - 1))]
        for k, value in enumerate(near + parts if side else parts + near):
            vel[side, k, 0:EDGE, :] = blank
            vel[side, k, EDGE + cols :, :] = blank
            vel[side, k, EDGE : EDGE + cols, :] = value
        for k in range(HL):
            at = side * HL + k
            r = k + side * (rows + HL)
            full = from_x((HV - 1) * cols + k * 16, 16)
            table[at], list_rim[r // per] = one_hot(full, cols), rim_lists(full, list_rim[r // per], r, cols)
            spin[at] = lax.dot_general(full[2 * K :].astype(BF), ones, ROWS_DOT, preferred_element_type=F32)[0:cols]
        for k in range(HL + 2):
            i = k + (rows - 2 if side else -HL)
            turn[side * (HL + 2) + k] = row_of(i, rows, spin_own, spin, HL) + vorticity(vel.at[side], k + 2, EDGE, cols)
    pack_rows(own, vel_halo, ob, oa, lists, fixed_a, fixed_b)


def inner_kernel(
    vel, vel_halo, spin_own, spin_ends, turn_own, turn_ends, table_own, table_ends,
    ends, rest, pb, pa, cells_ends, cells_rest,
    out, cells_far, mid_rim, drift_rim, spin_rim, total, prof_rim,
    mid, names, prof, drift, sems,
):
    rows, cols, lanes = out.shape
    copies = []
    wr, wc = rest.shape[0] + 2 * HX, rest.shape[1]
    for part, to in (
        (cells_ends.at[pl.ds(0, HX)], cells_far.at[pl.ds(0, HX)]),
        (cells_rest, cells_far.at[pl.ds(HX, wr - 2 * HX)]),
        (cells_ends.at[pl.ds(HX, HX)], cells_far.at[pl.ds(wr - HX, HX)]),
    ):
        copies.append(pltpu.make_async_copy(part, to, sems.at[len(copies)]))
    for copy in copies:
        copy.start()
    listed = rows + 2 * HL
    prow = wr + 2 * HX
    even_x = is_even("gx")
    lane = iota((1, lanes), 1)
    blank = jnp.zeros((EDGE, lanes), F32)
    for x in range(prow):
        if HX <= x < HX + wr:
            i = x - HX
            own = ends[i] if i < HX else rest[i - HX] if i < wr - HX else ends[i - wr + 2 * HX]
            part = own.astype(F32)
        elif x < HX:
            part = pick(even_x, pb[x], pa[x])
        else:
            part = pick(even_x, pa[x - HX - wr], pb[x - HX - wr])
        part = turned(part)
        prof[x * wc : (x + 1) * wc, :] = part
        names[x * wc : (x + 1) * wc, :] = part.astype(BF)
    prof_rim[...] = jnp.zeros(prof_rim.shape, F32)
    for c in range(HY):
        prof_rim[0, pl.ds(HY + c, prow, stride=2 * HY), :] = prof[pl.ds(c, prow, stride=wc), :]
        prof_rim[1, pl.ds(c, prow, stride=2 * HY), :] = prof[pl.ds(wc - HY + c, prow, stride=wc), :]

    block = 3 * wc

    def first(r, vel_ref, table_ref, turn_ref, spin_ref, vk, tk, uk):
        named = names[pl.ds(pl.multiple_of((r + 1) // 2 * wc, wc), block), :]
        stokes = lax.dot_general(table_ref[tk], named, ROWS_DOT, preferred_element_type=F32)[0:cols]
        drift[r] = stokes
        new = vel_ref[vk] + STEP * (turn_ref[uk] * stokes)
        mid[r, 0:EDGE, :] = blank
        mid[r, EDGE + cols :, :] = blank
        mid[r, EDGE : EDGE + cols, :] = new
        mid_rim[r, 0] = new[0 : 2 * EDGE]
        mid_rim[r, 1] = new[cols - 2 * EDGE :]
        for where in range(2):
            begin = RIM if where == 0 else cols - RIM - EDGE
            drift_rim[r, where] = drift[r, begin : begin + EDGE, :]
            spin_rim[r, where] = spin_ref[tk, begin : begin + EDGE, :]

    for i in [*range(-HL, 2), *range(rows - 2, rows + HL)]:
        end = i + HL if i < 2 else i - rows + HL + 4
        if 0 <= i < rows:
            first(i + HL, vel, table_own, turn_ends, spin_own, i, i, end)
        else:
            far = 0 if i < 0 else rows
            first(i + HL, vel_halo, table_ends, turn_ends, spin_ends, i - far + HV, i - far + HL, end)
    unroll = (rows - 4) // 2

    def first_step(m, _):
        for u in range(unroll):
            i = m * unroll + u + 2
            first(i + HL, vel, table_own, turn_own, spin_own, i, i, i - 2)
        return 0

    lax.fori_loop(0, 2, first_step, 0)

    average = averager(lanes)
    means = jnp.zeros((cols, lanes), F32)
    ready = []
    for n in range(rows + 2):
        r = n + HL - 1
        absolute = row_of(n - 1, rows, spin_own, spin_ends, HL) + vorticity(mid, r, EDGE, cols)
        old = row_of(n - 1, rows, vel, vel_halo, HV) + mid[r, EDGE : EDGE + cols, :]
        new = 0.5 * old + (0.5 * STEP) * (absolute * drift[r])
        ready.append(new)
        if len(ready) == 2 or n == rows + 1:
            means = add_means(means, n + 1 - len(ready), ready, average)
            ready = []
        if 1 <= n <= rows:
            out[n - 1] = new
    total[...] = means

    for copy in copies:
        copy.wait()


def rim_kernel(
    own, vel_halo, ya, yb, mid_rim, drift_rim, spin_rim, total, list_rim, prof_rim, wave_shares, chosen, spread, inner,
    out, current_far,
    vel, mid, prof, drift, spin, picked, means, strips, current, sems,
):
    rows, cols, lanes = own.shape
    vrow = rows + 2 * HV
    wr, wc = current.shape[1], current.shape[2]
    listed = rows + 2 * HL
    prow = wr + 2 * HX
    even_y = is_even("gy")
    has_south, has_north = inside("gy")
    lane = iota((1, lanes), 1)
    sub = iota((EDGE, 1), 0)
    slots, vel_rows = y_rows(rows)

    def from_y(start, n):
        a, b = ya[start : start + n, :], yb[start : start + n, :]
        return pick(even_y, b, a) * has_south, pick(even_y, a, b) * has_north

    middle = pl.ds(EDGE, cols - 2 * EDGE)
    copies = [pltpu.make_async_copy(inner.at[:, middle, :], out.at[:, middle, :], sems.at[0])]
    copies[0].start()

    blank = jnp.zeros((EDGE, lanes), F32)
    for r in range(vrow):
        vel[0, r, 0:EDGE, :] = blank
        vel[1, r, 2 * EDGE :, :] = blank
        ref, k = (own, r - HV) if HV <= r < HV + rows else (vel_halo, r if r < HV else r - rows)
        vel[0, r, EDGE:, :] = ref[k, 0 : 2 * EDGE, :]
        vel[1, r, 0 : 2 * EDGE, :] = ref[k, cols - 2 * EDGE : cols, :]
    for start in range(0, vel_rows, 2 * EDGE):
        pieces = from_y(slots + start, 2 * EDGE)
        for i in range(2):
            low, high = (p[i * EDGE : i * EDGE + EDGE] for p in pieces)
            low_moved, high_moved = pltpu.roll(low, lanes // 2, 1), pltpu.roll(high, lanes // 2, 1)
            low_in = jnp.where(sub % RIM == 0, low_moved, low)
            for j in range(2):
                r = (start + i * EDGE) // RIM + j
                if r < vrow:
                    at = j * RIM
                    vel[0, r, EDGE - RIM : EDGE, :] = low_in[at : at + RIM]
                    vel[0, r, EDGE - RIM - 1 : EDGE - RIM, :] = low[at : at + 1]
                    vel[1, r, 2 * EDGE : 2 * EDGE + RIM, :] = high[at : at + RIM]
                    vel[1, r, 2 * EDGE + RIM : 2 * EDGE + RIM + 1, :] = high_moved[at + RIM - 1 : at + RIM]

    prof[...] = prof_rim[...]
    south, north = from_y(0, slots)
    south, north = turned(south), turned(north)
    for c in range(HY):
        prof[0, pl.ds(c, TALL, stride=2 * HY), :] = south[TALL * c : TALL * (c + 1)]
        prof[1, pl.ds(HY + c, TALL, stride=2 * HY), :] = north[TALL * c : TALL * (c + 1)]

    per = lanes // 16
    start = slots + vel_rows
    span = 2 * per * HY
    place = iota((2 * span, lanes), 0).astype(F32)
    part = lane % 16
    offset = (part // EDGE) * span + ((lane // 16 + 1) // 2) * (2 * HY) + (part % EDGE) // RIM
    sub16 = iota((16, 1), 0)
    ones = jnp.ones((8, lanes), F32)
    none = jnp.zeros((2 * span, lanes), F32)
    for g in range(-(-listed // per)):
        tile, to = list_place(g * per, lanes)
        south, north = from_y(start + tile * 16, 16)
        full = list_rim[g]
        full = jnp.where(part // RIM == 0, pltpu.roll(south, (-to) % lanes, 1), full)
        full = jnp.where(part // RIM == 3, pltpu.roll(north, (3 * RIM - to) % lanes, 1), full)
        third = jnp.where(full >= 6.0, 2.0, jnp.where(full >= 3.0, 1.0, 0.0))
        full = jnp.where(sub16 < K, third + full + offset.astype(F32), full)
        hot = jnp.zeros((2 * span, lanes), F32)
        for k in range(K):
            hot = hot + jnp.where(place == full[k : k + 1], full[K + k : K + k + 1], 0.0)
        left = jnp.concatenate([hot, full[2 * K :], blank], axis=0).astype(BF)
        begin = g * (per // 2) * 2 * HY
        named = jnp.concatenate([prof[0, begin : begin + span, :], prof[1, begin : begin + span, :]], axis=0)
        right = jnp.concatenate([
            jnp.concatenate([named, blank, blank], axis=0),
            jnp.concatenate([none, ones, blank], axis=0),
        ], axis=1).astype(BF)
        both = lax.dot_general(left, right, ROWS_DOT, preferred_element_type=F32)
        for i in range(min(per, listed - g * per)):
            for side in range(2):
                at = i * 16 + side * EDGE
                drift[side, g * per + i] = both[at : at + EDGE, 0:lanes]
                spin[side, g * per + i] = both[at : at + EDGE, lanes:]

    lift = HV - HL
    for r in range(listed):
        for side in range(2):
            base = RIM + side * EDGE
            mid[side, r, 2 * EDGE * side : 2 * EDGE * side + EDGE, :] = blank
            mid[side, r, EDGE - side * EDGE : 3 * EDGE - side * EDGE, :] = mid_rim[r, side]
            absolute = spin[side, r] + vorticity(vel.at[side], r + lift, base, EDGE)
            new = vel[side, r + lift, base : base + EDGE, :] + STEP * (absolute * drift[side, r])
            mid[side, r, base : base + EDGE, :] = new

    average = averager(lanes)
    acc = jnp.zeros((2 * EDGE, lanes), F32)
    ready = []
    step = rows // PARTS
    begins = (EDGE - 1, EDGE + 1)
    for n in range(rows + 2):
        r = n + HL - 1
        both = []
        for side, begin in enumerate(begins):
            order = 1 - 2 * side

            def joined(here, there):
                return jnp.concatenate([here, there][::order], axis=0)[begin - RIM : begin - RIM + EDGE]

            absolute = joined(spin[side, r], spin_rim[r, side]) + vorticity(mid.at[side], r, begin, EDGE)
            old = vel[side, r + lift, begin : begin + EDGE, :] + mid[side, r, begin : begin + EDGE, :]
            new = 0.5 * old + (0.5 * STEP) * (absolute * joined(drift[side, r], drift_rim[r, side]))
            both.append(new)
            if 1 <= n <= rows:
                kept = inner[n - 1, side * (cols - EDGE) : side * (cols - EDGE) + EDGE, :]
                moved = pltpu.roll(new, EDGE - 1 if side == 0 else 1, 0)
                strips[side, n - 1] = jnp.where(sub == (EDGE - 1 if side == 0 else 0), kept, moved)
        ready.append(jnp.concatenate(both, axis=0))
        if len(ready) == 9 or n == rows + 1:
            acc = add_means(acc, n + 1 - len(ready), ready, average)
            ready = []
        if n and n % step == 0:
            part = pl.ds(n - step, step)
            for side, at in ((0, 0), (1, cols - EDGE)):
                one, two = strips.at[side, part], out.at[part, pl.ds(at, EDGE), :]
                copies.append(pltpu.make_async_copy(one, two, sems.at[len(copies)]))
                copies[-1].start()
    count = cols + 2 * RIM
    means[0:EDGE] = blank
    means[count - EDGE :] = blank
    means[RIM - 1 : RIM - 1 + EDGE] = acc[0:EDGE]
    means[RIM - 1 + EDGE : count - RIM + 1 - EDGE] = total[EDGE - 1 : cols - EDGE + 1, :]
    means[count - RIM + 1 - EDGE : count - RIM + 1] = acc[EDGE:]

    named = chosen[...].astype(BF)
    picked[...] = sum(
        lax.dot_general(p, named, ROWS_DOT, preferred_element_type=F32) for p in split(means[...])
    )
    summed = [
        sum(wave_shares[near] * picked[pl.ds(2 * near + c, wr, stride=2 * RX), :] for near in range(RX + 2))
        for c in range(2)
    ]
    sums = sum(
        jnp.dot(p, spread[...], preferred_element_type=F32) for p in split(jnp.concatenate(summed, axis=0))
    )
    current[0] = sums[0:wr, 0:wc]
    current[1] = sums[wr:, 0:wc]
    copies.append(pltpu.make_async_copy(current, current_far, sems.at[len(copies)]))
    copies[-1].start()
    for copy in copies:
        copy.wait()


VMEM = pl.BlockSpec(memory_space=pltpu.VMEM)
ANY = pl.BlockSpec(memory_space=pltpu.HBM)


def call(kernel, name, outs, *args, scratch=(), any_in=(), any_out=()):
    args = [pltpu.with_memory_space_constraint(v, pltpu.HBM) if i in any_in else v for i, v in enumerate(args)]
    return pl.pallas_call(
        kernel,
        out_shape=tuple(jax.ShapeDtypeStruct(shape, dtype) for shape, dtype in outs),
        in_specs=[ANY if i in any_in else VMEM for i in range(len(args))],
        out_specs=tuple(ANY if i in any_out else VMEM for i in range(len(outs))),
        scratch_shapes=list(scratch),
        compiler_params=pltpu.CompilerParams(vmem_limit_bytes=14 << 20),
        name=name,
    )(*args)


def shards(
    spectrum, courant, source, wave_land, stokes_kernel, velocity, coriolis,
    ocean_codes, ocean_weights, wave_codes, wave_weights,
):
    wr, wc, bins = spectrum.shape
    rows, cols, lanes = velocity.shape
    listed = rows + 2 * HL
    prow = wr + 2 * HX

    with jax.named_scope("spectrum_edges"):
        codes, weights = jnp.transpose(ocean_codes, (0, 2, 1)), jnp.transpose(ocean_weights, (0, 2, 1))
        size = sum(x_rows(cols)) + wc * bins // lanes
        outs = [((size, lanes), BF)] * 2 + [((wr, bins), BF)] * 2 + [((rows, 16, lanes), F32)]
        outs += [(spectrum.shape, BF), (courant.shape, F32), ((wc, wr), F32), ((wc, wr), F32)]
        oa, ob, ya, yb, lists, spectrum, courant, source, land = call(
            edges_kernel, "edges", outs,
            spectrum, courant, source, wave_land, codes, weights, coriolis, velocity, any_in=range(8),
            scratch=[
                pltpu.VMEM(source.shape, F32),
                pltpu.VMEM(wave_land.shape, wave_land.dtype),
                pltpu.VMEM(codes.shape, codes.dtype),
                pltpu.VMEM(weights.shape, F32),
                pltpu.VMEM(coriolis.shape, F32),
                pltpu.VMEM((2, HV, cols, lanes), F32),
                pltpu.SemaphoreType.DMA((9,)),
            ],
        )
        oa, ob = exchange("gx", oa, ob)
        ya, yb = exchange("gy", ya, yb)

    with jax.named_scope("prepare_own"):
        groups = -(-listed // (lanes // 16))
        level = (cols, lanes)
        spin_own, turn_own, table_own, list_own, wave_shares, chosen, spread, stokes_kernel = call(
            prepare_own_kernel, "prepare_own",
            [
                ((rows, *level), F32), ((rows - 4, *level), F32), ((rows, 3 * wc, lanes), BF), ((groups, 16, lanes), F32),
                ((RX + 2, wr, lanes), F32), ((cols + 2 * RIM, lanes), F32), ((lanes, lanes), BF),
                (stokes_kernel.shape, BF),
            ],
            velocity, lists, jnp.transpose(wave_codes, (0, 2, 1)), jnp.transpose(wave_weights, (0, 2, 1)),
            stokes_kernel, any_in=(2, 3, 4),
            scratch=[
                pltpu.VMEM((rows, cols + 2 * EDGE, lanes), F32),
                pltpu.VMEM((wr, K, wc), wave_codes.dtype),
                pltpu.VMEM((wr, K, wc), F32),
                pltpu.SemaphoreType.DMA((3,)),
            ],
        )

    with jax.named_scope("wave"):
        edge = (HX, wc, lanes)
        sides = call(sides_kernel, "sides", [((2, wc, bins), BF)], ob, oa, list_own)[0]
        cells_ends, ends, pa, pb = call(
            wave_ends_kernel, "wave_ends",
            [((2 * HX, wc, bins), BF), ((2 * HX, wc, lanes), BF), (edge, BF), (edge, BF)],
            spectrum, sides, ya, yb, courant, source, land, stokes_kernel,
        )
        pa, pb = exchange("gx", pa, pb)
        cells_rest, rest = call(
            wave_rest_kernel, "wave_rest",
            [((wr - 2 * HX, wc, bins), BF), ((wr - 2 * HX, wc, lanes), BF)],
            spectrum, ya, yb, courant, source, land, stokes_kernel, ends,
        )

    with jax.named_scope("prepare_ends"):
        size = y_rows(rows)[1] + (list_place(listed - 1, lanes)[0] + 1) * 16
        vel_halo, spin_ends, turn_ends, table_ends, list_rim, fixed_a, fixed_b = call(
            prepare_ends_kernel, "prepare_ends",
            [
                ((2 * HV, *level), F32), ((2 * HL, *level), F32), ((2 * HL + 4, *level), F32),
                ((2 * HL, 3 * wc, lanes), BF), ((groups, 16, lanes), F32),
                ((size, lanes), BF), ((size, lanes), BF),
            ],
            velocity, ob, oa, lists, spin_own, list_own,
            scratch=[pltpu.VMEM((2, 2 * HV - 1, cols + 2 * EDGE, lanes), F32)],
        )

    with jax.named_scope("halo"):
        size += y_rows(rows)[0]
        ya, yb = call(
            halo_kernel, "halo", [((size, lanes), BF)] * 2, fixed_a, fixed_b, ends, rest, pb, pa
        )
        ya, yb = exchange("gy", ya, yb)

    with jax.named_scope("inner"):
        scratch = [
            pltpu.VMEM((listed, cols + 2 * EDGE, lanes), F32),
            pltpu.VMEM((prow * wc, lanes), BF),
            pltpu.VMEM((prow * wc, lanes), F32),
            pltpu.VMEM((listed, cols, lanes), F32),
            pltpu.SemaphoreType.DMA((3,)),
        ]
        result, new_spectrum, mid_rim, drift_rim, spin_rim, total, prof_rim = call(
            inner_kernel, "inner",
            [
                (velocity.shape, F32),
                (spectrum.shape, BF),
                ((listed, 2, 2 * EDGE, lanes), F32),
                ((listed, 2, EDGE, lanes), F32),
                ((listed, 2, EDGE, lanes), F32),
                ((cols, lanes), F32),
                ((2, 2 * HY * (TALL + 4), lanes), F32),
            ],
            velocity, vel_halo, spin_own, spin_ends, turn_own, turn_ends, table_own, table_ends,
            ends, rest, pb, pa,
            cells_ends, cells_rest, scratch=scratch, any_out=(1,),
        )

    with jax.named_scope("rim"):
        scratch = [
            pltpu.VMEM((2, rows + 2 * HV, 3 * EDGE, lanes), F32),
            pltpu.VMEM((2, listed, 3 * EDGE, lanes), F32),
            pltpu.VMEM((2, 2 * HY * (TALL + 4), lanes), F32),
            pltpu.VMEM((2, listed, EDGE, lanes), F32),
            pltpu.VMEM((2, listed, EDGE, lanes), F32),
            pltpu.VMEM((lanes, lanes), F32),
            pltpu.VMEM((cols + 2 * RIM, lanes), F32),
            pltpu.VMEM((2, rows, EDGE, lanes), F32),
            pltpu.VMEM((2, wr, wc), F32),
            pltpu.SemaphoreType.DMA((2 + 2 * PARTS,)),
        ]
        new_velocity, current = call(
            rim_kernel, "rim", [(velocity.shape, F32), ((2, wr, wc), F32)],
            velocity, vel_halo, ya, yb, mid_rim, drift_rim, spin_rim, total, list_rim, prof_rim, wave_shares, chosen, spread,
            result, scratch=scratch, any_out=(0, 1),
        )
    return new_spectrum, new_velocity, current


def solution(mesh):
    return jax.shard_map(
        shards,
        mesh=mesh,
        in_specs=(
            P("gx", "gy", None), P(), P("gx", "gy"), P("gx", "gy"), P(), P("gx", "gy", None),
            P("gx", "gy"), P("gx", "gy", None), P("gx", "gy", None), P("gx", "gy", None), P("gx", "gy", None),
        ),
        out_specs=(P("gx", "gy", None), P("gx", "gy", None), P(None, "gx", "gy")),
        check_vma=False,
    )
```

```python
import jax
import jax.numpy as jnp
from jax import lax
from jax.experimental import pallas as pl
from jax.experimental.pallas import tpu as pltpu
from jax.sharding import PartitionSpec as P

K = 4
RX = 2
RY = 4
STEP = 0.5
PARTS = 2
TALL = 24
RIM = 4
HV, HL = 5, 3
HX, HY = 3, 2
EDGE = 8
BF = jnp.bfloat16
F32 = jnp.float32
ROWS_DOT = (((0,), (0,)), ((), ()))


def partner(i, count, parity):
    return (i ^ 1) if parity == 0 else ((i + 1) ^ 1) - 1


def swap(value, axis, parity):
    nx, ny = lax.axis_size("gx"), lax.axis_size("gy")
    pairs = []
    for x in range(nx):
        for y in range(ny):
            tx, ty = x, y
            if axis == "gx":
                tx = partner(x, nx, parity) % nx
            else:
                ty = partner(y, ny, parity)
                if not 0 <= ty < ny:
                    tx, ty = x ^ 1, y
            pairs.append((x * ny + y, tx * ny + ty))
    return lax.ppermute(value, ("gx", "gy"), pairs)


def exchange(axis, to_a, to_b):
    from_a = swap(to_a, axis, 0)
    from_b = swap(to_b, axis, 1)
    return from_a, from_b


def is_even(axis):
    return lax.axis_index(axis) % 2 == 0


def inside(axis):
    index = lax.axis_index(axis)
    before = jnp.where(index == 0, 0.0, 1.0).astype(F32)
    after = jnp.where(index == lax.axis_size(axis) - 1, 0.0, 1.0).astype(F32)
    return before, after


def pick(cond, one, other):
    return jnp.where(cond, one.astype(F32), other.astype(F32))


def split(value):
    high = value.astype(BF)
    return high, (value - high.astype(F32)).astype(BF)


def split3(value):
    high = value.astype(BF)
    rest = value - high.astype(F32)
    middle = rest.astype(BF)
    return high, middle, (rest - middle.astype(F32)).astype(BF)


def iota(shape, dim):
    return lax.broadcasted_iota(jnp.int32, shape, dim)


def x_rows(cols):
    return (HV - 1) * cols, HL * 16


def edges_kernel(*refs):
    (spec_far, courant_far, source_far, land_far, codes_far, weights_far, coriolis_far, vel_far) = refs[:8]
    (oa, ob, ya, yb, lists, spec, courant, source_t, land_t) = refs[8:17]
    (source, land, codes, weights, coriolis, vel, sems) = refs[17:]
    rows, cols, bins = spec.shape
    lanes = vel.shape[-1]
    pairs = [(spec_far, spec)]
    pairs += [(vel_far.at[pl.ds(at, HV)], vel.at[i]) for i, at in ((0, 0), (1, vel_far.shape[0] - HV))]
    pairs += [(codes_far, codes), (weights_far, weights), (coriolis_far, coriolis)]
    pairs += [(courant_far, courant), (source_far, source), (land_far, land)]
    copies = [pltpu.make_async_copy(one, two, sems.at[i]) for i, (one, two) in enumerate(pairs)]
    for copy in copies:
        copy.start()
    even_x, even_y = is_even("gx"), is_even("gy")

    def put(at, last, first):
        n = last.shape[0]
        oa[at : at + n] = jnp.where(even_x, last, first).astype(BF)
        ob[at : at + n] = jnp.where(even_x, first, last).astype(BF)

    at, cell = iota((2 * rows, rows * cols), 0), iota((2 * rows, rows * cols), 1)
    wanted = jnp.where(at < rows, at * cols, (at - rows) * cols + cols - 1)
    chosen = (cell == wanted).astype(F32).astype(BF)
    copies[0].wait()
    sides = jnp.dot(chosen, spec[...].reshape(rows * cols, bins), preferred_element_type=F32)
    start = sum(x_rows(codes.shape[2]))
    for i in range(bins // lanes):
        part = slice(i * lanes, (i + 1) * lanes)
        put(start + i * cols, spec[rows - 1, :, part].astype(F32), spec[0, :, part].astype(F32))
    first, last = sides[0:rows], sides[rows:]
    ya[...] = jnp.where(even_y, last, first).astype(BF)
    yb[...] = jnp.where(even_y, first, last).astype(BF)

    for copy in copies[1:]:
        copy.wait()
    source_t[...] = source[...].T
    land_t[...] = land[...].astype(F32).T
    listed, wide = codes.shape[0], codes.shape[2]
    is_u = iota((1, lanes), 1) < lanes // 2
    outer = [
        jnp.where(is_u, pltpu.roll(vel[side, one], lanes // 2, 1), vel[side, two])
        for side, one, two in ((1, 0, 1), (0, HV - 1, HV - 2))
    ]
    put(0, *outer)
    for i in range(1, HV - 1):
        put(i * wide, vel[1, i + 1], vel[0, i - 1])
    for r in range(listed):
        lists[r] = jnp.zeros((16, lanes), F32)
        weight = weights[r]
        turn = coriolis[r : r + 1, :]
        high = turn.astype(BF).astype(F32)
        lists[r, 0:K, 0:wide] = codes[r].astype(F32)
        lists[r, K : 2 * K, 0:wide] = weight / jnp.sum(weight, axis=0, keepdims=True)
        lists[r, 2 * K : 2 * K + 1, 0:wide] = high
        lists[r, 2 * K + 1 : 2 * K + 2, 0:wide] = turn - high
    for i in range(HL):
        put((HV - 1) * wide + i * 16, lists[listed - HL + i], lists[i])


def advance(chosen, spec, sides, ya, yb, courant, source, land, weights, at_once, put):
    rows, cols, _ = spec.shape
    even_y = is_even("gy")
    has_south, has_north = inside("gy")
    south = pick(even_y, yb[...], ya[...]) * has_south
    north = pick(even_y, ya[...], yb[...]) * has_north
    cx, cy = courant[0:1, :], courant[1:2, :]
    ax, ay = jnp.abs(cx), jnp.abs(cy)
    from_west, from_south = cx > 0.0, cy > 0.0
    keep = 1.0 - ax - ay
    sub = iota((cols, 1), 0)
    cells = []
    for x in chosen:
        center = spec[x].astype(F32)
        before = spec[x - 1].astype(F32) if x else sides[0]
        after = spec[x + 1].astype(F32) if x < rows - 1 else sides[1]
        below = jnp.where(sub == 0, south[x : x + 1, :], pltpu.roll(center, 1, 0))
        above = jnp.where(sub == cols - 1, north[x : x + 1, :], pltpu.roll(center, cols - 1, 0))
        advected = (
            keep * center
            + ax * jnp.where(from_west, before, after)
            + ay * jnp.where(from_south, below, above)
        )
        wind = 1.0 + 0.2 * source[:, x : x + 1]
        updated = land[:, x : x + 1] * (advected * (wind - 0.1 * advected))
        cells.append(updated.astype(BF))
        if len(cells) == at_once:
            parts = jnp.dot(jnp.concatenate(cells, axis=0), weights[...], preferred_element_type=F32)
            for i, value in enumerate(cells):
                put(x - at_once + 1 + i, value, parts[i * cols : (i + 1) * cols])
            cells = []


def spectrum_of(ref, cols, bins):
    lanes = ref.shape[1]
    start = ref.shape[0] - cols * bins // lanes
    blocks = [ref[start + i * cols : start + (i + 1) * cols, :] for i in range(bins // lanes)]
    return jnp.concatenate(blocks, axis=1)


def side_kernel(xb, after, side):
    side[...] = spectrum_of(xb, *side.shape)


def wave_ends_kernel(spec, side, ya, yb, xa, courant, source, land, weights, out, profile, pa, pb):
    rows, cols, bins = spec.shape
    even_x = is_even("gx")
    parts = []

    def put(x, value, part):
        i = len(parts)
        out[i], profile[i] = value, part.astype(BF)
        parts.append(part)

    ends = list(range(HX)) + list(range(rows - HX, rows))
    one, two = side[...], spectrum_of(xa, cols, bins)
    sides = pick(even_x, one, two), pick(even_x, two, one)
    advance(ends, spec, sides, ya, yb, courant, source, land, weights, HX, put)
    for i in range(HX):
        first, last = parts[i], parts[HX + i]
        pa[i] = jnp.where(even_x, last, first).astype(BF)
        pb[i] = jnp.where(even_x, first, last).astype(BF)


def wave_rest_kernel(spec, ya, yb, courant, source, land, weights, ends, out, profile):
    rows = spec.shape[0]

    def put(x, value, part):
        out[x - HX], profile[x - HX] = value, part.astype(BF)

    advance(range(HX, rows - HX), spec, None, ya, yb, courant, source, land, weights, (rows - 2 * HX) // 2, put)


def list_place(r, lanes):
    per = lanes // 16
    return r // (4 * per), (r % per) * 16 + RIM * ((r // per) % 4)


def y_rows(rows):
    pairs = (rows + 2 * HV + 1) // 2
    return TALL * HY, (pairs + pairs % 2) * EDGE


def row_of(i, rows, own, ends, reach):
    return own[i] if 0 <= i < rows else ends[i + reach if i < 0 else i - rows + reach]


def pack_rows(vel, vel_halo, ob, oa, lists, ya, yb):
    rows, cols, lanes = vel.shape
    vrow = rows + 2 * HV
    slots = 0
    even_x, even_y = is_even("gx"), is_even("gy")

    def put(at, last, first):
        n = last.shape[0]
        ya[at : at + n] = jnp.where(even_y, last, first).astype(BF)
        yb[at : at + n] = jnp.where(even_y, first, last).astype(BF)

    sub = iota((EDGE, 1), 0)
    is_u = iota((1, lanes), 1) < lanes // 2
    blocks = []
    for r in range(vrow):
        to = RIM * (r % 2)

        def ends_of(ref, k):
            return ref[k, cols - EDGE : cols, :], ref[k, 0:EDGE, :]

        i = r - HV
        if 0 <= i < rows:
            last, first = ends_of(vel, i)
        else:
            last, first = ends_of(vel_halo, r if i < 0 else r - rows)

        def moved(value, one, two):
            return pltpu.roll(value, (two - one) % EDGE, 0) if one != two else value

        one, two = moved(last, EDGE - RIM, to), moved(last, EDGE - RIM - 1, to)
        last = jnp.where(sub == to, jnp.where(is_u, two, pltpu.roll(one, lanes // 2, 1)), one)
        one, two = moved(first, 0, to), moved(first, RIM, to + RIM - 1)
        first = jnp.where(sub == to + RIM - 1, jnp.where(is_u, one, pltpu.roll(two, lanes // 2, 1)), one)
        blocks.append((last, first))
    pairs = [
        [jnp.where(sub < RIM, blocks[r][i], blocks[r + 1][i]) for i in range(2)] for r in range(0, vrow, 2)
    ]
    pairs += [[jnp.zeros((EDGE, lanes), F32)] * 2] * (len(pairs) % 2)
    for i in range(0, len(pairs), 2):
        put(slots + i * EDGE, *[jnp.concatenate([pairs[i][j], pairs[i + 1][j]], axis=0) for j in range(2)])
    start = slots + len(pairs) * EDGE

    group = iota((1, lanes), 1) // RIM
    x_start = (HV - 1) * cols
    tiles = list_place(rows + 2 * HL - 1, lanes)[0] + 1
    acc = [[jnp.zeros((16, lanes), F32)] * 2 for _ in range(tiles)]
    for r in range(rows + 2 * HL):
        if HL <= r < HL + rows:
            own = lists[r - HL]
        else:
            i = r if r < HL else r - HL - rows
            at = x_start + i * 16
            one, two = (ob, oa) if r < HL else (oa, ob)
            own = pick(even_x, one[at : at + 16, :], two[at : at + 16, :])
        tile, to = list_place(r, lanes)
        acc[tile] = [
            jnp.where(group == to // RIM, pltpu.roll(own, (to - where) % lanes, 1), a)
            for a, where in zip(acc[tile], (cols - RIM, 0))
        ]
    for tile in range(tiles):
        put(start + tile * 16, acc[tile][0], acc[tile][1])


def halo_kernel(fixed_a, fixed_b, columns, ends, rest, pb, pa, ya, yb):
    lanes = rest.shape[2]
    even_x, even_y = is_even("gx"), is_even("gy")
    wr, wc = rest.shape[0] + 2 * HX, rest.shape[1]

    def put(at, last, first):
        n = last.shape[0]
        ya[at : at + n] = jnp.where(even_y, last, first).astype(BF)
        yb[at : at + n] = jnp.where(even_y, first, last).astype(BF)

    before, after = pick(even_x, pb[...], pa[...]), pick(even_x, pa[...], pb[...])
    joined = jnp.concatenate([before.astype(BF), ends[0:HX], rest[...], ends[HX:], after.astype(BF)], axis=0)
    count = (wr + 2 * HX) * wc
    slots = TALL * HY
    sides = jnp.dot(columns[...], joined.reshape(count, lanes), preferred_element_type=F32)
    put(0, sides[0:slots], sides[slots:])
    ya[slots:], yb[slots:] = fixed_a[...], fixed_b[...]


def vorticity(ref, r, base, count):
    half = ref.shape[-1] // 2
    is_u = iota((1, 2 * half), 1) < half

    def at(dx, dy):
        return ref[r + dx, base + dy : base + dy + count, :]

    near = jnp.where(is_u, at(0, -1), at(1, 0)) - jnp.where(is_u, at(0, 1), at(-1, 0))
    far = jnp.where(is_u, at(0, -2), at(2, 0)) - jnp.where(is_u, at(0, 2), at(-2, 0))
    part = (8.0 / 12.0) * near - (1.0 / 12.0) * far
    return part + pltpu.roll(part, half, 1)


def averager(lanes):
    at = iota((2 * lanes, lanes), 0)
    to = iota((2 * lanes, lanes), 1)
    half = lanes // 2
    return jnp.where((at % lanes) // half == to % 2, 1.0 / half, 0.0).astype(BF)


def add_means(acc, first, values, average):
    size, lanes = values[0].shape
    parts = jnp.concatenate([jnp.concatenate(split(v), axis=1) for v in values], axis=0)
    sums = jnp.dot(parts, average, preferred_element_type=F32)
    place = iota((1, lanes), 1) // 2
    for i in range(len(values)):
        acc = jnp.where(place == first + i, sums[i * size : (i + 1) * size], acc)
    return acc


def turned(value):
    half = value.shape[-1] // 2
    sign = jnp.where(iota((1, 2 * half), 1) < half, 1.0, -1.0)
    return pltpu.roll(value, half, 1) * sign


def one_hot(full, cols):
    lanes = full.shape[1]
    wave_cols = cols // RY
    codes = full[0:EDGE]
    third = jnp.where(codes >= 6.0, 2.0, jnp.where(codes >= 3.0, 1.0, 0.0))
    slot = third * (wave_cols - 3.0) + codes + (iota((1, lanes), 1) // RY).astype(F32) - 1.0
    place = iota((3 * wave_cols, lanes), 0).astype(F32)
    hot = jnp.where(place == slot[0:1], full[K : K + 1], 0.0)
    for k in range(1, K):
        hot = hot + jnp.where(place == slot[k : k + 1], full[K + k : K + k + 1], 0.0)
    return hot.astype(BF)


def rim_lists(full, rim, r, cols):
    lanes = full.shape[1]
    lane = iota((1, lanes), 1)
    to = (r % (lanes // 16)) * 16
    rim = jnp.where(lane // RIM == to // RIM + 1, pltpu.roll(full, (to + RIM) % lanes, 1), rim)
    return jnp.where(lane // RIM == to // RIM + 2, pltpu.roll(full, (to + 3 * RIM - cols) % lanes, 1), rim)


def prepare_own_kernel(
    own, lists, codes_far, weights_far, basis_far,
    spin, turn, table, list_rim, wave_shares, chosen, spread, basis, columns,
    vel, codes, weights, sems,
):
    rows, cols, lanes = own.shape
    pairs = ((codes_far, codes), (weights_far, weights), (basis_far, basis))
    copies = [pltpu.make_async_copy(one, two, sems.at[i]) for i, (one, two) in enumerate(pairs)]
    for copy in copies:
        copy.start()
    per = lanes // 16
    blank = jnp.zeros((EDGE, lanes), F32)

    def fill(i, _):
        vel[i, 0:EDGE, :] = blank
        vel[i, EDGE + cols :, :] = blank
        vel[i, EDGE : EDGE + cols, :] = own[i]
        return 0

    lax.fori_loop(0, rows, fill, 0, unroll=8)
    rim = [jnp.zeros((16, lanes), F32)] * list_rim.shape[0]
    for i in range(rows):
        g = (i + HL) // per
        full = lists[i]
        table[i], rim[g] = one_hot(full, cols), rim_lists(full, rim[g], i + HL, cols)
    for g, value in enumerate(rim):
        list_rim[g] = value

    ones = jnp.ones((8, lanes), BF)

    def widened(i):
        return lax.dot_general(lists[i, 2 * K :, :].astype(BF), ones, ROWS_DOT, preferred_element_type=F32)[0:cols]

    for i in (0, 1, rows - 2, rows - 1):
        spin[i] = widened(i)
    half = (rows - 4) // 2

    def absolute(m, _):
        for u in range(half):
            i = m * half + u + 2
            wide = widened(i)
            spin[i] = wide
            turn[i - 2] = wide + vorticity(vel, i, EDGE, cols)
        return 0

    lax.fori_loop(0, 2, absolute, 0)

    wc = cols // RY
    lane = iota((1, lanes), 1)
    slots, wr = TALL * HY, rows // RX
    at, cell = iota(columns.shape, 0), iota(columns.shape, 1)
    rest = at % slots
    column = rest // TALL + jnp.where(at < slots, wc - HY, 0)
    row = rest % TALL
    columns[...] = ((row < wr + 2 * HX) & (cell == row * wc + column)).astype(F32).astype(BF)

    at, to = iota(chosen.shape, 0), iota(chosen.shape, 1)
    reach = (RY + 2) * wc
    chosen[...] = ((to < reach) & (at == RY * (to % wc) + to // wc + RIM - 1)).astype(F32)
    at, to = iota((lanes, lanes), 0), iota((lanes, lanes), 1)
    spread[...] = ((at < reach) & (at % wc == to)).astype(F32).astype(BF)

    for copy in copies:
        copy.wait()
    at, to = iota((wc, lanes), 0), iota((wc, lanes), 1)
    repeat = ((to < reach) & (to % wc == at)).astype(F32).astype(BF)
    shift = (lane // wc).astype(F32)
    weight = [weights[:, k, :] for k in range(K)]
    whole = sum(weight[1:], weight[0])
    code = [jnp.dot(codes[:, k, :].astype(F32).astype(BF), repeat, preferred_element_type=F32) for k in range(K)]
    share = [
        sum(jnp.dot(p, repeat, preferred_element_type=F32) for p in split3(weight[k] / whole)) for k in range(K)
    ]
    for near in range(RX + 2):
        wave_shares[near] = sum(
            jnp.where(code[k] == near * (RY + 2.0) + shift, share[k], 0.0) for k in range(K)
        )


def prepare_ends_kernel(
    own, ob, oa, lists, spin_own, list_own, vel_halo, spin, turn, table, list_rim, fixed_a, fixed_b, vel
):
    rows, cols, lanes = own.shape
    per = lanes // 16
    even_x = is_even("gx")
    blank = jnp.zeros((EDGE, lanes), F32)
    list_rim[...] = list_own[...]
    ones = jnp.ones((8, lanes), BF)
    for side in range(2):
        one, two = (oa, ob) if side else (ob, oa)

        def from_x(start, n):
            return pick(even_x, one[start : start + n, :], two[start : start + n, :])

        parts = [from_x(i * cols, cols) for i in range(HV - 1)]
        outer = pltpu.roll(parts[0], lanes // 2, 1)
        parts = parts[1:] + [parts[0], outer] if side else [outer] + parts
        for k in range(HV):
            vel_halo[side * HV + k] = parts[k]
        near = [own[i] for i in (range(rows - HV + 1, rows) if side else range(HV - 1))]
        for k, value in enumerate(near + parts if side else parts + near):
            vel[side, k, 0:EDGE, :] = blank
            vel[side, k, EDGE + cols :, :] = blank
            vel[side, k, EDGE : EDGE + cols, :] = value
        for k in range(HL):
            at = side * HL + k
            r = k + side * (rows + HL)
            full = from_x((HV - 1) * cols + k * 16, 16)
            table[at], list_rim[r // per] = one_hot(full, cols), rim_lists(full, list_rim[r // per], r, cols)
            spin[at] = lax.dot_general(full[2 * K :].astype(BF), ones, ROWS_DOT, preferred_element_type=F32)[0:cols]
        for k in range(HL + 2):
            i = k + (rows - 2 if side else -HL)
            turn[side * (HL + 2) + k] = row_of(i, rows, spin_own, spin, HL) + vorticity(vel.at[side], k + 2, EDGE, cols)
    pack_rows(own, vel_halo, ob, oa, lists, fixed_a, fixed_b)


def inner_kernel(
    vel, vel_halo, spin_own, spin_ends, turn_own, turn_ends, table_own, table_ends,
    ends, rest, pb, pa, cells_ends, cells_rest,
    out, cells_far, mid_rim, drift_rim, spin_rim, total, prof_rim,
    mid, names, prof, drift, sems,
):
    rows, cols, lanes = out.shape
    copies = []
    wr, wc = rest.shape[0] + 2 * HX, rest.shape[1]
    for part, to in (
        (cells_ends.at[pl.ds(0, HX)], cells_far.at[pl.ds(0, HX)]),
        (cells_rest, cells_far.at[pl.ds(HX, wr - 2 * HX)]),
        (cells_ends.at[pl.ds(HX, HX)], cells_far.at[pl.ds(wr - HX, HX)]),
    ):
        copies.append(pltpu.make_async_copy(part, to, sems.at[len(copies)]))
    for copy in copies:
        copy.start()
    listed = rows + 2 * HL
    prow = wr + 2 * HX
    even_x = is_even("gx")
    lane = iota((1, lanes), 1)
    blank = jnp.zeros((EDGE, lanes), F32)
    for x in range(prow):
        if HX <= x < HX + wr:
            i = x - HX
            own = ends[i] if i < HX else rest[i - HX] if i < wr - HX else ends[i - wr + 2 * HX]
            part = own.astype(F32)
        elif x < HX:
            part = pick(even_x, pb[x], pa[x])
        else:
            part = pick(even_x, pa[x - HX - wr], pb[x - HX - wr])
        part = turned(part)
        prof[x * wc : (x + 1) * wc, :] = part
        names[x * wc : (x + 1) * wc, :] = part.astype(BF)
    prof_rim[...] = jnp.zeros(prof_rim.shape, F32)
    for c in range(HY):
        prof_rim[0, pl.ds(HY + c, prow, stride=2 * HY), :] = prof[pl.ds(c, prow, stride=wc), :]
        prof_rim[1, pl.ds(c, prow, stride=2 * HY), :] = prof[pl.ds(wc - HY + c, prow, stride=wc), :]

    block = 3 * wc

    def first(r, vel_ref, table_ref, turn_ref, spin_ref, vk, tk, uk):
        named = names[pl.ds(pl.multiple_of((r + 1) // 2 * wc, wc), block), :]
        stokes = lax.dot_general(table_ref[tk], named, ROWS_DOT, preferred_element_type=F32)[0:cols]
        drift[r] = stokes
        new = vel_ref[vk] + STEP * (turn_ref[uk] * stokes)
        mid[r, 0:EDGE, :] = blank
        mid[r, EDGE + cols :, :] = blank
        mid[r, EDGE : EDGE + cols, :] = new
        for where in range(2):
            begin = RIM if where == 0 else cols - RIM - EDGE
            mid_rim[r, where] = mid[r, EDGE + begin : 2 * EDGE + begin, :]
            drift_rim[r, where] = drift[r, begin : begin + EDGE, :]
            spin_rim[r, where] = spin_ref[tk, begin : begin + EDGE, :]

    for i in [*range(-HL, 2), *range(rows - 2, rows + HL)]:
        end = i + HL if i < 2 else i - rows + HL + 4
        if 0 <= i < rows:
            first(i + HL, vel, table_own, turn_ends, spin_own, i, i, end)
        else:
            far = 0 if i < 0 else rows
            first(i + HL, vel_halo, table_ends, turn_ends, spin_ends, i - far + HV, i - far + HL, end)
    unroll = (rows - 4) // 2

    def first_step(m, _):
        for u in range(unroll):
            i = m * unroll + u + 2
            first(i + HL, vel, table_own, turn_own, spin_own, i, i, i - 2)
        return 0

    lax.fori_loop(0, 2, first_step, 0)

    average = averager(lanes)
    means = jnp.zeros((cols, lanes), F32)
    ready = []
    for n in range(rows + 2):
        r = n + HL - 1
        absolute = row_of(n - 1, rows, spin_own, spin_ends, HL) + vorticity(mid, r, EDGE, cols)
        old = row_of(n - 1, rows, vel, vel_halo, HV) + mid[r, EDGE : EDGE + cols, :]
        new = 0.5 * old + (0.5 * STEP) * (absolute * drift[r])
        ready.append(new)
        if len(ready) == 2 or n == rows + 1:
            means = add_means(means, n + 1 - len(ready), ready, average)
            ready = []
        if 1 <= n <= rows:
            out[n - 1] = new
    total[...] = means

    for copy in copies:
        copy.wait()


def rim_kernel(
    own, vel_halo, ya, yb, mid_rim, drift_rim, spin_rim, total, list_rim, prof_rim, wave_shares, chosen, spread, inner,
    out, current_far,
    vel, mid, prof, drift, spin, picked, means, strips, current, sems,
):
    rows, cols, lanes = own.shape
    vrow = rows + 2 * HV
    wr, wc = current.shape[1], current.shape[2]
    listed = rows + 2 * HL
    prow = wr + 2 * HX
    even_y = is_even("gy")
    has_south, has_north = inside("gy")
    lane = iota((1, lanes), 1)
    sub = iota((EDGE, 1), 0)
    slots, vel_rows = y_rows(rows)

    def from_y(start, n):
        a, b = ya[start : start + n, :], yb[start : start + n, :]
        return pick(even_y, b, a) * has_south, pick(even_y, a, b) * has_north

    middle = pl.ds(EDGE, cols - 2 * EDGE)
    copies = [pltpu.make_async_copy(inner.at[:, middle, :], out.at[:, middle, :], sems.at[0])]
    copies[0].start()

    blank = jnp.zeros((EDGE, lanes), F32)
    for r in range(vrow):
        vel[0, r, 0:EDGE, :] = blank
        vel[1, r, 2 * EDGE :, :] = blank
        ref, k = (own, r - HV) if HV <= r < HV + rows else (vel_halo, r if r < HV else r - rows)
        vel[0, r, EDGE:, :] = ref[k, 0 : 2 * EDGE, :]
        vel[1, r, 0 : 2 * EDGE, :] = ref[k, cols - 2 * EDGE : cols, :]
    for start in range(0, vel_rows, 2 * EDGE):
        pieces = from_y(slots + start, 2 * EDGE)
        for i in range(2):
            low, high = (p[i * EDGE : i * EDGE + EDGE] for p in pieces)
            low_moved, high_moved = pltpu.roll(low, lanes // 2, 1), pltpu.roll(high, lanes // 2, 1)
            low_in = jnp.where(sub % RIM == 0, low_moved, low)
            for j in range(2):
                r = (start + i * EDGE) // RIM + j
                if r < vrow:
                    at = j * RIM
                    vel[0, r, EDGE - RIM : EDGE, :] = low_in[at : at + RIM]
                    vel[0, r, EDGE - RIM - 1 : EDGE - RIM, :] = low[at : at + 1]
                    vel[1, r, 2 * EDGE : 2 * EDGE + RIM, :] = high[at : at + RIM]
                    vel[1, r, 2 * EDGE + RIM : 2 * EDGE + RIM + 1, :] = high_moved[at + RIM - 1 : at + RIM]

    prof[...] = prof_rim[...]
    south, north = from_y(0, slots)
    south, north = turned(south), turned(north)
    for c in range(HY):
        prof[0, pl.ds(c, TALL, stride=2 * HY), :] = south[TALL * c : TALL * (c + 1)]
        prof[1, pl.ds(HY + c, TALL, stride=2 * HY), :] = north[TALL * c : TALL * (c + 1)]

    per = lanes // 16
    start = slots + vel_rows
    span = 2 * per * HY
    place = iota((2 * span, lanes), 0).astype(F32)
    part = lane % 16
    offset = (part // EDGE) * span + ((lane // 16 + 1) // 2) * (2 * HY) + (part % EDGE) // RIM
    sub16 = iota((16, 1), 0)
    ones = jnp.ones((8, lanes), F32)
    none = jnp.zeros((2 * span, lanes), F32)
    for g in range(-(-listed // per)):
        tile, to = list_place(g * per, lanes)
        south, north = from_y(start + tile * 16, 16)
        full = list_rim[g]
        full = jnp.where(part // RIM == 0, pltpu.roll(south, (-to) % lanes, 1), full)
        full = jnp.where(part // RIM == 3, pltpu.roll(north, (3 * RIM - to) % lanes, 1), full)
        third = jnp.where(full >= 6.0, 2.0, jnp.where(full >= 3.0, 1.0, 0.0))
        full = jnp.where(sub16 < K, third + full + offset.astype(F32), full)
        hot = jnp.zeros((2 * span, lanes), F32)
        for k in range(K):
            hot = hot + jnp.where(place == full[k : k + 1], full[K + k : K + k + 1], 0.0)
        left = jnp.concatenate([hot, full[2 * K :], blank], axis=0).astype(BF)
        begin = g * (per // 2) * 2 * HY
        named = jnp.concatenate([prof[0, begin : begin + span, :], prof[1, begin : begin + span, :]], axis=0)
        right = jnp.concatenate([
            jnp.concatenate([named, blank, blank], axis=0),
            jnp.concatenate([none, ones, blank], axis=0),
        ], axis=1).astype(BF)
        both = lax.dot_general(left, right, ROWS_DOT, preferred_element_type=F32)
        for i in range(min(per, listed - g * per)):
            for side in range(2):
                at = i * 16 + side * EDGE
                drift[side, g * per + i] = both[at : at + EDGE, 0:lanes]
                spin[side, g * per + i] = both[at : at + EDGE, lanes:]

    lift = HV - HL
    for r in range(listed):
        for side in range(2):
            base = RIM + side * EDGE
            kept = RIM + EDGE - side * EDGE
            mid[side, r, kept : kept + EDGE, :] = mid_rim[r, side]
            absolute = spin[side, r] + vorticity(vel.at[side], r + lift, base, EDGE)
            new = vel[side, r + lift, base : base + EDGE, :] + STEP * (absolute * drift[side, r])
            mid[side, r, base : base + EDGE, :] = new

    average = averager(lanes)
    acc = jnp.zeros((2 * EDGE, lanes), F32)
    ready = []
    step = rows // PARTS
    begins = (EDGE - 1, EDGE + 1)
    for n in range(rows + 2):
        r = n + HL - 1
        both = []
        for side, begin in enumerate(begins):
            order = 1 - 2 * side

            def joined(here, there):
                return jnp.concatenate([here, there][::order], axis=0)[begin - RIM : begin - RIM + EDGE]

            absolute = joined(spin[side, r], spin_rim[r, side]) + vorticity(mid.at[side], r, begin, EDGE)
            old = vel[side, r + lift, begin : begin + EDGE, :] + mid[side, r, begin : begin + EDGE, :]
            new = 0.5 * old + (0.5 * STEP) * (absolute * joined(drift[side, r], drift_rim[r, side]))
            both.append(new)
            if 1 <= n <= rows:
                kept = inner[n - 1, side * (cols - EDGE) : side * (cols - EDGE) + EDGE, :]
                moved = pltpu.roll(new, EDGE - 1 if side == 0 else 1, 0)
                strips[side, n - 1] = jnp.where(sub == (EDGE - 1 if side == 0 else 0), kept, moved)
        ready.append(jnp.concatenate(both, axis=0))
        if len(ready) == 9 or n == rows + 1:
            acc = add_means(acc, n + 1 - len(ready), ready, average)
            ready = []
        if n and n % step == 0:
            part = pl.ds(n - step, step)
            for side, at in ((0, 0), (1, cols - EDGE)):
                one, two = strips.at[side, part], out.at[part, pl.ds(at, EDGE), :]
                copies.append(pltpu.make_async_copy(one, two, sems.at[len(copies)]))
                copies[-1].start()
    count = cols + 2 * RIM
    means[0:EDGE] = blank
    means[count - EDGE : count] = blank
    means[RIM - 1 : RIM - 1 + EDGE] = acc[0:EDGE]
    means[RIM - 1 + EDGE : count - RIM + 1 - EDGE] = total[EDGE - 1 : cols - EDGE + 1, :]
    means[count - RIM + 1 - EDGE : count - RIM + 1] = acc[EDGE:]

    means[count:] = jnp.zeros((means.shape[0] - count, lanes), F32)
    named = chosen[...].astype(BF)
    picked[...] = lax.dot_general(
        jnp.concatenate(split(means[...]), axis=0), jnp.concatenate([named] * 2, axis=0), ROWS_DOT,
        preferred_element_type=F32,
    )
    summed = [
        sum(wave_shares[near] * picked[pl.ds(2 * near + c, wr, stride=2 * RX), :] for near in range(RX + 2))
        for c in range(2)
    ]
    sums = jnp.dot(
        jnp.concatenate(split(jnp.concatenate(summed, axis=0)), axis=1),
        jnp.concatenate([spread[...]] * 2, axis=0),
        preferred_element_type=F32,
    )
    current[0] = sums[0:wr, 0:wc]
    current[1] = sums[wr:, 0:wc]
    copies.append(pltpu.make_async_copy(current, current_far, sems.at[len(copies)]))
    copies[-1].start()
    for copy in copies:
        copy.wait()


VMEM = pl.BlockSpec(memory_space=pltpu.VMEM)
ANY = pl.BlockSpec(memory_space=pltpu.HBM)


def call(kernel, name, outs, *args, scratch=(), any_in=(), any_out=()):
    args = [pltpu.with_memory_space_constraint(v, pltpu.HBM) if i in any_in else v for i, v in enumerate(args)]
    return pl.pallas_call(
        kernel,
        out_shape=tuple(jax.ShapeDtypeStruct(shape, dtype) for shape, dtype in outs),
        in_specs=[ANY if i in any_in else VMEM for i in range(len(args))],
        out_specs=tuple(ANY if i in any_out else VMEM for i in range(len(outs))),
        scratch_shapes=list(scratch),
        compiler_params=pltpu.CompilerParams(vmem_limit_bytes=14 << 20),
        name=name,
    )(*args)


def shards(
    spectrum, courant, source, wave_land, stokes_kernel, velocity, coriolis,
    ocean_codes, ocean_weights, wave_codes, wave_weights,
):
    wr, wc, bins = spectrum.shape
    rows, cols, lanes = velocity.shape
    listed = rows + 2 * HL
    prow = wr + 2 * HX

    with jax.named_scope("spectrum_edges"):
        codes, weights = jnp.transpose(ocean_codes, (0, 2, 1)), jnp.transpose(ocean_weights, (0, 2, 1))
        size = sum(x_rows(cols)) + wc * bins // lanes
        outs = [((size, lanes), BF)] * 2 + [((wr, bins), BF)] * 2 + [((rows, 16, lanes), F32)]
        outs += [(spectrum.shape, BF), (courant.shape, F32), ((wc, wr), F32), ((wc, wr), F32)]
        oa, ob, ya, yb, lists, spectrum, courant, source, land = call(
            edges_kernel, "edges", outs,
            spectrum, courant, source, wave_land, codes, weights, coriolis, velocity, any_in=range(8),
            scratch=[
                pltpu.VMEM(source.shape, F32),
                pltpu.VMEM(wave_land.shape, wave_land.dtype),
                pltpu.VMEM(codes.shape, codes.dtype),
                pltpu.VMEM(weights.shape, F32),
                pltpu.VMEM(coriolis.shape, F32),
                pltpu.VMEM((2, HV, cols, lanes), F32),
                pltpu.SemaphoreType.DMA((9,)),
            ],
        )
        oa, ob = exchange("gx", oa, ob)
        ya, yb = exchange("gy", ya, yb)

    with jax.named_scope("prepare_own"):
        groups = -(-listed // (lanes // 16))
        level = (cols, lanes)
        named = -(-(cols + 2 * RIM) // 16) * 16
        spin_own, turn_own, table_own, list_own, wave_shares, chosen, spread, stokes_kernel, columns = call(
            prepare_own_kernel, "prepare_own",
            [
                ((rows, *level), F32), ((rows - 4, *level), F32), ((rows, 3 * wc, lanes), BF), ((groups, 16, lanes), F32),
                ((RX + 2, wr, lanes), F32), ((named, lanes), F32), ((lanes, lanes), BF),
                (stokes_kernel.shape, BF), ((2 * TALL * HY, prow * wc), BF),
            ],
            velocity, lists, jnp.transpose(wave_codes, (0, 2, 1)), jnp.transpose(wave_weights, (0, 2, 1)),
            stokes_kernel, any_in=(2, 3, 4),
            scratch=[
                pltpu.VMEM((rows, cols + 2 * EDGE, lanes), F32),
                pltpu.VMEM((wr, K, wc), wave_codes.dtype),
                pltpu.VMEM((wr, K, wc), F32),
                pltpu.SemaphoreType.DMA((3,)),
            ],
        )

    with jax.named_scope("wave"):
        edge = (HX, wc, lanes)
        side = call(side_kernel, "side", [((wc, bins), BF)], ob, list_own)[0]
        cells_ends, ends, pa, pb = call(
            wave_ends_kernel, "wave_ends",
            [((2 * HX, wc, bins), BF), ((2 * HX, wc, lanes), BF), (edge, BF), (edge, BF)],
            spectrum, side, ya, yb, oa, courant, source, land, stokes_kernel,
        )
        pa, pb = exchange("gx", pa, pb)
        cells_rest, rest = call(
            wave_rest_kernel, "wave_rest",
            [((wr - 2 * HX, wc, bins), BF), ((wr - 2 * HX, wc, lanes), BF)],
            spectrum, ya, yb, courant, source, land, stokes_kernel, ends,
        )

    with jax.named_scope("prepare_ends"):
        size = y_rows(rows)[1] + (list_place(listed - 1, lanes)[0] + 1) * 16
        vel_halo, spin_ends, turn_ends, table_ends, list_rim, fixed_a, fixed_b = call(
            prepare_ends_kernel, "prepare_ends",
            [
                ((2 * HV, *level), F32), ((2 * HL, *level), F32), ((2 * HL + 4, *level), F32),
                ((2 * HL, 3 * wc, lanes), BF), ((groups, 16, lanes), F32),
                ((size, lanes), BF), ((size, lanes), BF),
            ],
            velocity, ob, oa, lists, spin_own, list_own,
            scratch=[pltpu.VMEM((2, 2 * HV - 1, cols + 2 * EDGE, lanes), F32)],
        )

    with jax.named_scope("halo"):
        size += y_rows(rows)[0]
        ya, yb = call(
            halo_kernel, "halo", [((size, lanes), BF)] * 2, fixed_a, fixed_b, columns, ends, rest, pb, pa
        )
        ya, yb = exchange("gy", ya, yb)

    with jax.named_scope("inner"):
        scratch = [
            pltpu.VMEM((listed, cols + 2 * EDGE, lanes), F32),
            pltpu.VMEM((prow * wc, lanes), BF),
            pltpu.VMEM((prow * wc, lanes), F32),
            pltpu.VMEM((listed, cols, lanes), F32),
            pltpu.SemaphoreType.DMA((3,)),
        ]
        result, new_spectrum, mid_rim, drift_rim, spin_rim, total, prof_rim = call(
            inner_kernel, "inner",
            [
                (velocity.shape, F32),
                (spectrum.shape, BF),
                ((listed, 2, EDGE, lanes), F32),
                ((listed, 2, EDGE, lanes), F32),
                ((listed, 2, EDGE, lanes), F32),
                ((cols, lanes), F32),
                ((2, 2 * HY * (TALL + 4), lanes), F32),
            ],
            velocity, vel_halo, spin_own, spin_ends, turn_own, turn_ends, table_own, table_ends,
            ends, rest, pb, pa,
            cells_ends, cells_rest, scratch=scratch, any_out=(1,),
        )

    with jax.named_scope("rim"):
        scratch = [
            pltpu.VMEM((2, rows + 2 * HV, 3 * EDGE, lanes), F32),
            pltpu.VMEM((2, listed, 3 * EDGE, lanes), F32),
            pltpu.VMEM((2, 2 * HY * (TALL + 4), lanes), F32),
            pltpu.VMEM((2, listed, EDGE, lanes), F32),
            pltpu.VMEM((2, listed, EDGE, lanes), F32),
            pltpu.VMEM((lanes, lanes), F32),
            pltpu.VMEM((named, lanes), F32),
            pltpu.VMEM((2, rows, EDGE, lanes), F32),
            pltpu.VMEM((2, wr, wc), F32),
            pltpu.SemaphoreType.DMA((2 + 2 * PARTS,)),
        ]
        new_velocity, current = call(
            rim_kernel, "rim", [(velocity.shape, F32), ((2, wr, wc), F32)],
            velocity, vel_halo, ya, yb, mid_rim, drift_rim, spin_rim, total, list_rim, prof_rim, wave_shares, chosen, spread,
            result, scratch=scratch, any_out=(0, 1),
        )
    return new_spectrum, new_velocity, current


def solution(mesh):
    return jax.shard_map(
        shards,
        mesh=mesh,
        in_specs=(
            P("gx", "gy", None), P(), P("gx", "gy"), P("gx", "gy"), P(), P("gx", "gy", None),
            P("gx", "gy"), P("gx", "gy", None), P("gx", "gy", None), P("gx", "gy", None), P("gx", "gy", None),
        ),
        out_specs=(P("gx", "gy", None), P("gx", "gy", None), P(None, "gx", "gy")),
        check_vma=False,
    )
```

```python
import jax
import jax.numpy as jnp
from jax import lax
from jax.experimental import pallas as pl
from jax.experimental.pallas import tpu as pltpu
from jax.sharding import PartitionSpec as P

K = 4
RX = 2
RY = 4
STEP = 0.5
PARTS = 2
TALL = 24
RIM = 4
HV, HL = 5, 3
HX, HY = 3, 2
EDGE = 8
BF = jnp.bfloat16
F32 = jnp.float32
ROWS_DOT = (((0,), (0,)), ((), ()))


def partner(i, count, parity):
    return (i ^ 1) if parity == 0 else ((i + 1) ^ 1) - 1


def swap(value, axis, parity):
    nx, ny = lax.axis_size("gx"), lax.axis_size("gy")
    pairs = []
    for x in range(nx):
        for y in range(ny):
            tx, ty = x, y
            if axis == "gx":
                tx = partner(x, nx, parity) % nx
            else:
                ty = partner(y, ny, parity)
                if not 0 <= ty < ny:
                    tx, ty = x ^ 1, y
            pairs.append((x * ny + y, tx * ny + ty))
    return lax.ppermute(value, ("gx", "gy"), pairs)


def exchange(axis, to_a, to_b):
    from_a = swap(to_a, axis, 0)
    from_b = swap(to_b, axis, 1)
    return from_a, from_b


def is_even(axis):
    return lax.axis_index(axis) % 2 == 0


def inside(axis):
    index = lax.axis_index(axis)
    before = jnp.where(index == 0, 0.0, 1.0).astype(F32)
    after = jnp.where(index == lax.axis_size(axis) - 1, 0.0, 1.0).astype(F32)
    return before, after


def pick(cond, one, other):
    return jnp.where(cond, one.astype(F32), other.astype(F32))


def split(value):
    high = value.astype(BF)
    return high, (value - high.astype(F32)).astype(BF)


def split3(value):
    high = value.astype(BF)
    rest = value - high.astype(F32)
    middle = rest.astype(BF)
    return high, middle, (rest - middle.astype(F32)).astype(BF)


def iota(shape, dim):
    return lax.broadcasted_iota(jnp.int32, shape, dim)


def x_rows(cols):
    return (HV - 1) * cols, HL * 16


def edges_kernel(*refs):
    (spec_far, courant_far, source_far, land_far, codes_far, weights_far, coriolis_far, vel_far) = refs[:8]
    (oa, ob, ya, yb, lists, spec, courant, source_t, land_t) = refs[8:17]
    (source, land, codes, weights, coriolis, vel, sems) = refs[17:]
    rows, cols, bins = spec.shape
    lanes = vel.shape[-1]
    pairs = [(spec_far, spec)]
    pairs += [(vel_far.at[pl.ds(at, HV)], vel.at[i]) for i, at in ((0, 0), (1, vel_far.shape[0] - HV))]
    pairs += [(codes_far, codes), (weights_far, weights), (coriolis_far, coriolis)]
    pairs += [(courant_far, courant), (source_far, source), (land_far, land)]
    copies = [pltpu.make_async_copy(one, two, sems.at[i]) for i, (one, two) in enumerate(pairs)]
    for copy in copies:
        copy.start()
    even_x, even_y = is_even("gx"), is_even("gy")

    def put(at, last, first):
        n = last.shape[0]
        oa[at : at + n] = jnp.where(even_x, last, first).astype(BF)
        ob[at : at + n] = jnp.where(even_x, first, last).astype(BF)

    at, cell = iota((2 * rows, rows * cols), 0), iota((2 * rows, rows * cols), 1)
    wanted = jnp.where(at < rows, at * cols, (at - rows) * cols + cols - 1)
    chosen = (cell == wanted).astype(F32).astype(BF)
    copies[0].wait()
    sides = jnp.dot(chosen, spec[...].reshape(rows * cols, bins), preferred_element_type=F32)
    start = sum(x_rows(codes.shape[2]))
    for i in range(bins // lanes):
        part = slice(i * lanes, (i + 1) * lanes)
        put(start + i * cols, spec[rows - 1, :, part].astype(F32), spec[0, :, part].astype(F32))
    first, last = sides[0:rows], sides[rows:]
    ya[...] = jnp.where(even_y, last, first).astype(BF)
    yb[...] = jnp.where(even_y, first, last).astype(BF)

    for copy in copies[1:]:
        copy.wait()
    source_t[...] = source[...].T
    land_t[...] = land[...].astype(F32).T
    listed, wide = codes.shape[0], codes.shape[2]
    is_u = iota((1, lanes), 1) < lanes // 2
    outer = [
        jnp.where(is_u, pltpu.roll(vel[side, one], lanes // 2, 1), vel[side, two])
        for side, one, two in ((1, 0, 1), (0, HV - 1, HV - 2))
    ]
    put(0, *outer)
    for i in range(1, HV - 1):
        put(i * wide, vel[1, i + 1], vel[0, i - 1])
    for r in range(listed):
        lists[r] = jnp.zeros((16, lanes), F32)
        weight = weights[r]
        turn = coriolis[r : r + 1, :]
        high = turn.astype(BF).astype(F32)
        lists[r, 0:K, 0:wide] = codes[r].astype(F32)
        lists[r, K : 2 * K, 0:wide] = weight / jnp.sum(weight, axis=0, keepdims=True)
        lists[r, 2 * K : 2 * K + 1, 0:wide] = high
        lists[r, 2 * K + 1 : 2 * K + 2, 0:wide] = turn - high
    for i in range(HL):
        put((HV - 1) * wide + i * 16, lists[listed - HL + i], lists[i])


def advance(chosen, spec, sides, ya, yb, courant, source, land, weights, at_once, put):
    rows, cols, _ = spec.shape
    even_y = is_even("gy")
    has_south, has_north = inside("gy")
    south = pick(even_y, yb[...], ya[...]) * has_south
    north = pick(even_y, ya[...], yb[...]) * has_north
    cx, cy = courant[0:1, :], courant[1:2, :]
    ax, ay = jnp.abs(cx), jnp.abs(cy)
    from_west, from_south = cx > 0.0, cy > 0.0
    keep = 1.0 - ax - ay
    sub = iota((cols, 1), 0)
    cells = []
    for x in chosen:
        center = spec[x].astype(F32)
        before = spec[x - 1].astype(F32) if x else sides[0]
        after = spec[x + 1].astype(F32) if x < rows - 1 else sides[1]
        below = jnp.where(sub == 0, south[x : x + 1, :], pltpu.roll(center, 1, 0))
        above = jnp.where(sub == cols - 1, north[x : x + 1, :], pltpu.roll(center, cols - 1, 0))
        advected = (
            keep * center
            + ax * jnp.where(from_west, before, after)
            + ay * jnp.where(from_south, below, above)
        )
        wind = 1.0 + 0.2 * source[:, x : x + 1]
        updated = land[:, x : x + 1] * (advected * (wind - 0.1 * advected))
        cells.append(updated.astype(BF))
        if len(cells) == at_once:
            parts = jnp.dot(jnp.concatenate(cells, axis=0), weights[...], preferred_element_type=F32)
            for i, value in enumerate(cells):
                put(x - at_once + 1 + i, value, parts[i * cols : (i + 1) * cols])
            cells = []


def spectrum_of(ref, cols, bins):
    lanes = ref.shape[1]
    start = ref.shape[0] - cols * bins // lanes
    blocks = [ref[start + i * cols : start + (i + 1) * cols, :] for i in range(bins // lanes)]
    return jnp.concatenate(blocks, axis=1)


def side_kernel(xb, after, side):
    side[...] = spectrum_of(xb, *side.shape)


def wave_ends_kernel(spec, side, ya, yb, xa, courant, source, land, weights, out, profile, pa, pb):
    rows, cols, bins = spec.shape
    even_x = is_even("gx")
    parts = []

    def put(x, value, part):
        i = len(parts)
        out[i], profile[i] = value, part.astype(BF)
        parts.append(part)

    ends = list(range(HX)) + list(range(rows - HX, rows))
    one, two = side[...], spectrum_of(xa, cols, bins)
    sides = pick(even_x, one, two), pick(even_x, two, one)
    advance(ends, spec, sides, ya, yb, courant, source, land, weights, HX, put)
    for i in range(HX):
        first, last = parts[i], parts[HX + i]
        pa[i] = jnp.where(even_x, last, first).astype(BF)
        pb[i] = jnp.where(even_x, first, last).astype(BF)


def wave_rest_kernel(spec, ya, yb, courant, source, land, weights, ends, out, profile):
    rows = spec.shape[0]

    def put(x, value, part):
        out[x - HX], profile[x - HX] = value, part.astype(BF)

    advance(range(HX, rows - HX), spec, None, ya, yb, courant, source, land, weights, (rows - 2 * HX) // 2, put)


def list_place(r, lanes):
    per = lanes // 16
    return r // (4 * per), (r % per) * 16 + RIM * ((r // per) % 4)


def y_rows(rows):
    pairs = (rows + 2 * HV + 1) // 2
    return TALL * HY, (pairs + pairs % 2) * EDGE


def row_of(i, rows, own, ends, reach):
    return own[i] if 0 <= i < rows else ends[i + reach if i < 0 else i - rows + reach]


def pack_rows(vel, vel_halo, ob, oa, lists, ya, yb):
    rows, cols, lanes = vel.shape
    vrow = rows + 2 * HV
    slots = 0
    even_x, even_y = is_even("gx"), is_even("gy")

    def put(at, last, first):
        n = last.shape[0]
        ya[at : at + n] = jnp.where(even_y, last, first).astype(BF)
        yb[at : at + n] = jnp.where(even_y, first, last).astype(BF)

    sub = iota((EDGE, 1), 0)
    is_u = iota((1, lanes), 1) < lanes // 2
    blocks = []
    for r in range(vrow):
        to = RIM * (r % 2)

        def ends_of(ref, k):
            return ref[k, cols - EDGE : cols, :], ref[k, 0:EDGE, :]

        i = r - HV
        if 0 <= i < rows:
            last, first = ends_of(vel, i)
        else:
            last, first = ends_of(vel_halo, r if i < 0 else r - rows)

        def moved(value, one, two):
            return pltpu.roll(value, (two - one) % EDGE, 0) if one != two else value

        one, two = moved(last, EDGE - RIM, to), moved(last, EDGE - RIM - 1, to)
        last = jnp.where(sub == to, jnp.where(is_u, two, pltpu.roll(one, lanes // 2, 1)), one)
        one, two = moved(first, 0, to), moved(first, RIM, to + RIM - 1)
        first = jnp.where(sub == to + RIM - 1, jnp.where(is_u, one, pltpu.roll(two, lanes // 2, 1)), one)
        blocks.append((last, first))
    pairs = [
        [jnp.where(sub < RIM, blocks[r][i], blocks[r + 1][i]) for i in range(2)] for r in range(0, vrow, 2)
    ]
    pairs += [[jnp.zeros((EDGE, lanes), F32)] * 2] * (len(pairs) % 2)
    for i in range(0, len(pairs), 2):
        put(slots + i * EDGE, *[jnp.concatenate([pairs[i][j], pairs[i + 1][j]], axis=0) for j in range(2)])
    start = slots + len(pairs) * EDGE

    group = iota((1, lanes), 1) // RIM
    x_start = (HV - 1) * cols
    tiles = list_place(rows + 2 * HL - 1, lanes)[0] + 1
    acc = [[jnp.zeros((16, lanes), F32)] * 2 for _ in range(tiles)]
    for r in range(rows + 2 * HL):
        if HL <= r < HL + rows:
            own = lists[r - HL]
        else:
            i = r if r < HL else r - HL - rows
            at = x_start + i * 16
            one, two = (ob, oa) if r < HL else (oa, ob)
            own = pick(even_x, one[at : at + 16, :], two[at : at + 16, :])
        tile, to = list_place(r, lanes)
        acc[tile] = [
            jnp.where(group == to // RIM, pltpu.roll(own, (to - where) % lanes, 1), a)
            for a, where in zip(acc[tile], (cols - RIM, 0))
        ]
    for tile in range(tiles):
        put(start + tile * 16, acc[tile][0], acc[tile][1])


def halo_kernel(fixed_a, fixed_b, columns, ends, rest, pb, pa, ya, yb):
    lanes = rest.shape[2]
    even_x, even_y = is_even("gx"), is_even("gy")
    wr, wc = rest.shape[0] + 2 * HX, rest.shape[1]

    def put(at, last, first):
        n = last.shape[0]
        ya[at : at + n] = jnp.where(even_y, last, first).astype(BF)
        yb[at : at + n] = jnp.where(even_y, first, last).astype(BF)

    before, after = pick(even_x, pb[...], pa[...]), pick(even_x, pa[...], pb[...])
    joined = jnp.concatenate([before.astype(BF), ends[0:HX], rest[...], ends[HX:], after.astype(BF)], axis=0)
    count = (wr + 2 * HX) * wc
    slots = TALL * HY
    sides = jnp.dot(columns[...], joined.reshape(count, lanes), preferred_element_type=F32)
    put(0, sides[0:slots], sides[slots:])
    ya[slots:], yb[slots:] = fixed_a[...], fixed_b[...]


def vorticity(ref, r, base, count):
    half = ref.shape[-1] // 2
    is_u = iota((1, 2 * half), 1) < half

    def at(dx, dy):
        return ref[r + dx, base + dy : base + dy + count, :]

    near = jnp.where(is_u, at(0, -1), at(1, 0)) - jnp.where(is_u, at(0, 1), at(-1, 0))
    far = jnp.where(is_u, at(0, -2), at(2, 0)) - jnp.where(is_u, at(0, 2), at(-2, 0))
    part = (8.0 / 12.0) * near - (1.0 / 12.0) * far
    return part + pltpu.roll(part, half, 1)


def averager(lanes):
    at = iota((2 * lanes, lanes), 0)
    to = iota((2 * lanes, lanes), 1)
    half = lanes // 2
    return jnp.where((at % lanes) // half == to % 2, 1.0 / half, 0.0).astype(BF)


def add_means(acc, first, values, average):
    size, lanes = values[0].shape
    parts = jnp.concatenate([jnp.concatenate(split(v), axis=1) for v in values], axis=0)
    sums = jnp.dot(parts, average, preferred_element_type=F32)
    place = iota((1, lanes), 1) // 2
    for i in range(len(values)):
        acc = jnp.where(place == first + i, sums[i * size : (i + 1) * size], acc)
    return acc


def turned(value):
    half = value.shape[-1] // 2
    sign = jnp.where(iota((1, 2 * half), 1) < half, 1.0, -1.0)
    return pltpu.roll(value, half, 1) * sign


def one_hot(full, cols):
    lanes = full.shape[1]
    wave_cols = cols // RY
    codes = full[0:EDGE]
    third = jnp.where(codes >= 6.0, 2.0, jnp.where(codes >= 3.0, 1.0, 0.0))
    slot = third * (wave_cols - 3.0) + codes + (iota((1, lanes), 1) // RY).astype(F32) - 1.0
    place = iota((3 * wave_cols, lanes), 0).astype(F32)
    hot = jnp.where(place == slot[0:1], full[K : K + 1], 0.0)
    for k in range(1, K):
        hot = hot + jnp.where(place == slot[k : k + 1], full[K + k : K + k + 1], 0.0)
    return hot.astype(BF)


def rim_lists(full, rim, r, cols):
    lanes = full.shape[1]
    lane = iota((1, lanes), 1)
    to = (r % (lanes // 16)) * 16
    rim = jnp.where(lane // RIM == to // RIM + 1, pltpu.roll(full, (to + RIM) % lanes, 1), rim)
    return jnp.where(lane // RIM == to // RIM + 2, pltpu.roll(full, (to + 3 * RIM - cols) % lanes, 1), rim)


def prepare_own_kernel(
    own, lists, codes_far, weights_far, basis_far,
    spin, turn, table, list_rim, wave_shares, chosen, spread, basis, columns,
    vel, codes, weights, sems,
):
    rows, cols, lanes = own.shape
    pairs = ((codes_far, codes), (weights_far, weights), (basis_far, basis))
    copies = [pltpu.make_async_copy(one, two, sems.at[i]) for i, (one, two) in enumerate(pairs)]
    for copy in copies:
        copy.start()
    per = lanes // 16
    blank = jnp.zeros((EDGE, lanes), F32)

    def fill(i, _):
        vel[i, 0:EDGE, :] = blank
        vel[i, EDGE + cols :, :] = blank
        vel[i, EDGE : EDGE + cols, :] = own[i]
        return 0

    lax.fori_loop(0, rows, fill, 0, unroll=8)
    rim = [jnp.zeros((16, lanes), F32)] * list_rim.shape[0]
    for i in range(rows):
        g = (i + HL) // per
        full = lists[i]
        table[i], rim[g] = one_hot(full, cols), rim_lists(full, rim[g], i + HL, cols)
    for g, value in enumerate(rim):
        list_rim[g] = value

    ones = jnp.ones((8, lanes), BF)

    def widened(i):
        return lax.dot_general(lists[i, 2 * K :, :].astype(BF), ones, ROWS_DOT, preferred_element_type=F32)[0:cols]

    for i in (0, 1, rows - 2, rows - 1):
        spin[i] = widened(i)
    half = (rows - 4) // 2

    def absolute(m, _):
        for u in range(half):
            i = m * half + u + 2
            wide = widened(i)
            spin[i] = wide
            turn[i - 2] = wide + vorticity(vel, i, EDGE, cols)
        return 0

    lax.fori_loop(0, 2, absolute, 0)

    wc = cols // RY
    lane = iota((1, lanes), 1)
    slots, wr = TALL * HY, rows // RX
    at, cell = iota(columns.shape, 0), iota(columns.shape, 1)
    rest = at % slots
    column = rest // TALL + jnp.where(at < slots, wc - HY, 0)
    row = rest % TALL
    columns[...] = ((row < wr + 2 * HX) & (cell == row * wc + column)).astype(F32).astype(BF)

    at, to = iota(chosen.shape, 0), iota(chosen.shape, 1)
    reach = (RY + 2) * wc
    chosen[...] = ((to < reach) & (at == RY * (to % wc) + to // wc + RIM - 1)).astype(F32)
    at, to = iota((lanes, lanes), 0), iota((lanes, lanes), 1)
    spread[...] = ((at < reach) & (at % wc == to)).astype(F32).astype(BF)

    for copy in copies:
        copy.wait()
    at, to = iota((wc, lanes), 0), iota((wc, lanes), 1)
    repeat = ((to < reach) & (to % wc == at)).astype(F32).astype(BF)
    shift = (lane // wc).astype(F32)
    weight = [weights[:, k, :] for k in range(K)]
    whole = sum(weight[1:], weight[0])
    code = [jnp.dot(codes[:, k, :].astype(F32).astype(BF), repeat, preferred_element_type=F32) for k in range(K)]
    share = [
        sum(jnp.dot(p, repeat, preferred_element_type=F32) for p in split3(weight[k] / whole)) for k in range(K)
    ]
    for near in range(RX + 2):
        wave_shares[near] = sum(
            jnp.where(code[k] == near * (RY + 2.0) + shift, share[k], 0.0) for k in range(K)
        )


def prepare_ends_kernel(
    own, ob, oa, lists, spin_own, list_own, vel_halo, spin, turn, table, list_rim, fixed_a, fixed_b, vel
):
    rows, cols, lanes = own.shape
    per = lanes // 16
    even_x = is_even("gx")
    blank = jnp.zeros((EDGE, lanes), F32)
    list_rim[...] = list_own[...]
    ones = jnp.ones((8, lanes), BF)
    for side in range(2):
        one, two = (oa, ob) if side else (ob, oa)

        def from_x(start, n):
            return pick(even_x, one[start : start + n, :], two[start : start + n, :])

        parts = [from_x(i * cols, cols) for i in range(HV - 1)]
        outer = pltpu.roll(parts[0], lanes // 2, 1)
        parts = parts[1:] + [parts[0], outer] if side else [outer] + parts
        for k in range(HV):
            vel_halo[side * HV + k] = parts[k]
        near = [own[i] for i in (range(rows - HV + 1, rows) if side else range(HV - 1))]
        for k, value in enumerate(near + parts if side else parts + near):
            vel[side, k, 0:EDGE, :] = blank
            vel[side, k, EDGE + cols :, :] = blank
            vel[side, k, EDGE : EDGE + cols, :] = value
        for k in range(HL):
            at = side * HL + k
            r = k + side * (rows + HL)
            full = from_x((HV - 1) * cols + k * 16, 16)
            table[at], list_rim[r // per] = one_hot(full, cols), rim_lists(full, list_rim[r // per], r, cols)
            spin[at] = lax.dot_general(full[2 * K :].astype(BF), ones, ROWS_DOT, preferred_element_type=F32)[0:cols]
        for k in range(HL + 2):
            i = k + (rows - 2 if side else -HL)
            turn[side * (HL + 2) + k] = row_of(i, rows, spin_own, spin, HL) + vorticity(vel.at[side], k + 2, EDGE, cols)
    pack_rows(own, vel_halo, ob, oa, lists, fixed_a, fixed_b)


def inner_kernel(
    vel, vel_halo, spin_own, spin_ends, turn_own, turn_ends, table_own, table_ends,
    ends, rest, pb, pa, cells_ends, cells_rest,
    out, cells_far, mid_rim, drift_rim, spin_rim, total, prof_rim,
    mid, names, prof, drift, sems,
):
    rows, cols, lanes = out.shape
    copies = []
    wr, wc = rest.shape[0] + 2 * HX, rest.shape[1]
    for part, to in (
        (cells_ends.at[pl.ds(0, HX)], cells_far.at[pl.ds(0, HX)]),
        (cells_rest, cells_far.at[pl.ds(HX, wr - 2 * HX)]),
        (cells_ends.at[pl.ds(HX, HX)], cells_far.at[pl.ds(wr - HX, HX)]),
    ):
        copies.append(pltpu.make_async_copy(part, to, sems.at[len(copies)]))
    for copy in copies:
        copy.start()
    listed = rows + 2 * HL
    prow = wr + 2 * HX
    even_x = is_even("gx")
    lane = iota((1, lanes), 1)
    blank = jnp.zeros((EDGE, lanes), F32)
    for x in range(prow):
        if HX <= x < HX + wr:
            i = x - HX
            own = ends[i] if i < HX else rest[i - HX] if i < wr - HX else ends[i - wr + 2 * HX]
            part = own.astype(F32)
        elif x < HX:
            part = pick(even_x, pb[x], pa[x])
        else:
            part = pick(even_x, pa[x - HX - wr], pb[x - HX - wr])
        part = turned(part)
        prof[x * wc : (x + 1) * wc, :] = part
        names[x * wc : (x + 1) * wc, :] = part.astype(BF)
    prof_rim[...] = jnp.zeros(prof_rim.shape, F32)
    for c in range(HY):
        prof_rim[0, pl.ds(HY + c, prow, stride=2 * HY), :] = prof[pl.ds(c, prow, stride=wc), :]
        prof_rim[1, pl.ds(c, prow, stride=2 * HY), :] = prof[pl.ds(wc - HY + c, prow, stride=wc), :]

    block = 3 * wc

    def first(r, vel_ref, table_ref, turn_ref, spin_ref, vk, tk, uk):
        named = names[pl.ds(pl.multiple_of((r + 1) // 2 * wc, wc), block), :]
        stokes = lax.dot_general(table_ref[tk], named, ROWS_DOT, preferred_element_type=F32)[0:cols]
        drift[r] = stokes
        new = vel_ref[vk] + STEP * (turn_ref[uk] * stokes)
        mid[r, 0:EDGE, :] = blank
        mid[r, EDGE + cols :, :] = blank
        mid[r, EDGE : EDGE + cols, :] = new
        for where in range(2):
            begin = RIM if where == 0 else cols - RIM - EDGE
            mid_rim[r, where] = mid[r, EDGE + begin : 2 * EDGE + begin, :]
            drift_rim[r, where] = drift[r, begin : begin + EDGE, :]
            spin_rim[r, where] = spin_ref[tk, begin : begin + EDGE, :]

    for i in [*range(-HL, 2), *range(rows - 2, rows + HL)]:
        end = i + HL if i < 2 else i - rows + HL + 4
        if 0 <= i < rows:
            first(i + HL, vel, table_own, turn_ends, spin_own, i, i, end)
        else:
            far = 0 if i < 0 else rows
            first(i + HL, vel_halo, table_ends, turn_ends, spin_ends, i - far + HV, i - far + HL, end)
    unroll = (rows - 4) // 2

    def first_step(m, _):
        for u in range(unroll):
            i = m * unroll + u + 2
            first(i + HL, vel, table_own, turn_own, spin_own, i, i, i - 2)
        return 0

    lax.fori_loop(0, 2, first_step, 0)

    average = averager(lanes)
    means = jnp.zeros((cols, lanes), F32)
    ready = []
    for n in range(rows + 2):
        r = n + HL - 1
        absolute = row_of(n - 1, rows, spin_own, spin_ends, HL) + vorticity(mid, r, EDGE, cols)
        old = row_of(n - 1, rows, vel, vel_halo, HV) + mid[r, EDGE : EDGE + cols, :]
        new = 0.5 * old + (0.5 * STEP) * (absolute * drift[r])
        ready.append(new)
        if len(ready) == 2 or n == rows + 1:
            means = add_means(means, n + 1 - len(ready), ready, average)
            ready = []
        if 1 <= n <= rows:
            out[n - 1] = new
    total[...] = means

    for copy in copies:
        copy.wait()


def rim_kernel(
    own, vel_halo, ya, yb, mid_rim, drift_rim, spin_rim, total, list_rim, prof_rim, wave_shares, chosen, spread, inner,
    out, current_far,
    vel, mid, prof, drift, spin, picked, means, strips, current, sems,
):
    rows, cols, lanes = own.shape
    vrow = rows + 2 * HV
    wr, wc = current.shape[1], current.shape[2]
    listed = rows + 2 * HL
    prow = wr + 2 * HX
    even_y = is_even("gy")
    has_south, has_north = inside("gy")
    lane = iota((1, lanes), 1)
    sub = iota((EDGE, 1), 0)
    slots, vel_rows = y_rows(rows)

    def from_y(start, n):
        a, b = ya[start : start + n, :], yb[start : start + n, :]
        return pick(even_y, b, a) * has_south, pick(even_y, a, b) * has_north

    middle = pl.ds(EDGE, cols - 2 * EDGE)
    copies = [pltpu.make_async_copy(inner.at[:, middle, :], out.at[:, middle, :], sems.at[0])]
    copies[0].start()

    blank = jnp.zeros((EDGE, lanes), F32)
    for r in range(vrow):
        ref, k = (own, r - HV) if HV <= r < HV + rows else (vel_halo, r if r < HV else r - rows)
        vel[0, r, EDGE:, :] = ref[k, 0 : 2 * EDGE, :]
        vel[1, r, 0 : 2 * EDGE, :] = ref[k, cols - 2 * EDGE : cols, :]
    for start in range(0, vel_rows, 2 * EDGE):
        pieces = from_y(slots + start, 2 * EDGE)
        for i in range(2):
            low, high = (p[i * EDGE : i * EDGE + EDGE] for p in pieces)
            low_moved, high_moved = pltpu.roll(low, lanes // 2, 1), pltpu.roll(high, lanes // 2, 1)
            low_in = jnp.where(sub % RIM == 0, low_moved, low)
            for j in range(2):
                r = (start + i * EDGE) // RIM + j
                if r < vrow:
                    near = low_in if j else pltpu.roll(low_in, RIM, 0)
                    far = pltpu.roll(low, EDGE - 1 if j else RIM - 1, 0)
                    vel[0, r, 0:EDGE, :] = jnp.where(sub >= RIM, near, jnp.where(sub == RIM - 1, far, 0.0))
                    near = pltpu.roll(high, RIM, 0) if j else high
                    far = pltpu.roll(high_moved, RIM + 1 if j else 1, 0)
                    vel[1, r, 2 * EDGE :, :] = jnp.where(sub < RIM, near, jnp.where(sub == RIM, far, 0.0))

    prof[...] = prof_rim[...]
    south, north = from_y(0, slots)
    south, north = turned(south), turned(north)
    for c in range(HY):
        prof[0, pl.ds(c, TALL, stride=2 * HY), :] = south[TALL * c : TALL * (c + 1)]
        prof[1, pl.ds(HY + c, TALL, stride=2 * HY), :] = north[TALL * c : TALL * (c + 1)]

    per = lanes // 16
    start = slots + vel_rows
    span = 2 * per * HY
    place = iota((2 * span, lanes), 0).astype(F32)
    part = lane % 16
    offset = (part // EDGE) * span + ((lane // 16 + 1) // 2) * (2 * HY) + (part % EDGE) // RIM
    sub16 = iota((16, 1), 0)
    ones = jnp.ones((8, lanes), F32)
    none = jnp.zeros((2 * span, lanes), F32)
    for g in range(-(-listed // per)):
        tile, to = list_place(g * per, lanes)
        south, north = from_y(start + tile * 16, 16)
        full = list_rim[g]
        full = jnp.where(part // RIM == 0, pltpu.roll(south, (-to) % lanes, 1), full)
        full = jnp.where(part // RIM == 3, pltpu.roll(north, (3 * RIM - to) % lanes, 1), full)
        third = jnp.where(full >= 6.0, 2.0, jnp.where(full >= 3.0, 1.0, 0.0))
        full = jnp.where(sub16 < K, third + full + offset.astype(F32), full)
        hot = jnp.zeros((2 * span, lanes), F32)
        for k in range(K):
            hot = hot + jnp.where(place == full[k : k + 1], full[K + k : K + k + 1], 0.0)
        left = jnp.concatenate([hot, full[2 * K :], blank], axis=0).astype(BF)
        begin = g * (per // 2) * 2 * HY
        named = jnp.concatenate([prof[0, begin : begin + span, :], prof[1, begin : begin + span, :]], axis=0)
        right = jnp.concatenate([
            jnp.concatenate([named, blank, blank], axis=0),
            jnp.concatenate([none, ones, blank], axis=0),
        ], axis=1).astype(BF)
        both = lax.dot_general(left, right, ROWS_DOT, preferred_element_type=F32)
        for i in range(min(per, listed - g * per)):
            for side in range(2):
                at = i * 16 + side * EDGE
                drift[side, g * per + i] = both[at : at + EDGE, 0:lanes]
                spin[side, g * per + i] = both[at : at + EDGE, lanes:]

    lift = HV - HL
    for r in range(listed):
        for side in range(2):
            base = RIM + side * EDGE
            kept = RIM + EDGE - side * EDGE
            mid[side, r, kept : kept + EDGE, :] = mid_rim[r, side]
            absolute = spin[side, r] + vorticity(vel.at[side], r + lift, base, EDGE)
            new = vel[side, r + lift, base : base + EDGE, :] + STEP * (absolute * drift[side, r])
            mid[side, r, base : base + EDGE, :] = new

    average = averager(lanes)
    acc = jnp.zeros((2 * EDGE, lanes), F32)
    ready = []
    step = rows // PARTS
    begins = (EDGE - 1, EDGE + 1)
    for n in range(rows + 2):
        r = n + HL - 1
        both = []
        for side, begin in enumerate(begins):
            order = 1 - 2 * side

            def joined(here, there):
                return jnp.concatenate([here, there][::order], axis=0)[begin - RIM : begin - RIM + EDGE]

            absolute = joined(spin[side, r], spin_rim[r, side]) + vorticity(mid.at[side], r, begin, EDGE)
            old = vel[side, r + lift, begin : begin + EDGE, :] + mid[side, r, begin : begin + EDGE, :]
            new = 0.5 * old + (0.5 * STEP) * (absolute * joined(drift[side, r], drift_rim[r, side]))
            both.append(new)
            if 1 <= n <= rows:
                kept = inner[n - 1, side * (cols - EDGE) : side * (cols - EDGE) + EDGE, :]
                moved = pltpu.roll(new, EDGE - 1 if side == 0 else 1, 0)
                strips[side, n - 1] = jnp.where(sub == (EDGE - 1 if side == 0 else 0), kept, moved)
        ready.append(jnp.concatenate(both, axis=0))
        if len(ready) == 9 or n == rows + 1:
            acc = add_means(acc, n + 1 - len(ready), ready, average)
            ready = []
        if n and n % step == 0:
            part = pl.ds(n - step, step)
            for side, at in ((0, 0), (1, cols - EDGE)):
                one, two = strips.at[side, part], out.at[part, pl.ds(at, EDGE), :]
                copies.append(pltpu.make_async_copy(one, two, sems.at[len(copies)]))
                copies[-1].start()
    count = cols + 2 * RIM
    means[0:EDGE] = blank
    means[count - EDGE : count] = blank
    means[RIM - 1 : RIM - 1 + EDGE] = acc[0:EDGE]
    means[RIM - 1 + EDGE : count - RIM + 1 - EDGE] = total[EDGE - 1 : cols - EDGE + 1, :]
    means[count - RIM + 1 - EDGE : count - RIM + 1] = acc[EDGE:]

    means[count:] = jnp.zeros((means.shape[0] - count, lanes), F32)
    named = chosen[...].astype(BF)
    picked[...] = lax.dot_general(
        jnp.concatenate(split(means[...]), axis=0), jnp.concatenate([named] * 2, axis=0), ROWS_DOT,
        preferred_element_type=F32,
    )
    summed = [
        sum(wave_shares[near] * picked[pl.ds(2 * near + c, wr, stride=2 * RX), :] for near in range(RX + 2))
        for c in range(2)
    ]
    sums = jnp.dot(
        jnp.concatenate(split(jnp.concatenate(summed, axis=0)), axis=1),
        jnp.concatenate([spread[...]] * 2, axis=0),
        preferred_element_type=F32,
    )
    current[0] = sums[0:wr, 0:wc]
    current[1] = sums[wr:, 0:wc]
    copies.append(pltpu.make_async_copy(current, current_far, sems.at[len(copies)]))
    copies[-1].start()
    for copy in copies:
        copy.wait()


VMEM = pl.BlockSpec(memory_space=pltpu.VMEM)
ANY = pl.BlockSpec(memory_space=pltpu.HBM)


def call(kernel, name, outs, *args, scratch=(), any_in=(), any_out=()):
    args = [pltpu.with_memory_space_constraint(v, pltpu.HBM) if i in any_in else v for i, v in enumerate(args)]
    return pl.pallas_call(
        kernel,
        out_shape=tuple(jax.ShapeDtypeStruct(shape, dtype) for shape, dtype in outs),
        in_specs=[ANY if i in any_in else VMEM for i in range(len(args))],
        out_specs=tuple(ANY if i in any_out else VMEM for i in range(len(outs))),
        scratch_shapes=list(scratch),
        compiler_params=pltpu.CompilerParams(vmem_limit_bytes=14 << 20),
        name=name,
    )(*args)


def shards(
    spectrum, courant, source, wave_land, stokes_kernel, velocity, coriolis,
    ocean_codes, ocean_weights, wave_codes, wave_weights,
):
    wr, wc, bins = spectrum.shape
    rows, cols, lanes = velocity.shape
    listed = rows + 2 * HL
    prow = wr + 2 * HX

    with jax.named_scope("spectrum_edges"):
        codes, weights = jnp.transpose(ocean_codes, (0, 2, 1)), jnp.transpose(ocean_weights, (0, 2, 1))
        size = sum(x_rows(cols)) + wc * bins // lanes
        outs = [((size, lanes), BF)] * 2 + [((wr, bins), BF)] * 2 + [((rows, 16, lanes), F32)]
        outs += [(spectrum.shape, BF), (courant.shape, F32), ((wc, wr), F32), ((wc, wr), F32)]
        oa, ob, ya, yb, lists, spectrum, courant, source, land = call(
            edges_kernel, "edges", outs,
            spectrum, courant, source, wave_land, codes, weights, coriolis, velocity, any_in=range(8),
            scratch=[
                pltpu.VMEM(source.shape, F32),
                pltpu.VMEM(wave_land.shape, wave_land.dtype),
                pltpu.VMEM(codes.shape, codes.dtype),
                pltpu.VMEM(weights.shape, F32),
                pltpu.VMEM(coriolis.shape, F32),
                pltpu.VMEM((2, HV, cols, lanes), F32),
                pltpu.SemaphoreType.DMA((9,)),
            ],
        )
        oa, ob = exchange("gx", oa, ob)
        ya, yb = exchange("gy", ya, yb)

    with jax.named_scope("prepare_own"):
        groups = -(-listed // (lanes // 16))
        level = (cols, lanes)
        named = -(-(cols + 2 * RIM) // 16) * 16
        spin_own, turn_own, table_own, list_own, wave_shares, chosen, spread, stokes_kernel, columns = call(
            prepare_own_kernel, "prepare_own",
            [
                ((rows, *level), F32), ((rows - 4, *level), F32), ((rows, 3 * wc, lanes), BF), ((groups, 16, lanes), F32),
                ((RX + 2, wr, lanes), F32), ((named, lanes), F32), ((lanes, lanes), BF),
                (stokes_kernel.shape, BF), ((2 * TALL * HY, prow * wc), BF),
            ],
            velocity, lists, jnp.transpose(wave_codes, (0, 2, 1)), jnp.transpose(wave_weights, (0, 2, 1)),
            stokes_kernel, any_in=(2, 3, 4),
            scratch=[
                pltpu.VMEM((rows, cols + 2 * EDGE, lanes), F32),
                pltpu.VMEM((wr, K, wc), wave_codes.dtype),
                pltpu.VMEM((wr, K, wc), F32),
                pltpu.SemaphoreType.DMA((3,)),
            ],
        )

    with jax.named_scope("wave"):
        edge = (HX, wc, lanes)
        side = call(side_kernel, "side", [((wc, bins), BF)], ob, list_own)[0]
        cells_ends, ends, pa, pb = call(
            wave_ends_kernel, "wave_ends",
            [((2 * HX, wc, bins), BF), ((2 * HX, wc, lanes), BF), (edge, BF), (edge, BF)],
            spectrum, side, ya, yb, oa, courant, source, land, stokes_kernel,
        )
        pa, pb = exchange("gx", pa, pb)
        cells_rest, rest = call(
            wave_rest_kernel, "wave_rest",
            [((wr - 2 * HX, wc, bins), BF), ((wr - 2 * HX, wc, lanes), BF)],
            spectrum, ya, yb, courant, source, land, stokes_kernel, ends,
        )

    with jax.named_scope("prepare_ends"):
        size = y_rows(rows)[1] + (list_place(listed - 1, lanes)[0] + 1) * 16
        vel_halo, spin_ends, turn_ends, table_ends, list_rim, fixed_a, fixed_b = call(
            prepare_ends_kernel, "prepare_ends",
            [
                ((2 * HV, *level), F32), ((2 * HL, *level), F32), ((2 * HL + 4, *level), F32),
                ((2 * HL, 3 * wc, lanes), BF), ((groups, 16, lanes), F32),
                ((size, lanes), BF), ((size, lanes), BF),
            ],
            velocity, ob, oa, lists, spin_own, list_own,
            scratch=[pltpu.VMEM((2, 2 * HV - 1, cols + 2 * EDGE, lanes), F32)],
        )

    with jax.named_scope("halo"):
        size += y_rows(rows)[0]
        ya, yb = call(
            halo_kernel, "halo", [((size, lanes), BF)] * 2, fixed_a, fixed_b, columns, ends, rest, pb, pa
        )
        ya, yb = exchange("gy", ya, yb)

    with jax.named_scope("inner"):
        scratch = [
            pltpu.VMEM((listed, cols + 2 * EDGE, lanes), F32),
            pltpu.VMEM((prow * wc, lanes), BF),
            pltpu.VMEM((prow * wc, lanes), F32),
            pltpu.VMEM((listed, cols, lanes), F32),
            pltpu.SemaphoreType.DMA((3,)),
        ]
        result, new_spectrum, mid_rim, drift_rim, spin_rim, total, prof_rim = call(
            inner_kernel, "inner",
            [
                (velocity.shape, F32),
                (spectrum.shape, BF),
                ((listed, 2, EDGE, lanes), F32),
                ((listed, 2, EDGE, lanes), F32),
                ((listed, 2, EDGE, lanes), F32),
                ((cols, lanes), F32),
                ((2, 2 * HY * (TALL + 4), lanes), F32),
            ],
            velocity, vel_halo, spin_own, spin_ends, turn_own, turn_ends, table_own, table_ends,
            ends, rest, pb, pa,
            cells_ends, cells_rest, scratch=scratch, any_out=(1,),
        )

    with jax.named_scope("rim"):
        scratch = [
            pltpu.VMEM((2, rows + 2 * HV, 3 * EDGE, lanes), F32),
            pltpu.VMEM((2, listed, 3 * EDGE, lanes), F32),
            pltpu.VMEM((2, 2 * HY * (TALL + 4), lanes), F32),
            pltpu.VMEM((2, listed, EDGE, lanes), F32),
            pltpu.VMEM((2, listed, EDGE, lanes), F32),
            pltpu.VMEM((lanes, lanes), F32),
            pltpu.VMEM((named, lanes), F32),
            pltpu.VMEM((2, rows, EDGE, lanes), F32),
            pltpu.VMEM((2, wr, wc), F32),
            pltpu.SemaphoreType.DMA((2 + 2 * PARTS,)),
        ]
        new_velocity, current = call(
            rim_kernel, "rim", [(velocity.shape, F32), ((2, wr, wc), F32)],
            velocity, vel_halo, ya, yb, mid_rim, drift_rim, spin_rim, total, list_rim, prof_rim, wave_shares, chosen, spread,
            result, scratch=scratch, any_out=(0, 1),
        )
    return new_spectrum, new_velocity, current


def solution(mesh):
    return jax.shard_map(
        shards,
        mesh=mesh,
        in_specs=(
            P("gx", "gy", None), P(), P("gx", "gy"), P("gx", "gy"), P(), P("gx", "gy", None),
            P("gx", "gy"), P("gx", "gy", None), P("gx", "gy", None), P("gx", "gy", None), P("gx", "gy", None),
        ),
        out_specs=(P("gx", "gy", None), P("gx", "gy", None), P(None, "gx", "gy")),
        check_vma=False,
    )
```
